128 devices in a mesh: dp: 4 (over z_lo, core), row: 8 (over y, z_hi), col: 4 (over x).
Axes of the slice: x: 4, y: 4, z: 4 (z_hi: 2, z_lo: 2; z = z_hi * 2 + z_lo), core: 2. Of those that a mesh axis runs over, the one named last changes fastest.
Arguments:
- tokens: bfloat16 [16384, 1536], P(('dp', 'row'), 'col'), may hold values from -6 to 6
- positions: int32 [16384], P(('dp', 'col')), may hold values from 0 to 6142, as said below
- attn_gain: float32 [1536], P('col'), may hold values from 0.1 to 1.9
- qkv_weight: bfloat16 [1536, 3072], P('col', 'row'), may hold values from -0.15625 to 0.15625
- output_weight: bfloat16 [1536, 1536], P('row', 'col'), may hold values from -1.25 to 1.25
- ffn_gain: float32 [1536], P('col'), may hold values from 0.1 to 1.9
- gate_weight: bfloat16 [1536, 4096], P('col', 'row'), may hold values from -0.15625 to 0.15625
- up_weight: bfloat16 [1536, 4096], P('col', 'row'), may hold values from -0.15625 to 0.15625
- down_weight: bfloat16 [4096, 1536], P('row', 'col'), may hold values from -0.09375 to 0.09375
- cotangent: bfloat16 [16384, 1536], P(('dp', 'row'), 'col'), may hold values from -6 to 6
Outputs:
- mixed: float32 [16384, 1536], P(('dp', 'row'), 'col')
- tokens_grad: float32 [16384, 1536], P(('dp', 'row'), 'col')
- attn_dgain: float32 [1536], P('col')
- qkv_grad: float32 [1536, 3072], P('col', 'row')
- output_grad: float32 [1536, 1536], P('row', 'col')
- ffn_dgain: float32 [1536], P('col')
- gate_grad: float32 [1536, 4096], P('col', 'row')
- up_grad: float32 [1536, 4096], P('col', 'row')
- down_grad: float32 [4096, 1536], P('row', 'col')
The draws below stay inside these ranges and needn't reach their ends.
Inputs may be any that keep to these rules, and one draw needn't show every extreme that they name: Within each sequence of 1024 tokens the positions rise by one or two from each token to the next, and a sequence's first position is at most 4096.
All inputs are finite; a program needn't handle non-finite values.
Results may differ from the reference program's by a relative error of at most 0.02.
Values may be sent and summed in bfloat16 or wider, within the bound.
A program may use at most 192 MiB of HBM per device.

```python
import math
import jax
import jax.numpy as jnp
from jax import lax

D = 1536
H = 16
KVH = 8
HD = 96
FF = 4096
LEN = 1024
QKV = 3072
SEQS = 16
TOKENS = 16384
N_DP = 4


def draw_positions(key, part):
    key = jax.random.fold_in(key, 7)
    first_key, second_key, third_key = jax.random.split(key, 3)
    starts = jax.random.randint(first_key, (SEQS, 1), 0, 4097)
    strides = jax.random.randint(second_key, (SEQS, LEN), 1, 3)
    chosen = jax.random.randint(third_key, (), 0, SEQS)
    other = (chosen + 1) % SEQS
    index = jnp.arange(SEQS, dtype=jnp.int32)[:, None]
    strides = jnp.where(index == chosen, 2, strides)
    starts = jnp.where(index == chosen, 4096, starts)
    starts = jnp.where(index == other, 0, starts)
    rises = jnp.cumsum(strides, axis=1) - strides[:, :1]
    return (starts + rises).reshape(TOKENS).astype(jnp.int32)


def steps_of(stream_key, extent, pieces, least, high):
    loudness, own = 1.0, jax.random.fold_in(stream_key, 6)
    for dim, blocks in pieces:
        steps = jnp.exp(jax.random.uniform(jax.random.fold_in(own, dim), (blocks,), jnp.float32, least / len(pieces), high / len(pieces)))
        loudness = loudness * jnp.repeat(steps, extent[dim] // blocks).reshape([-1 if axis == dim else 1 for axis in range(len(extent))])
    return loudness


def normal_values(key, dims, scale, bound, cuts=(), held_as=jnp.bfloat16):
    values = jax.random.normal(key, dims, jnp.float32) * scale
    if len(cuts) > 0:
        values = steps_of(key, dims, cuts, -0.22, 0.18) * values
    return jnp.clip(values, min=-bound, max=bound).astype(held_as)


def setup_inputs(seed: int = 0) -> dict:
    key_of = jax.random.split(jax.random.key(seed), 11)
    tokens = normal_values(key_of[0], (TOKENS, D), 1.0, 6.0, ((0, 32), (1, 4)))
    positions = draw_positions(jax.random.fold_in(key_of[10], 71), 0)
    attn_gain = jnp.clip(1.0 + 0.18 * jax.random.normal(key_of[2], (D,), jnp.float32), 0.1, 1.9)
    qkv_weight = normal_values(key_of[3], (D, QKV), D ** -0.5, 0.15625, ((0, 4), (1, 8)))
    output_weight = normal_values(key_of[4], (H * HD, D), (max(D // 64, 1)) ** -0.5, 1.25, ((0, 8), (1, 4)))
    ffn_gain = jnp.clip(1.0 + 0.18 * jax.random.normal(key_of[5], (D,), jnp.float32), 0.1, 1.9)
    gate_weight = normal_values(key_of[6], (D, FF), D ** -0.5, 0.15625, ((0, 4), (1, 8)))
    up_weight = normal_values(key_of[7], (D, FF), D ** -0.5, 0.15625, ((0, 4), (1, 8)))
    down_weight = normal_values(key_of[8], (FF, D), FF ** -0.5, 0.09375, ((0, 8), (1, 4)))
    cotangent = normal_values(key_of[9], (TOKENS, D), 1.0, 6.0, ((0, 32), (1, 4)))
    return dict(tokens=tokens, positions=positions, attn_gain=attn_gain, qkv_weight=qkv_weight, output_weight=output_weight, ffn_gain=ffn_gain, gate_weight=gate_weight, up_weight=up_weight, down_weight=down_weight, cotangent=cotangent)


epsilon = 1e-05
rope_base = 100000.0
masked_score = -1e+30
highest = lax.Precision.HIGHEST

@jax.custom_vjp
def low(v):
    return lax.optimization_barrier(v.astype(jnp.bfloat16)).astype(jnp.float32)

@jax.custom_vjp
def low_back(v):
    return v

def low_keep(v):
    return (low(v), None)

def low_pass(kept, grad):
    return (grad,)

def back_keep(v):
    return (v, None)

def back_low(kept, grad):
    return (low(grad),)
low.defvjp(low_keep, low_pass)
low_back.defvjp(back_keep, back_low)

def rope_tables(places, head_size):
    half_size = head_size // 2
    frequency = rope_base ** (-(jnp.arange(half_size, dtype=jnp.float32) * 2.0 / head_size))
    angles = places.astype(jnp.float32)[:, None] * frequency[None, :]
    return (jnp.cos(angles), jnp.sin(angles))

def rotate(vectors, cosine, sine):
    half_size = vectors.shape[-1] // 2
    first_half = vectors[..., :half_size]
    second_half = vectors[..., half_size:]
    return jnp.concatenate([first_half * cosine - second_half * sine, second_half * cosine + first_half * sine], axis=-1)

def rms_scale(source, gain):
    return source * lax.rsqrt(lax.optimization_barrier(jnp.mean(source * source, axis=-1, keepdims=True)) + epsilon) * gain

def attend(inputs):
    queries, keys, values = inputs
    raw = jnp.einsum('qhgd,khd->hgqk', queries, keys, precision=highest)
    scores = low_back(raw) * (1.0 / math.sqrt(HD))
    index = jnp.arange(LEN)
    allowed = index[None, :] <= index[:, None]
    scores = jnp.where(allowed[None, None], scores, masked_score)
    top = lax.optimization_barrier(jnp.max(scores, axis=-1, keepdims=True))
    exponent = jnp.exp(scores - top)
    probs = exponent / lax.optimization_barrier(jnp.sum(exponent, axis=-1, keepdims=True))
    return jnp.einsum('hgqk,khd->qhgd', low(probs), values, precision=highest)

def layer(source, places, attn_gain, qkv_weight, output_weight, ffn_gain, gate_weight, up_weight, down_weight):
    count = source.shape[0]
    seq_count = count // LEN
    group = H // KVH
    normed = low(rms_scale(source, attn_gain))
    projected = low_back(jnp.dot(normed, qkv_weight, precision=highest))
    shaped = projected.reshape(seq_count, LEN, KVH, group + 2, HD)
    cosine, sine = rope_tables(places, HD)
    cosine = cosine.reshape(seq_count, LEN, 1, 1, -1)
    sine = sine.reshape(seq_count, LEN, 1, 1, -1)
    queries = low(rotate(shaped[..., :group, :], cosine, sine))
    keys = low(rotate(shaped[..., group, :], cosine[..., 0, :], sine[..., 0, :]))
    values = low(shaped[..., group + 1, :])
    attended = lax.map(jax.checkpoint(attend), (queries, keys, values))
    attended = low(low_back(attended.reshape(count, H * HD)))
    middle = source + low_back(jnp.dot(attended, output_weight, precision=highest))
    normed_ffn = low(rms_scale(middle, ffn_gain))
    gate = low_back(jnp.dot(normed_ffn, gate_weight, precision=highest))
    up_values = low_back(jnp.dot(normed_ffn, up_weight, precision=highest))
    hidden = low(gate * jax.nn.sigmoid(gate) * up_values)
    return middle + low_back(jnp.dot(hidden, down_weight, precision=highest))

def reference(tokens, positions, attn_gain, qkv_weight, output_weight, ffn_gain, gate_weight, up_weight, down_weight, cotangent):
    group_tokens = TOKENS // N_DP
    sources = tokens.astype(jnp.float32).reshape(N_DP, group_tokens, D)
    places_all = positions.reshape(N_DP, group_tokens)
    cotangents = cotangent.astype(jnp.float32).reshape(N_DP, group_tokens, D)
    params = (attn_gain.astype(jnp.float32), qkv_weight.astype(jnp.float32), output_weight.astype(jnp.float32), ffn_gain.astype(jnp.float32), gate_weight.astype(jnp.float32), up_weight.astype(jnp.float32), down_weight.astype(jnp.float32))

    def step(totals, group_inputs):
        source, places, cotan = group_inputs

        def forward(source_in, gain_one, joint, outward, gain_two, gating, upward, downward):
            return layer(source_in, places, gain_one, joint, outward, gain_two, gating, upward, downward)
        result, pullback = jax.vjp(forward, source, params[0], params[1], params[2], params[3], params[4], params[5], params[6])
        grads = pullback(cotan)
        summed = tuple((total + grad for total, grad in zip(totals, grads[1:])))
        return (summed, (result, grads[0]))
    initial = tuple((jnp.zeros_like(param) for param in params))
    totals, outputs = lax.scan(step, initial, (sources, places_all, cotangents))
    mixed, tokens_grad = outputs
    return (mixed.reshape(TOKENS, D), tokens_grad.reshape(TOKENS, D), totals[0], totals[1], totals[2], totals[3], totals[4], totals[5], totals[6])
```

```python
import math

import jax
import jax.numpy as jnp
from jax import lax
from jax.sharding import Mesh
from jax.sharding import PartitionSpec as P

D = 1536
H = 16
KVH = 8
HD = 96
LEN = 1024
GROUP = H // KVH
AXES = ("zl", "core", "y", "zh", "x")
DP_ROW = ("zl", "core", "y", "zh")
bf16 = jnp.bfloat16
f32 = jnp.float32

epsilon = 1e-05
rope_base = 100000.0
masked_score = -1e30
SIZES = {"zl": 2, "core": 2, "y": 4, "zh": 2, "x": 4}


def fetch(values, axis, step):
    n = SIZES[axis]
    return lax.ppermute(values, axis, [((i + step) % n, i) for i in range(n)])


def fetch_z(values, flip):
    flip = (flip & 1) * 2 + flip // 2
    return lax.ppermute(values, ("zl", "zh"), [(i ^ flip, i) for i in range(4)])


def send_xy(values):
    return lax.ppermute(values, ("y", "x"), [(y * 4 + x, x * 4 + y) for y in range(4) for x in range(4)])


def gather_ring(values, axis):
    return [values] + [fetch(values, axis, k) for k in range(1, SIZES[axis])]


def gather_z(values):
    return [values] + [fetch_z(values, k) for k in range(1, 4)]


def scatter_ring(blocks, axis):
    total = blocks[0].astype(f32)
    for k in range(1, 4):
        total = total + fetch(blocks[k].astype(bf16), axis, -k).astype(f32)
    return total


def scatter_z(blocks):
    total = blocks[0].astype(f32)
    for k in range(1, 4):
        total = total + fetch_z(blocks[k].astype(bf16), k).astype(f32)
    return total


def rolled(stack, start):
    return lax.dynamic_slice_in_dim(jnp.concatenate([stack, stack], 0), start, 4, axis=0)


def ordered(flag, own, other):
    return jnp.where(flag == 0, own, other), jnp.where(flag == 0, other, own)


def dot(a, b, dims):
    return lax.dot_general(a, b, (dims, ((), ())), preferred_element_type=f32)


def rope_tables(places):
    half_size = HD // 2
    frequency = rope_base ** (-(jnp.arange(half_size, dtype=f32) * 2.0 / HD))
    angles = places.astype(f32)[:, None] * frequency[None, :]
    return jnp.cos(angles), jnp.sin(angles)


def rotate(vectors, cosine, sine):
    half_size = vectors.shape[-1] // 2
    a, b = vectors[..., :half_size], vectors[..., half_size:]
    return jnp.concatenate([a * cosine - b * sine, b * cosine + a * sine], axis=-1)


def block_scores(query_block, key_seq, start):
    raw = jnp.einsum("qhd,kd->hqk", query_block, key_seq, preferred_element_type=f32)
    raw = raw * (1.0 / math.sqrt(HD))
    rows = start + jnp.arange(query_block.shape[0], dtype=jnp.int32)
    cols = jnp.arange(key_seq.shape[0], dtype=jnp.int32)
    return jnp.where((cols[None, :] <= rows[:, None])[None], raw, masked_score)


def attention_forward(q, k, v):
    outs, logs = [], []
    for start in (0, 512):
        keys, values = k[: start + 512], v[: start + 512]
        scores = block_scores(q[start : start + 512], keys, start)
        top = jnp.max(scores, axis=-1, keepdims=True)
        exponent = jnp.exp(scores - top)
        totals = jnp.sum(exponent, axis=-1, keepdims=True)
        probs = (exponent / totals).astype(bf16)
        outs.append(jnp.einsum("hqk,kd->qhd", probs, values, preferred_element_type=f32))
        logs.append((top + jnp.log(totals))[..., 0])
    return jnp.concatenate(outs, 0).astype(bf16), logs


def attention_backward(q, k, v, grad, logs):
    scale = 1.0 / math.sqrt(HD)
    dqs = []
    dk = jnp.zeros((LEN, HD), f32)
    dv = jnp.zeros((LEN, HD), f32)
    for i, start in enumerate((0, 512)):
        n = start + 512
        qb, gb = q[start:n], grad[start:n]
        scores = block_scores(qb, k[:n], start)
        probs = jnp.exp(scores - logs[i][..., None])
        dpr = jnp.einsum("qhd,kd->hqk", gb, v[:n], preferred_element_type=f32)
        inner = jnp.sum(probs * dpr, axis=-1, keepdims=True)
        ds = (probs * (dpr - inner) * scale).astype(bf16)
        dqs.append(jnp.einsum("hqk,kd->qhd", ds, k[:n], preferred_element_type=f32))
        dk = dk.at[:n].add(jnp.einsum("hqk,qhd->kd", ds, qb, preferred_element_type=f32))
        dv = dv.at[:n].add(jnp.einsum("hqk,qhd->kd", probs.astype(bf16), gb, preferred_element_type=f32))
    return jnp.concatenate(dqs, 0), dk, dv


def per_device(
    tokens,
    positions,
    attn_gain,
    qkv_weight,
    output_weight,
    ffn_gain,
    gate_weight,
    up_weight,
    down_weight,
    cotangent,
):
    ix, iy = lax.axis_index("x"), lax.axis_index("y")
    zl, zh, core = lax.axis_index("zl"), lax.axis_index("zh"), lax.axis_index("core")
    quarter = zl * 2 + core

    x_full = jnp.concatenate(gather_ring(tokens, "x"), 1).astype(f32)
    gains = gather_ring(jnp.stack([attn_gain, ffn_gain]), "x")
    gains = jnp.concatenate(gains, 1)
    gain_a, gain_f = gains[0], gains[1]
    places = rolled(jnp.stack(gather_ring(positions, "x")), (iy - ix + 4) % 4)[0]
    places = lax.dynamic_slice_in_dim(places, zh * 512, 512)

    qo = jnp.concatenate([qkv_weight.T, output_weight], 0)
    qo = lax.dynamic_slice_in_dim(qo, quarter * 144, 144, axis=0)
    qo = send_xy(qo)
    qo = rolled(jnp.stack(gather_ring(qo, "y")), (ix - iy + 4) % 4)
    qo = jnp.concatenate([qo[0], qo[1], qo[2], qo[3]], 1)
    zs = gather_z(qo)
    own = jnp.concatenate(ordered(zl, zs[0], zs[1]), 0).reshape(2, 144, D)
    far = jnp.concatenate(ordered(zl, zs[2], zs[3]), 0).reshape(2, 144, D)
    pair = jnp.stack([own, far])
    pair = jnp.stack(ordered(core, pair, fetch(pair, "core", 1)), 2)
    heads = pair.reshape(2, 576, D)
    w_qkv = heads[:, :384].reshape(768, D)
    w_out = heads[:, 384:].reshape(384, D)

    def hidden_rows(w):
        blocks = lax.dynamic_slice_in_dim(w.reshape(4, 4, 32, 384), quarter, 1, axis=1)[:, 0]
        return rolled(blocks, ix)

    mine = jnp.stack([hidden_rows(gate_weight.T), hidden_rows(up_weight.T), hidden_rows(down_weight)], 1)
    ffn = jnp.concatenate([mine[0]] + [fetch(mine[4 - k], "x", k) for k in range(1, 4)], 2)
    half_a = jnp.concatenate(gather_z(jnp.concatenate(gather_ring(ffn[:, :16], "y"), 1)), 1)
    half_b = jnp.concatenate(gather_ring(jnp.concatenate(gather_z(ffn[:, 16:]), 1), "y"), 1)
    ffn = jnp.concatenate([half_a, half_b], 1)
    ffn = jnp.concatenate([ffn, fetch(ffn, "core", 1)], 1)
    w_gate, w_up, w_down = ffn[0], ffn[1], ffn[2]

    rinv1 = lax.rsqrt(jnp.mean(x_full * x_full, axis=1) + epsilon)
    a1 = (x_full * rinv1[:, None] * gain_a[None, :]).astype(bf16)
    proj = dot(a1, w_qkv, ((1,), (1,))).reshape(512, 2, 4, HD)
    cosine, sine = rope_tables(places)
    cosine, sine = cosine[:, None, None], sine[:, None, None]
    rot = rotate(proj[:, :, :3], cosine, sine)
    qkv = jnp.concatenate([rot, proj[:, :, 3:]], 2).astype(bf16)
    first, second = ordered(zh, qkv[:, 0], fetch(qkv[:, 1], "zh", 1))
    seq = jnp.concatenate([first, second], 0)
    att, logs = attention_forward(seq[:, :2], seq[:, 2], seq[:, 3])
    lower, upper = att[:512], att[512:]
    stay, go = ordered(zh, lower, upper)
    att_pair = jnp.concatenate([stay.reshape(512, 192), fetch(go.reshape(512, 192), "zh", 1)], 1)
    branch = dot(att_pair, w_out, ((1,), (0,)))
    middle = tokens.astype(f32) + scatter_ring([branch[:, 384 * k : 384 * k + 384] for k in range(4)], "x")

    m_full = jnp.concatenate(gather_ring(middle.astype(bf16), "x"), 1).astype(f32)
    rinv2 = lax.rsqrt(jnp.mean(m_full * m_full, axis=1) + epsilon)
    a2 = (m_full * rinv2[:, None] * gain_f[None, :]).astype(bf16)
    cot = jnp.concatenate(gather_ring(cotangent, "x"), 1)
    gate = dot(a2, w_gate, ((1,), (1,)))
    up = dot(a2, w_up, ((1,), (1,)))
    dh = dot(cot, w_down, ((1,), (1,)))
    sg = jax.nn.sigmoid(gate)
    silu = gate * sg
    hidden = (silu * up).astype(bf16)
    dgate = (dh * up * sg * (1.0 + gate * (1.0 - sg))).astype(bf16)
    dup = (dh * silu).astype(bf16)
    da2 = dot(dgate, w_gate, ((1,), (0,))) + dot(dup, w_up, ((1,), (0,)))
    da2 = scatter_ring([da2[:, 384 * k : 384 * k + 384] for k in range(4)], "x")
    inner2 = jnp.sum(dgate.astype(f32) * gate + dup.astype(f32) * up, axis=1).reshape(4, 128)
    inner2 = sum(gather_ring(inner2, "x")).reshape(512) / rinv2
    gain_f_own, gain_a_own = ffn_gain[None, :], attn_gain[None, :]
    ffn_dgain = jnp.sum(da2 * middle * rinv2[:, None], axis=0)
    dmiddle = (
        cotangent.astype(f32)
        + rinv2[:, None] * gain_f_own * da2
        - middle * (rinv2 * rinv2 * rinv2 * inner2 / D)[:, None]
    )
    dz = jnp.concatenate(gather_ring(dmiddle.astype(bf16), "x"), 1)
    datt = dot(dz, w_out, ((1,), (1,))).astype(bf16)
    down = dot(hidden, w_down, ((1,), (0,)))
    mixed = middle + scatter_ring([down[:, 384 * k : 384 * k + 384] for k in range(4)], "x")
    g_ffn = jnp.stack([dot(dgate, a2, ((0,), (0,))), dot(dup, a2, ((0,), (0,))), dot(hidden, cot, ((0,), (0,)))])

    def reduce_hidden(g):
        keep = g[:, :512] + fetch(g[:, 512:].astype(bf16), "core", 1).astype(f32)
        a, b = keep[:, :256], keep[:, 256:]
        a = scatter_z([a[:, 64 * k : 64 * k + 64] for k in range(4)])
        a = scatter_ring([a[:, 16 * k : 16 * k + 16] for k in range(4)], "y")
        b = scatter_ring([b[:, 64 * k : 64 * k + 64] for k in range(4)], "y")
        b = scatter_z([b[:, 16 * k : 16 * k + 16] for k in range(4)])
        part = jnp.concatenate([a, b], 1).astype(bf16)
        back = [part[:, :, :384]] + [fetch(part[:, :, 384 * k : 384 * k + 384], "x", -k) for k in range(1, 4)]
        blocks = rolled(jnp.stack([back[0], back[3], back[2], back[1]]), (4 - ix) % 4)
        quarters = jnp.stack(ordered(core, blocks, fetch(blocks, "core", 1)), 2)
        quarters = jnp.stack(ordered(zl, quarters, fetch(quarters, "zl", 1)), 2)
        return quarters.transpose(1, 0, 2, 3, 4, 5).reshape(3, 512, 384).astype(f32)

    g_gate, g_up, g_down = reduce_hidden(g_ffn)

    own_half, far_half = datt[:, :192], datt[:, 192:]
    g_lo, g_hi = ordered(zh, own_half, fetch(far_half, "zh", 1))
    g_seq = jnp.concatenate([g_lo, g_hi], 0).reshape(LEN, GROUP, HD)
    dq, dk, dv = attention_backward(seq[:, :2], seq[:, 2], seq[:, 3], g_seq, logs)
    dqkv = jnp.concatenate([dq, dk[:, None], dv[:, None]], 1).astype(bf16)
    stay, go = ordered(zh, dqkv[:512], dqkv[512:])
    dpair = jnp.stack([stay, fetch(go, "zh", 1)], 1).astype(f32)
    inner1 = jnp.sum(dpair * qkv.astype(f32), axis=(1, 2, 3)).reshape(4, 128)
    inner1 = sum(gather_ring(inner1, "x")).reshape(512) / rinv1
    turned = rotate(dpair[:, :, :3], cosine, -sine)
    dproj = jnp.concatenate([turned, dpair[:, :, 3:]], 2).astype(bf16).reshape(512, 768)
    da1 = dot(dproj, w_qkv, ((1,), (0,)))
    da1 = scatter_ring([da1[:, 384 * k : 384 * k + 384] for k in range(4)], "x")
    x_own = tokens.astype(f32)
    attn_dgain = jnp.sum(da1 * x_own * rinv1[:, None], axis=0)
    tokens_grad = (
        dmiddle
        + rinv1[:, None] * gain_a_own * da1
        - x_own * (rinv1 * rinv1 * rinv1 * inner1 / D)[:, None]
    )

    gw_qkv = dot(dproj, a1, ((0,), (0,))).reshape(2, 384, D)
    gw_out = dot(att_pair, dz, ((0,), (0,))).reshape(2, 192, D)
    g = jnp.concatenate([gw_qkv, gw_out], 1).reshape(2, 2, 2, 144, D)
    keep, give = ordered(core, g[:, :, 0], g[:, :, 1])
    g = keep + fetch(give.astype(bf16), "core", 1).astype(f32)
    g_own, g_far = ordered(zl, g[:, 0], g[:, 1])
    g = scatter_z([g_own[0], g_far[0], g_own[1], g_far[1]])
    cols = jnp.stack([g[:, 384 * k : 384 * k + 384] for k in range(4)])
    cols = rolled(cols, (iy - ix + 4) % 4)
    g = scatter_ring([cols[k] for k in range(4)], "y").astype(bf16)
    g = send_xy(g)
    g = jnp.stack(ordered(core, g, fetch(g, "core", 1)))
    g = jnp.stack(ordered(zl, g, fetch(g, "zl", 1))).reshape(576, 384).astype(f32)
    qkv_grad, output_grad = g[:384].T, g[384:]

    attn_dgain, ffn_dgain = lax.psum((attn_dgain, ffn_dgain), DP_ROW)
    return (
        mixed,
        tokens_grad,
        attn_dgain,
        qkv_grad,
        output_grad,
        ffn_dgain,
        g_gate.T,
        g_up.T,
        g_down,
    )


def solution(mesh):
    finer = Mesh(mesh.devices.reshape(2, 2, 4, 2, 4), AXES)
    row = ("y", "zh")
    in_specs = (
        P(DP_ROW, "x"),
        P(("zl", "core", "x")),
        P("x"),
        P("x", row),
        P(row, "x"),
        P("x"),
        P("x", row),
        P("x", row),
        P(row, "x"),
        P(DP_ROW, "x"),
    )
    out_specs = (
        P(DP_ROW, "x"),
        P(DP_ROW, "x"),
        P("x"),
        P("x", row),
        P(row, "x"),
        P("x"),
        P("x", row),
        P("x", row),
        P(row, "x"),
    )
    return jax.shard_map(per_device, mesh=finer, in_specs=in_specs, out_specs=out_specs, check_vma=False)
```

```python
import functools
import math

import jax
import jax.numpy as jnp
import numpy as np
from jax import lax
from jax.experimental import pallas as pl
from jax.experimental.pallas import tpu as pltpu
from jax.sharding import Mesh
from jax.sharding import PartitionSpec as P

D = 1536
HD = 96
AXES = ("zl", "core", "y", "zh", "x")
DP_ROW = ("zl", "core", "y", "zh")
bf16 = jnp.bfloat16
f32 = jnp.float32
i32 = jnp.int32
MESH = pl.DeviceIdType.MESH
VM = pl.BlockSpec(memory_space=pltpu.VMEM)
ANY = pl.BlockSpec(memory_space=pl.ANY)

epsilon = 1e-05
rope_base = 100000.0
masked_score = -1e30
score_scale = math.log2(math.e) / math.sqrt(HD)
H0, H1 = pl.ds(0, 256), pl.ds(256, 256)


def dot(a, b):
    return lax.dot_general(a, b, (((1,), (0,)), ((), ())), preferred_element_type=f32)


def dot_t(a, b):
    return lax.dot_general(a, b, (((1,), (1,)), ((), ())), preferred_element_type=f32)


def lanes(index, width):
    return pl.ds(pl.multiple_of(index * width, 128), width)


class Place:
    def __init__(self):
        self.x, self.y = lax.axis_index("x"), lax.axis_index("y")
        self.zl, self.zh, self.core = lax.axis_index("zl"), lax.axis_index("zh"), lax.axis_index("core")
        self.quarter = self.zl * 2 + self.core
        self.ahead, self.behind, self.across = [(self.x + k) % 4 for k in (1, 3, 2)]
        self.right, self.left, self.far = {"x": self.ahead}, {"x": self.behind}, {"x": self.across}
        self.ys = [{"y": (self.y + k) % 4} for k in (1, 3, 2)]
        self.zs = [{"zl": 1 - self.zl}, {"zl": 1 - self.zl, "zh": 1 - self.zh}, {"zh": 1 - self.zh}]
        self.twin = {"core": 1 - self.core}
        self.mirror = {"x": self.y, "y": self.x}

    def enter(self):
        barrier = pltpu.get_barrier_semaphore()
        peers = [self.right, self.left, self.far, *self.ys, *self.zs, self.twin]
        for peer in peers:
            pl.semaphore_signal(barrier, inc=1, device_id=peer, device_id_type=MESH)

        @pl.when(self.x != self.y)
        def _():
            pl.semaphore_signal(barrier, inc=1, device_id=self.mirror, device_id_type=MESH)
            pl.semaphore_wait(barrier, len(peers) + 1)

        @pl.when(self.x == self.y)
        def _():
            pl.semaphore_wait(barrier, len(peers))


class Links:
    def __init__(self, send, recv, local):
        self.send, self.recv, self.local, self.count, self.local_count = send, recv, local, 0, 0
        self.open = []

    def make(self, src, dst, device):
        i = self.count
        self.count += 1
        return pltpu.make_async_remote_copy(
            src, dst, self.send.at[i], self.recv.at[i], device_id=device, device_id_type=MESH
        )

    def start(self, src, dst, device):
        copy = self.make(src, dst, device)
        copy.start()
        self.open.append(copy)
        return copy

    def spread(self, ref, devices):
        return [self.start(ref, ref, device) for device in devices]

    def keep(self, src, dst):
        copy = pltpu.make_async_copy(src, dst, self.local.at[self.local_count])
        self.local_count += 1
        copy.start()
        return copy

    def close(self):
        for copy in self.open:
            copy.wait_send()
        self.open = []


def arrive(copies):
    for copy in copies:
        copy.wait_recv()


class RingGather:
    def __init__(self, links, here, src, buf):
        cols = lanes(here.x, 384)
        self.links, self.here, self.buf = links, here, buf
        self.first = [
            links.start(src(H0), buf.at[H0, cols], here.right),
            links.start(src(H1), buf.at[H1, cols], here.left),
        ]
        self.second = [
            links.start(src(H1), buf.at[H1, cols], here.right),
            links.start(src(H0), buf.at[H0, cols], here.left),
        ]

    def forward(self):
        here, buf = self.here, self.buf
        self.first[0].wait_recv()
        a = buf.at[H0, lanes(here.behind, 384)]
        self.third = [self.links.start(a, a, here.right)]
        self.first[1].wait_recv()
        b = buf.at[H1, lanes(here.ahead, 384)]
        self.third += [self.links.start(b, b, here.left)]

    def finish(self):
        arrive(self.second)
        arrive(self.third)


class RingScatter:
    def __init__(self, links, here, part, slots):
        self.links, self.here, self.part, self.slots = links, here, part, slots

    def send_far(self):
        h, p, s = self.here, self.part, self.slots
        self.r0 = self.links.start(p.at[h.across, H0], s.at[0], h.right)
        self.l0 = self.links.start(p.at[h.across, H1], s.at[1], h.left)

    def send_near(self):
        h, p, s = self.here, self.part, self.slots
        self.r1 = self.links.start(p.at[h.ahead, H1], s.at[2], h.right)
        self.l1 = self.links.start(p.at[h.behind, H0], s.at[3], h.left)

    def forward(self):
        h, p, s = self.here, self.part, self.slots
        self.r0.wait_recv()
        p[h.ahead, H0] = (p[h.ahead, H0].astype(f32) + s[0].astype(f32)).astype(bf16)
        self.r2 = self.links.start(p.at[h.ahead, H0], s.at[4], h.right)
        self.l0.wait_recv()
        p[h.behind, H1] = (p[h.behind, H1].astype(f32) + s[1].astype(f32)).astype(bf16)
        self.l2 = self.links.start(p.at[h.behind, H1], s.at[5], h.left)

    def finish(self):
        arrive([self.r1, self.l1, self.r2, self.l2])

    def received(self, half):
        s = self.slots
        pair = (4, 3) if half == 0 else (2, 5)
        return s[pair[0]].astype(f32) + s[pair[1]].astype(f32)


def sine_cosine(angle):
    turns = jnp.floor(angle * (1.0 / (2.0 * math.pi)) + 0.5)
    r = angle - turns * 6.28125
    r = r - turns * 0.0019350051879882812
    r = r - turns * 3.0199159819185874e-07
    t = r * 0.5
    t2 = t * t
    s = 1.0 / 6227020800.0
    for c in (-1.0 / 39916800, 1.0 / 362880, -1.0 / 5040, 1.0 / 120, -1.0 / 6, 1.0):
        s = s * t2 + c
    s = s * t
    c_ = 1.0 / 479001600.0
    for c in (-1.0 / 3628800, 1.0 / 40320, -1.0 / 720, 1.0 / 24, -0.5, 1.0):
        c_ = c_ * t2 + c
    return 2.0 * s * c_, 1.0 - 2.0 * s * s


def turn(head, cosine, sine):
    return head * cosine + pltpu.roll(head, 64, 1) * sine


def forward_kernel(
    tokens, pos, gains, qkvw, ow, gw, uw, dw, cot, freq, perm, permo,
    a1, stats, qkv, kvr, att, cosb, sinb, middle, mf, cotf, gn, wqkv, wo, wg, wu, wd,
    xf, posb, wpad, acc, top, tot, packed, part, slots, send, recv, local,
):
    here = Place()
    links = Links(send, recv, local)
    x, y, zl, zh, core, quarter = here.x, here.y, here.zl, here.zh, here.core, here.quarter
    hid = zh * 4 + y
    here.enter()

    own_qkv = wqkv.at[zh, x, zl, core]
    own_o = wo.at[zh, zl, core, :, lanes(x, 384)]
    src_qkv, src_o = qkvw.at[pl.ds(quarter * 96, 96)], ow.at[pl.ds(quarter * 48, 48)]
    mirror = [links.make(src_qkv, own_qkv, here.mirror), links.make(src_o, own_o, here.mirror)]
    stay = [pltpu.make_async_copy(src_qkv, own_qkv, local.at[0]), pltpu.make_async_copy(src_o, own_o, local.at[1])]
    links.local_count = 2

    @pl.when(x != y)
    def _():
        for copy in mirror:
            copy.start()

    @pl.when(x == y)
    def _():
        for copy in stay:
            copy.start()

    ring_x = RingGather(links, here, lambda half: tokens.at[half], xf)
    kept = [links.keep(tokens, xf.at[:, lanes(x, 384)])]
    small = []
    for peer in (here.right, here.left, here.far):
        small += [links.start(pos, posb.at[x], peer), links.start(gains, gn.at[:, lanes(x, 384)], peer)]
    kept += [links.keep(pos, posb.at[x]), links.keep(gains, gn.at[:, lanes(x, 384)])]

    def hidden_slices(ref_g, ref_u, ref_d, target):
        rows = pl.ds(quarter * 96, 96)
        return [
            (ref_g.at[rows, lanes(target, 128)], wg.at[x, zl, core, :, lanes(hid, 128)]),
            (ref_u.at[rows, lanes(target, 128)], wu.at[x, zl, core, :, lanes(hid, 128)]),
            (ref_d.at[pl.ds(target * 128 + quarter * 32, 32)], wd.at[zh, y, zl, core, :, lanes(x, 384)]),
        ]

    swaps = []
    for peer, target in ((here.right, here.ahead), (here.left, here.behind), (here.far, here.across)):
        swaps += [links.start(src, dst, peer) for src, dst in hidden_slices(gw, uw, dw, target)]
    swap_kept = [links.keep(src, dst) for src, dst in hidden_slices(gw, uw, dw, x)]

    @pl.when(x != y)
    def _():
        for copy in mirror:
            copy.wait()

    @pl.when(x == y)
    def _():
        for copy in stay:
            copy.wait()

    a, b, oa, ob = pl.ds(0, 48), pl.ds(48, 48), pl.ds(0, 32), pl.ds(32, 16)
    y_cols = lanes(y, 384)
    head_a = links.spread(wqkv.at[zh, y, zl, core, a], here.ys)
    head_b = links.spread(wqkv.at[zh, y, zl, core, b], here.zs)
    head_a += links.spread(wo.at[zh, zl, core, oa, y_cols], here.ys)
    head_b += links.spread(wo.at[zh, zl, core, ob, y_cols], here.zs)
    ring_x.forward()
    arrive(head_a)
    head_a = links.spread(wqkv.at[zh, :, zl, core, a], here.zs)
    head_a += links.spread(wo.at[zh, zl, core, oa], here.zs)
    arrive(head_b)
    head_b = links.spread(wqkv.at[:, y, :, core, b], here.ys)
    head_b += links.spread(wo.at[:, :, core, ob, y_cols], here.ys)

    for copy in kept:
        copy.wait()
    arrive(small)
    mine = posb[y]
    mine = jnp.where(zh == 0, mine[0:4], mine[4:8]).astype(f32)
    lane = lax.broadcasted_iota(i32, (128, 128), 1)
    for c in range(4):
        column = jnp.broadcast_to(mine[c : c + 1], (128, 128)).T
        sine, cosine = sine_cosine(column * freq[0:1])
        cosb[pl.ds(c * 128, 128)] = cosine
        sinb[pl.ds(c * 128, 128)] = jnp.where(lane < 64, -sine, sine)

    ring_x.finish()
    ring_c = RingGather(links, here, lambda half: cot.at[half], cotf)
    cot_kept = links.keep(cot, cotf.at[:, lanes(x, 384)])

    def norm_rows(i, _):
        rows = pl.ds(pl.multiple_of(i * 64, 64), 64)
        value = xf[rows].astype(f32)
        inverse = lax.rsqrt(jnp.sum(value * value, axis=1, keepdims=True) * (1.0 / D) + epsilon)
        a1[rows] = (value * gn[0:1]).astype(bf16)
        stats[rows] = jnp.broadcast_to(inverse, (64, 128))
        return 0

    lax.fori_loop(0, 8, norm_rows, 0)

    arrive(head_a)
    arrive(head_b)
    core_qkv = links.spread(wqkv.at[:, :, :, core], [here.twin])
    core_o = links.spread(wo.at[:, :, core], [here.twin])

    for copy in swap_kept:
        copy.wait()
    arrive(swaps)
    hidden_a, hidden_b = [], []
    for ref in (wg, wu):
        hidden_a += links.spread(ref.at[:, zl, core, a, lanes(hid, 128)], here.ys)
        hidden_b += links.spread(ref.at[:, zl, core, b, lanes(hid, 128)], here.zs)
    da, db = pl.ds(0, 16), pl.ds(16, 16)
    hidden_a += links.spread(wd.at[zh, y, zl, core, da], here.ys)
    hidden_b += links.spread(wd.at[zh, y, zl, core, db], here.zs)

    arrive(core_qkv)

    def widen(i, _):
        rows = 4 * 96

        def block(j, _):
            w = wqkv[i, j].reshape(rows, 384)
            wpad[i, pl.ds(pl.multiple_of(j * rows, rows), rows)] = dot(w, perm[...]).astype(bf16)
            return 0

        lax.fori_loop(0, 4, block, 0)
        return 0

    lax.fori_loop(0, 2, widen, 0)

    def keys_values(g, _):
        pair = dot(a1[...], wpad[g, :, 256:512])
        inverse = stats[...]
        qkv[:, lanes(g * 4 + 2, 128)] = turn(pair[:, :128] * inverse, cosb[...], sinb[...]).astype(bf16)
        qkv[:, lanes(g * 4 + 3, 128)] = (pair[:, 128:] * inverse).astype(bf16)
        return 0

    lax.fori_loop(0, 2, keys_values, 0)
    over = [
        links.make(qkv.at[:, pl.ds(g * 512 + 256, 256)], kvr.at[g], here.zs[2]) for g in range(2)
    ]

    @pl.when(zh == 0)
    def _():
        for copy in over:
            copy.start()

    def queries(g, _):
        pair = dot(a1[...], wpad[g, :, 0:256])
        inverse = stats[...]
        for h in range(2):
            head = pair[:, h * 128 : h * 128 + 128] * inverse
            qkv[:, lanes(g * 4 + h, 128)] = turn(head, cosb[...], sinb[...]).astype(bf16)
        return 0

    lax.fori_loop(0, 2, queries, 0)
    ring_c.forward()

    def own_keys(i, _):
        g = i // 2
        for qb in range(2):
            rows, keys = pl.ds(qb * 256, 256), pl.ds(0, qb * 256 + 256)
            q = qkv[rows, lanes(g * 4 + i % 2, 128)]
            s = dot_t(q, qkv[keys, lanes(g * 4 + 2, 128)]) * score_scale
            index = lax.broadcasted_iota(i32, s.shape, 0) + qb * 256
            s = jnp.where(lax.broadcasted_iota(i32, s.shape, 1) <= index, s, masked_score)
            m = jnp.max(s, axis=1, keepdims=True)
            e = jnp.exp2(s - m)
            acc[i, rows] = dot(e.astype(bf16), qkv[keys, lanes(g * 4 + 3, 128)])
            top[i, rows] = jnp.broadcast_to(m, (256, 128))
            tot[i, rows] = jnp.broadcast_to(jnp.sum(e, axis=1, keepdims=True), (256, 128))
        return 0

    lax.fori_loop(0, 4, own_keys, 0)

    arrive(hidden_a)
    hidden_a = []
    for ref in (wg, wu):
        hidden_a += links.spread(ref.at[:, zl, core, a, lanes(zh, 512)], here.zs)
    hidden_a += links.spread(wd.at[zh, :, zl, core, da], here.zs)
    arrive(hidden_b)
    hidden_b = []
    for ref in (wg, wu):
        for other in range(2):
            hidden_b += links.spread(ref.at[:, :, core, b, lanes(other * 4 + y, 128)], here.ys)
    hidden_b += links.spread(wd.at[:, y, :, core, db], here.ys)

    @pl.when(zh == 1)
    def _():
        for copy in over:
            copy.wait_recv()

        def first_half(i, _):
            g = i // 2
            for qb in range(2):
                rows = pl.ds(qb * 256, 256)
                q = qkv[rows, lanes(g * 4 + i % 2, 128)]
                s = dot_t(q, kvr[g, :, 0:128]) * score_scale
                old = top[i, rows][:, 0:1]
                m = jnp.maximum(old, jnp.max(s, axis=1, keepdims=True))
                e = jnp.exp2(s - m)
                shrink = jnp.exp2(old - m)
                acc[i, rows] = acc[i, rows] * shrink + dot(e.astype(bf16), kvr[g, :, 128:256])
                tot[i, rows] = tot[i, rows] * shrink + jnp.sum(e, axis=1, keepdims=True)
                top[i, rows] = jnp.broadcast_to(m, (256, 128))
            return 0

        lax.fori_loop(0, 4, first_half, 0)

    @pl.when(zh == 0)
    def _():
        for copy in over:
            copy.wait_send()

    lane = lax.broadcasted_iota(i32, (512, 128), 1)
    for i in range(4):
        att[:, i * 128 : i * 128 + 128] = (acc[i] / tot[i]).astype(bf16)
        stats[...] = jnp.where(lane == i, top[i] + jnp.log2(tot[i]), stats[...])

    arrive(core_o)
    packed[...] = dot(att[...], permo[...]).astype(bf16)

    def project(block):
        w = wo[:, :, :, :, lanes(block, 384)].reshape(384, 384)
        return dot(packed[...], w)

    scatter = RingScatter(links, here, part, slots)
    part[here.across] = project(here.across).astype(bf16)
    scatter.send_far()
    part[here.ahead] = project(here.ahead).astype(bf16)
    part[here.behind] = project(here.behind).astype(bf16)
    scatter.send_near()
    middle[...] = project(x) + xf[:, lanes(x, 384)].astype(f32)
    scatter.forward()
    cot_kept.wait()
    ring_c.finish()
    scatter.finish()
    for half, rows in enumerate((H0, H1)):
        middle[rows] = middle[rows] + scatter.received(half)
    own = lanes(x, 384)
    mf[:, own] = middle[...].astype(bf16)
    ring_m = RingGather(links, here, lambda half: mf.at[half, own], mf)
    ring_m.forward()

    arrive(hidden_a)
    arrive(hidden_b)
    cores = [links.start(ref.at[:, :, core], ref.at[:, :, core], here.twin) for ref in (wg, wu)]
    cores.append(links.start(wd.at[:, :, :, core], wd.at[:, :, :, core], here.twin))
    ring_m.finish()
    arrive(cores)
    links.close()


def run_forward(tokens, pos, gains, qkvw, ow, gw, uw, dw, cot, consts):
    s = jax.ShapeDtypeStruct
    outs = [
        ("a1", (512, D), bf16, VM),
        ("stats", (512, 128), f32, VM),
        ("qkv", (512, 1024), bf16, VM),
        ("kvr", (2, 512, 256), bf16, VM),
        ("att", (512, 512), bf16, VM),
        ("cos", (512, 128), f32, VM),
        ("sin", (512, 128), f32, VM),
        ("middle", (512, 384), f32, VM),
        ("mf", (512, D), bf16, VM),
        ("cotf", (512, D), bf16, ANY),
        ("gn", (8, D), f32, VM),
        ("wqkv", (2, 4, 2, 2, 96, 384), bf16, VM),
        ("wo", (2, 2, 2, 48, D), bf16, VM),
        ("wg", (4, 2, 2, 96, 1024), bf16, ANY),
        ("wu", (4, 2, 2, 96, 1024), bf16, ANY),
        ("wd", (2, 4, 2, 2, 32, D), bf16, ANY),
    ]
    count = 128
    result = pl.pallas_call(
        forward_kernel,
        out_shape=[s(shape, dtype) for _, shape, dtype, _ in outs],
        in_specs=[ANY] * 9 + [VM] * 3,
        out_specs=[spec for _, _, _, spec in outs],
        scratch_shapes=[
            pltpu.VMEM((512, D), bf16),
            pltpu.VMEM((4, 8, 128), i32),
            pltpu.VMEM((2, D, 512), bf16),
            pltpu.VMEM((4, 512, 128), f32),
            pltpu.VMEM((4, 512, 128), f32),
            pltpu.VMEM((4, 512, 128), f32),
            pltpu.VMEM((512, 384), bf16),
            pltpu.VMEM((4, 512, 384), bf16),
            pltpu.VMEM((6, 256, 384), bf16),
            pltpu.SemaphoreType.DMA((count,)),
            pltpu.SemaphoreType.DMA((count,)),
            pltpu.SemaphoreType.DMA((16,)),
        ],
        compiler_params=pltpu.CompilerParams(
            collective_id=0, has_side_effects=True, vmem_limit_bytes=56 * 1024 * 1024
        ),
        name="forward",
    )(tokens, pos, gains, qkvw, ow, gw, uw, dw, cot, *consts)
    return {name: value for (name, _, _, _), value in zip(outs, result)}


def constants():
    half = HD // 2
    freq = np.zeros((8, 128), np.float32)
    rates = rope_base ** (-(np.arange(half) * 2.0 / HD))
    freq[:, :half] = rates
    freq[:, 64 : 64 + half] = rates
    perm = np.zeros((384, 512), np.float32)
    permo = np.zeros((512, 384), np.float32)
    for h in range(4):
        for d in range(HD):
            wide = d if (h == 3 or d < half) else d - half + 64
            perm[h * HD + d, h * 128 + wide] = 1
            permo[h * 128 + d, h * HD + d] = 1
    return jnp.asarray(freq), jnp.asarray(perm, bf16), jnp.asarray(permo, bf16)


def dot_first(a, b):
    return lax.dot_general(a, b, (((0,), (0,)), ((), ())), preferred_element_type=f32)


def column_to_rows(column, ref):
    for c in range(4):
        block = jnp.broadcast_to(column[c * 128 : c * 128 + 128], (128, 128)).T
        ref[c : c + 1] = block[0:1]


def rows_to_column(rows):
    return jnp.concatenate([jnp.broadcast_to(rows[c : c + 1], (128, 128)).T for c in range(4)], 0)


def backward_kernel(
    tokens, a1_in, stats, qkv, kvr, att, cosb, sinb, middle, mf_in, cotf, gn, wqkv_in, wo_in, wg_in, wu_in, wd_in,
    perm, permo,
    mixed, tgrad, dgain, fin_q, fin_o, fin_g, fin_u, fin_d,
    wqkv, wo, wg, wu, wd, a2, wide, hidden, dgate, dup, part, partd, slots, dzf, dmid, turned, datt, packed,
    dq, dkv, dkr, dks, dkin, dproj, small, sums, gains, rc_g, rc_u, rc_d, rc_q, rc_o,
    za_g, za_u, za_d, yb_g, yb_u, yb_d, ya_g, ya_u, ya_d, zb_g, zb_u, zb_d,
    za_q, za_o, yb_q, yb_o, ya_q, ya_o, zb_q, zb_o, send, recv, local,
):
    here = Place()
    links = Links(send, recv, local)
    x, y, zl, zh, core = here.x, here.y, here.zl, here.zh, here.core
    hid = zh * 4 + y
    own = lanes(x, 384)
    y_cols = lanes(y, 384)
    loads = [
        links.keep(src, dst)
        for src, dst in ((mf_in, a2), (wg_in, wg), (wu_in, wu), (wd_in, wd), (wo_in, wo), (wqkv_in, wqkv))
    ]
    dq[...] = jnp.zeros_like(dq)
    dkv[...] = jnp.zeros_like(dkv)
    here.enter()

    loads[0].wait()

    def norm_rows(i, _):
        rows = pl.ds(pl.multiple_of(i * 64, 64), 64)
        value = a2[rows].astype(f32)
        inverse = lax.rsqrt(jnp.sum(value * value, axis=1, keepdims=True) * (1.0 / D) + epsilon)
        a2[rows] = (value * inverse * gn[1:2]).astype(bf16)
        wide[rows] = jnp.broadcast_to(inverse, (64, 128))
        return 0

    lax.fori_loop(0, 8, norm_rows, 0)
    for copy in loads[1:4]:
        copy.wait()

    sums[...] = jnp.zeros_like(sums)

    def units(n, _):
        cols = lanes(n, 256)
        w_g = wg[:, :, :, :, cols].reshape(D, 256)
        w_u = wu[:, :, :, :, cols].reshape(D, 256)
        w_d = wd[n // 2, pl.ds((n % 2) * 2, 2)].reshape(256, D)
        for rows in (H0, H1):
            gate = dot(a2[rows], w_g)
            up = dot(a2[rows], w_u)
            dh = dot_t(cotf[rows], w_d)
            sg = 1.0 / (1.0 + jnp.exp(-gate))
            silu = gate * sg
            dg = (dh * up * (sg + silu * (1.0 - sg))).astype(bf16)
            du = (dh * silu).astype(bf16)
            hidden[rows, cols] = (silu * up).astype(bf16)
            dgate[rows, cols] = dg
            dup[rows, cols] = du
            inner = jnp.sum(dg.astype(f32) * gate + du.astype(f32) * up, axis=1, keepdims=True)
            sums[rows] = sums[rows] + inner
        return 0

    lax.fori_loop(0, 4, units, 0)

    def back_block(block):
        w_g = wg[block].reshape(384, 1024)
        w_u = wu[block].reshape(384, 1024)
        return dot_t(dgate[...], w_g) + dot_t(dup[...], w_u)

    scatter = RingScatter(links, here, part, slots.at[0])
    part[here.across] = back_block(here.across).astype(bf16)
    scatter.send_far()
    part[here.ahead] = back_block(here.ahead).astype(bf16)
    part[here.behind] = back_block(here.behind).astype(bf16)
    scatter.send_near()
    column_to_rows(sums[...], small.at[0, x])
    inner_sums = [links.start(small.at[0, x], small.at[0, x], p) for p in (here.right, here.left, here.far)]
    dmid[...] = back_block(x)
    scatter.forward()

    def down_block(block, _):
        cols = lanes(block, 384)
        partd[block] = dot(hidden[...], wd[:, :, :, :, :, cols].reshape(1024, 384)).astype(bf16)
        return 0

    lax.fori_loop(0, 4, down_block, 0)

    def down_grad(n, _):
        rows = hidden[:, lanes(n, 256)].T
        for c in range(3):
            cols = pl.ds(c * 512, 512)
            value = dot(rows, cotf[:, cols]).astype(bf16)
            wd[n // 2, pl.ds((n % 2) * 2, 2), :, :, :, cols] = value.reshape(2, 2, 2, 32, 512)
        return 0

    lax.fori_loop(0, 4, down_grad, 0)
    other = 1 - core
    cores = [links.start(wd.at[:, :, :, other], rc_d, here.twin)]

    def up_grads(block, _):
        rows = a2[:, lanes(block, 384)].T
        for source, target in ((dgate, wg), (dup, wu)):
            for c in range(2):
                cols = pl.ds(c * 512, 512)
                target[block, :, :, :, cols] = dot(rows, source[:, cols]).astype(bf16).reshape(2, 2, 96, 512)
        return 0

    lax.fori_loop(0, 4, up_grads, 0)
    cores += [
        links.start(wg.at[:, :, other], rc_g, here.twin),
        links.start(wu.at[:, :, other], rc_u, here.twin),
    ]
    load_a1 = links.keep(a1_in, a2)

    arrive(inner_sums)
    inner = rows_to_column(jnp.sum(small[0], axis=0)[0:4])[:, 0:1]
    scatter.finish()
    gains[...] = jnp.zeros_like(gains)
    for half, rows in enumerate((H0, H1)):
        da2 = dmid[rows] + scatter.received(half)
        m, inverse = middle[rows], wide[rows][:, 0:1]
        gains[1:2] = gains[1:2] + jnp.sum(da2 * m * inverse, axis=0, keepdims=True)
        factor = inner[half * 256 : half * 256 + 256] * inverse * inverse * (1.0 / D)
        value = cotf[rows, own].astype(f32) + inverse * gn[1:2, own] * da2 - m * factor
        dmid[rows] = value
        dzf[rows, own] = value.astype(bf16)
    ring_z = RingGather(links, here, lambda half: dzf.at[half, own], dzf)
    ring_z.forward()

    arrive(cores)

    def core_sum(i, _):
        for target, source in ((wg, rc_g), (wu, rc_u)):
            for j in range(2):
                target[i, j, core] = (target[i, j, core].astype(f32) + source[i, j].astype(f32)).astype(bf16)
        for k in range(2):
            for j in range(2):
                value = wd[k, i, j, core].astype(f32) + rc_d[k, i, j].astype(f32)
                wd[k, i, j, core] = value.astype(bf16)
        return 0

    lax.fori_loop(0, 4, core_sum, 0)
    a, b, da, db, oa, ob = pl.ds(0, 48), pl.ds(48, 48), pl.ds(0, 16), pl.ds(16, 16), pl.ds(0, 32), pl.ds(32, 16)
    z_places = [(1 - zl, zh), (1 - zl, 1 - zh), (zl, 1 - zh)]
    y_places = [(y + k) % 4 for k in (1, 3, 2)]
    round_a, round_b = [], []
    for j, (pzl, pzh) in enumerate(z_places):
        for ref, slot in ((wg, za_g), (wu, za_u)):
            round_a.append(links.start(ref.at[:, pzl, core, a, lanes(pzh, 512)], slot.at[j], here.zs[j]))
        round_a.append(links.start(wd.at[pzh, :, pzl, core, da], za_d.at[j], here.zs[j]))
    for j, py in enumerate(y_places):
        for ref, slot in ((wg, yb_g), (wu, yb_u)):
            for k in range(2):
                round_b.append(
                    links.start(ref.at[:, :, core, b, lanes(k * 4 + py, 128)], slot.at[j, k], here.ys[j])
                )
        round_b.append(links.start(wd.at[:, py, :, core, db], yb_d.at[j], here.ys[j]))

    ring_z.finish()

    scatter_d = RingScatter(links, here, partd, slots.at[1])
    scatter_d.send_far()
    scatter_d.send_near()

    loads[4].wait()
    packed[...] = dot_t(dzf[...], wo[...].reshape(384, D)).astype(bf16)
    datt[...] = dot_t(packed[...], permo[...]).astype(bf16)
    packed[...] = dot(att[...], permo[...]).astype(bf16)
    for c in range(3):
        cols = pl.ds(c * 512, 512)
        value = dot_first(packed[...], dzf[:, cols]).astype(bf16)
        wo[:, :, :, :, cols] = value.reshape(2, 2, 2, 48, 512)

    def pair(i, rows, k, v, visible):
        g = i // 2
        head = lanes(i, 128)
        q, grad = qkv[rows, lanes(g * 4 + i % 2, 128)], datt[rows, head]
        delta = jnp.sum(grad.astype(f32) * att[rows, head].astype(f32), axis=1, keepdims=True)
        lane = lax.broadcasted_iota(i32, (256, 128), 1)
        lse = jnp.sum(jnp.where(lane == i, stats[rows], 0.0), axis=1, keepdims=True)
        s = dot_t(q, k) * score_scale
        if visible is not None:
            s = jnp.where(visible(s.shape), s, masked_score)
        p = jnp.exp2(s - lse)
        ds = (p * (dot_t(grad, v) - delta) * (1.0 / math.sqrt(HD))).astype(bf16)
        dq[i, rows] = dq[i, rows] + dot(ds, k)
        return dot_first(ds, q), dot_first(p.astype(bf16), grad)

    give = [links.make(dks.at[g], dkin.at[g], here.zs[2]) for g in range(2)]

    @pl.when(zh == 1)
    def _():
        dkr[...] = jnp.zeros_like(dkr)

        def first_half(i, _):
            g = i // 2
            for qb in range(2):
                dk, dv = pair(i, pl.ds(qb * 256, 256), kvr[g, :, 0:128], kvr[g, :, 128:256], None)
                dkr[g, :, 0:128] = dkr[g, :, 0:128] + dk
                dkr[g, :, 128:256] = dkr[g, :, 128:256] + dv
            return 0

        for g in range(2):
            lax.fori_loop(2 * g, 2 * g + 2, first_half, 0)
            dks[g] = dkr[g].astype(bf16)
            give[g].start()

    scatter_d.forward()

    def own_keys(i, _):
        g = i // 2
        for qb in range(2):
            keys = pl.ds(0, qb * 256 + 256)

            def visible(shape):
                rows = lax.broadcasted_iota(i32, shape, 0) + qb * 256
                return lax.broadcasted_iota(i32, shape, 1) <= rows

            k, v = qkv[keys, lanes(g * 4 + 2, 128)], qkv[keys, lanes(g * 4 + 3, 128)]
            dk, dv = pair(i, pl.ds(qb * 256, 256), k, v, visible)
            dkv[g, keys, 0:128] = dkv[g, keys, 0:128] + dk
            dkv[g, keys, 128:256] = dkv[g, keys, 128:256] + dv
        return 0

    lax.fori_loop(0, 4, own_keys, 0)

    @pl.when(zh == 0)
    def _():
        for g in range(2):
            give[g].wait_recv()
            dkv[g] = dkv[g] + dkin[g].astype(f32)

    @pl.when(zh == 1)
    def _():
        for g in range(2):
            give[g].wait_send()

    arrive(round_a)
    for ref, slot in ((wg, za_g), (wu, za_u)):

        def add_z(i, _, ref=ref, slot=slot):
            cols = lanes(zh, 512)
            value = ref[i, zl, core, a, cols].astype(f32)
            for j in range(3):
                value = value + slot[j, i].astype(f32)
            ref[i, zl, core, a, cols] = value.astype(bf16)
            return 0

        lax.fori_loop(0, 4, add_z, 0)
    value = wd[zh, :, zl, core, da].astype(f32)
    for j in range(3):
        value = value + za_d[j].astype(f32)
    wd[zh, :, zl, core, da] = value.astype(bf16)
    round_a = []
    for j, py in enumerate(y_places):
        for ref, slot in ((wg, ya_g), (wu, ya_u)):
            round_a.append(
                links.start(ref.at[:, zl, core, a, lanes(zh * 4 + py, 128)], slot.at[j], here.ys[j])
            )
        round_a.append(links.start(wd.at[zh, py, zl, core, da], ya_d.at[j], here.ys[j]))
    arrive(round_b)
    for ref, slot in ((wg, yb_g), (wu, yb_u)):

        def add_y(i, _, ref=ref, slot=slot):
            for k in range(2):
                cols = lanes(k * 4 + y, 128)
                value = ref[i, :, core, b, cols].astype(f32)
                for j in range(3):
                    value = value + slot[j, k, i].astype(f32)
                ref[i, :, core, b, cols] = value.astype(bf16)
            return 0

        lax.fori_loop(0, 4, add_y, 0)
    value = wd[:, y, :, core, db].astype(f32)
    for j in range(3):
        value = value + yb_d[j].astype(f32)
    wd[:, y, :, core, db] = value.astype(bf16)
    round_b = []
    for j, (pzl, pzh) in enumerate(z_places):
        for ref, slot in ((wg, zb_g), (wu, zb_u)):
            round_b.append(
                links.start(ref.at[:, pzl, core, b, lanes(pzh * 4 + y, 128)], slot.at[j], here.zs[j])
            )
        round_b.append(links.start(wd.at[pzh, y, pzl, core, db], zb_d.at[j], here.zs[j]))

    sums[...] = jnp.zeros_like(sums)
    inverse = stats[:, 4:5]
    for i in range(4):
        q_cols = pl.ds((i // 2 * 4 + i % 2) * 128, 128)
        value = dq[i]
        sums[...] = sums[...] + jnp.sum(value * qkv[:, q_cols].astype(f32), axis=1, keepdims=True)
        turned[:, q_cols] = (turn(value, cosb[...], -sinb[...]) * inverse).astype(bf16)
    for g in range(2):
        kv_cols = pl.ds(g * 512 + 256, 256)
        value = dkv[g]
        sums[...] = sums[...] + jnp.sum(value * qkv[:, kv_cols].astype(f32), axis=1, keepdims=True)
        turned[:, g * 512 + 256 : g * 512 + 384] = (
            turn(value[:, :128], cosb[...], -sinb[...]) * inverse
        ).astype(bf16)
        turned[:, g * 512 + 384 : g * 512 + 512] = (value[:, 128:] * inverse).astype(bf16)
    column_to_rows(sums[...], small.at[1, x])
    inner_sums = [links.start(small.at[1, x], small.at[1, x], p) for p in (here.right, here.left, here.far)]
    for g in range(2):
        dproj[g] = dot_t(turned[:, g * 512 : g * 512 + 512], perm[...]).astype(bf16)
    loads[5].wait()

    def back_input(block):
        return sum(dot_t(dproj[g], wqkv[g, block].reshape(384, 384)) for g in range(2))

    scatter_d.finish()
    links.close()
    scatter = RingScatter(links, here, part, slots.at[2])
    part[here.across] = back_input(here.across).astype(bf16)
    scatter.send_far()
    part[here.ahead] = back_input(here.ahead).astype(bf16)
    part[here.behind] = back_input(here.behind).astype(bf16)
    scatter.send_near()
    tgrad[...] = back_input(x)

    load_a1.wait()

    def qkv_grads(block, _):
        rows = a2[:, lanes(block, 384)].T
        for g in range(2):
            wqkv[g, block] = dot(rows, dproj[g]).astype(bf16).reshape(2, 2, 96, 384)
        return 0

    lax.fori_loop(0, 4, qkv_grads, 0)
    cores = [
        links.start(wqkv.at[:, :, :, other], rc_q, here.twin),
        links.start(wo.at[:, :, other], rc_o, here.twin),
    ]
    scatter.forward()

    for half, rows in enumerate((H0, H1)):
        mixed[rows] = middle[rows] + partd[x, rows].astype(f32) + scatter_d.received(half)

    arrive(round_a)
    for ref, slot in ((wg, ya_g), (wu, ya_u)):
        cols = lanes(hid, 128)
        value = ref[:, zl, core, a, cols].astype(f32)
        for j in range(3):
            value = value + slot[j].astype(f32)
        ref[:, zl, core, a, cols] = value.astype(bf16)
    value = wd[zh, y, zl, core, da].astype(f32)
    for j in range(3):
        value = value + ya_d[j].astype(f32)
    wd[zh, y, zl, core, da] = value.astype(bf16)
    arrive(round_b)
    for ref, slot in ((wg, zb_g), (wu, zb_u)):
        cols = lanes(hid, 128)
        value = ref[:, zl, core, b, cols].astype(f32)
        for j in range(3):
            value = value + slot[j].astype(f32)
        ref[:, zl, core, b, cols] = value.astype(bf16)
    value = wd[zh, y, zl, core, db].astype(f32)
    for j in range(3):
        value = value + zb_d[j].astype(f32)
    wd[zh, y, zl, core, db] = value.astype(bf16)

    def hidden_blocks(target):
        return [
            (wg.at[target, zl, core, :, lanes(hid, 128)], fin_g.at[zl, core, :, lanes(x, 128)]),
            (wu.at[target, zl, core, :, lanes(hid, 128)], fin_u.at[zl, core, :, lanes(x, 128)]),
            (wd.at[zh, y, zl, core, :, lanes(target, 384)], fin_d.at[x, zl, core]),
        ]

    swaps = []
    for peer, target in ((here.right, here.ahead), (here.left, here.behind), (here.far, here.across)):
        swaps += [links.start(src, dst, peer) for src, dst in hidden_blocks(target)]
    swap_kept = [links.keep(src, dst) for src, dst in hidden_blocks(x)]

    arrive(cores)
    for g in range(2):

        def core_heads(i, _, g=g):
            for j in range(2):
                value = wqkv[g, i, j, core].astype(f32) + rc_q[g, i, j].astype(f32)
                wqkv[g, i, j, core] = value.astype(bf16)
            return 0

        lax.fori_loop(0, 4, core_heads, 0)
        for j in range(2):
            wo[g, j, core] = (wo[g, j, core].astype(f32) + rc_o[g, j].astype(f32)).astype(bf16)
    round_a, round_b = [], []
    for j, (pzl, pzh) in enumerate(z_places):
        round_a.append(links.start(wqkv.at[pzh, :, pzl, core, a], za_q.at[j], here.zs[j]))
        round_a.append(links.start(wo.at[pzh, pzl, core, oa], za_o.at[j], here.zs[j]))
    for j, py in enumerate(y_places):
        round_b.append(links.start(wqkv.at[:, py, :, core, b], yb_q.at[j], here.ys[j]))
        round_b.append(links.start(wo.at[:, :, core, ob, lanes(py, 384)], yb_o.at[j], here.ys[j]))

    arrive(inner_sums)
    inner = rows_to_column(jnp.sum(small[1], axis=0)[0:4])[:, 0:1]
    scatter.finish()
    for half, rows in enumerate((H0, H1)):
        da1 = tgrad[rows] + scatter.received(half)
        source, rinv = tokens[rows].astype(f32), stats[rows][:, 4:5]
        gains[0:1] = gains[0:1] + jnp.sum(da1 * source, axis=0, keepdims=True)
        factor = inner[half * 256 : half * 256 + 256] * rinv * rinv * (1.0 / D)
        tgrad[rows] = dmid[rows] + gn[0:1, own] * da1 - source * factor
    dgain[0] = gains[...]
    gain_y = [links.start(dgain.at[0], dgain.at[1 + j], here.ys[j]) for j in range(3)]

    for copy in swap_kept:
        copy.wait()
    arrive(swaps)
    fins = ((fin_g, 0), (fin_u, 0), (fin_d, 1))
    pick = lambda ref, lead, index: ref.at[(slice(None),) * lead + index]
    over = [pick(ref, lead, (zl, core)) for ref, lead in fins]
    across_zl = [links.start(v, v, here.zs[0]) for v in over]

    arrive(round_a)
    value = wqkv[zh, :, zl, core, a].astype(f32)
    value_o = wo[zh, zl, core, oa].astype(f32)
    for j in range(3):
        value = value + za_q[j].astype(f32)
        value_o = value_o + za_o[j].astype(f32)
    wqkv[zh, :, zl, core, a] = value.astype(bf16)
    wo[zh, zl, core, oa] = value_o.astype(bf16)
    round_a = []
    for j, py in enumerate(y_places):
        round_a.append(links.start(wqkv.at[zh, py, zl, core, a], ya_q.at[j], here.ys[j]))
        round_a.append(links.start(wo.at[zh, zl, core, oa, lanes(py, 384)], ya_o.at[j], here.ys[j]))
    arrive(round_b)
    value = wqkv[:, y, :, core, b].astype(f32)
    value_o = wo[:, :, core, ob, y_cols].astype(f32)
    for j in range(3):
        value = value + yb_q[j].astype(f32)
        value_o = value_o + yb_o[j].astype(f32)
    wqkv[:, y, :, core, b] = value.astype(bf16)
    wo[:, :, core, ob, y_cols] = value_o.astype(bf16)
    round_b = []
    for j, (pzl, pzh) in enumerate(z_places):
        round_b.append(links.start(wqkv.at[pzh, y, pzl, core, b], zb_q.at[j], here.zs[j]))
        round_b.append(links.start(wo.at[pzh, pzl, core, ob, y_cols], zb_o.at[j], here.zs[j]))

    arrive(gain_y)
    gains[...] = dgain[0] + dgain[1] + dgain[2] + dgain[3]
    dgain[4] = gains[...]
    gain_z = [links.start(dgain.at[4], dgain.at[5 + j], here.zs[j]) for j in range(3)]
    arrive(across_zl)
    both = [pick(ref, lead, (slice(None), core)) for ref, lead in fins]
    to_core = [links.start(v, v, here.twin) for v in both]

    arrive(round_a)
    value = wqkv[zh, y, zl, core, a].astype(f32)
    value_o = wo[zh, zl, core, oa, y_cols].astype(f32)
    for j in range(3):
        value = value + ya_q[j].astype(f32)
        value_o = value_o + ya_o[j].astype(f32)
    wqkv[zh, y, zl, core, a] = value.astype(bf16)
    wo[zh, zl, core, oa, y_cols] = value_o.astype(bf16)
    arrive(round_b)
    value = wqkv[zh, y, zl, core, b].astype(f32)
    value_o = wo[zh, zl, core, ob, y_cols].astype(f32)
    for j in range(3):
        value = value + zb_q[j].astype(f32)
        value_o = value_o + zb_o[j].astype(f32)
    wqkv[zh, y, zl, core, b] = value.astype(bf16)
    wo[zh, zl, core, ob, y_cols] = value_o.astype(bf16)
    src_q, src_o = wqkv.at[zh, y, zl, core], wo.at[zh, zl, core, :, y_cols]
    dst_q, dst_o = fin_q.at[zl, core], fin_o.at[zl, core]
    mirror = [links.make(src_q, dst_q, here.mirror), links.make(src_o, dst_o, here.mirror)]
    first = links.local_count
    stay = [pltpu.make_async_copy(src_q, dst_q, local.at[first]), pltpu.make_async_copy(src_o, dst_o, local.at[first + 1])]

    @pl.when(x != y)
    def _():
        for copy in mirror:
            copy.start()
        for copy in mirror:
            copy.wait()

    @pl.when(x == y)
    def _():
        for copy in stay:
            copy.start()
        for copy in stay:
            copy.wait()

    head_zl = [links.start(v, v, here.zs[0]) for v in (fin_q.at[zl, core], fin_o.at[zl, core])]
    arrive(gain_z)
    gains[...] = dgain[4] + dgain[5] + dgain[6] + dgain[7]
    dgain[8] = gains[...]
    gain_c = links.start(dgain.at[8], dgain.at[9], here.twin)
    arrive(head_zl)
    head_core = [links.start(v, v, here.twin) for v in (fin_q.at[:, core], fin_o.at[:, core])]
    arrive([gain_c])
    arrive(to_core)
    arrive(head_core)
    links.close()


def run_backward(tokens, k, consts):
    s = jax.ShapeDtypeStruct
    v = pltpu.VMEM
    _, perm, permo = consts
    outs = [
        s((512, 384), f32),
        s((512, 384), f32),
        s((10, 8, 384), f32),
        s((2, 2, 96, 384), bf16),
        s((2, 2, 48, 384), bf16),
        s((2, 2, 96, 512), bf16),
        s((2, 2, 96, 512), bf16),
        s((4, 2, 2, 32, 384), bf16),
    ]
    scratch = [
        v((2, 4, 2, 2, 96, 384), bf16),
        v((2, 2, 2, 48, D), bf16),
        v((4, 2, 2, 96, 1024), bf16),
        v((4, 2, 2, 96, 1024), bf16),
        v((2, 4, 2, 2, 32, D), bf16),
        v((512, D), bf16),
        v((512, 128), f32),
        v((512, 1024), bf16),
        v((512, 1024), bf16),
        v((512, 1024), bf16),
        v((4, 512, 384), bf16),
        v((4, 512, 384), bf16),
        v((3, 6, 256, 384), bf16),
        v((512, D), bf16),
        v((512, 384), f32),
        v((512, 1024), bf16),
        v((512, 512), bf16),
        v((512, 384), bf16),
        v((4, 512, 128), f32),
        v((2, 512, 256), f32),
        v((2, 512, 256), f32),
        v((2, 512, 256), bf16),
        v((2, 512, 256), bf16),
        v((2, 512, 384), bf16),
        v((2, 4, 8, 128), f32),
        v((512, 1), f32),
        v((8, 384), f32),
        v((4, 2, 96, 1024), bf16),
        v((4, 2, 96, 1024), bf16),
        v((2, 4, 2, 32, D), bf16),
        v((2, 4, 2, 96, 384), bf16),
        v((2, 2, 48, D), bf16),
        v((3, 4, 48, 512), bf16),
        v((3, 4, 48, 512), bf16),
        v((3, 4, 16, D), bf16),
        v((3, 2, 4, 2, 48, 128), bf16),
        v((3, 2, 4, 2, 48, 128), bf16),
        v((3, 2, 2, 16, D), bf16),
        v((3, 4, 48, 128), bf16),
        v((3, 4, 48, 128), bf16),
        v((3, 16, D), bf16),
        v((3, 4, 48, 128), bf16),
        v((3, 4, 48, 128), bf16),
        v((3, 16, D), bf16),
        v((3, 4, 48, 384), bf16),
        v((3, 32, D), bf16),
        v((3, 2, 2, 48, 384), bf16),
        v((3, 2, 2, 16, 384), bf16),
        v((3, 48, 384), bf16),
        v((3, 32, 384), bf16),
        v((3, 48, 384), bf16),
        v((3, 16, 384), bf16),
        pltpu.SemaphoreType.DMA((150,)),
        pltpu.SemaphoreType.DMA((150,)),
        pltpu.SemaphoreType.DMA((16,)),
    ]
    names = [
        ("a1", ANY), ("stats", VM), ("qkv", VM), ("kvr", VM), ("att", VM), ("cos", VM), ("sin", VM),
        ("middle", VM), ("mf", ANY), ("cotf", VM), ("gn", VM), ("wqkv", ANY), ("wo", ANY),
        ("wg", ANY), ("wu", ANY), ("wd", ANY),
    ]
    return pl.pallas_call(
        backward_kernel,
        out_shape=outs,
        in_specs=[VM] + [spec for _, spec in names] + [VM, VM],
        out_specs=[VM] * len(outs),
        scratch_shapes=scratch,
        compiler_params=pltpu.CompilerParams(
            collective_id=1, has_side_effects=True, vmem_limit_bytes=63 * 1024 * 1024
        ),
        name="backward",
    )(tokens, *[k[name] for name, _ in names], perm, permo)


def per_device(
    tokens,
    positions,
    attn_gain,
    qkv_weight,
    output_weight,
    ffn_gain,
    gate_weight,
    up_weight,
    down_weight,
    cotangent,
):
    consts = constants()
    gains = jnp.concatenate([attn_gain[None], ffn_gain[None], jnp.zeros((6, 384), f32)], 0)
    kept = run_forward(
        tokens, positions.reshape(8, 128), gains, qkv_weight, output_weight,
        gate_weight, up_weight, down_weight, cotangent, consts,
    )
    mixed, tgrad, dgain, g_q, g_o, g_g, g_u, g_d = run_backward(tokens, kept, consts)
    dgain = dgain[8] + dgain[9]
    return (
        mixed,
        tgrad,
        dgain[0],
        g_q.reshape(384, 384).astype(f32),
        g_o.reshape(192, 384).astype(f32),
        dgain[1],
        g_g.reshape(384, 512).astype(f32),
        g_u.reshape(384, 512).astype(f32),
        g_d.reshape(512, 384).astype(f32),
    )


def solution(mesh):
    finer = Mesh(mesh.devices.reshape(2, 2, 4, 2, 4), AXES)
    row = ("y", "zh")
    in_specs = (
        P(DP_ROW, "x"),
        P(("zl", "core", "x")),
        P("x"),
        P("x", row),
        P(row, "x"),
        P("x"),
        P("x", row),
        P("x", row),
        P(row, "x"),
        P(DP_ROW, "x"),
    )
    out_specs = (
        P(DP_ROW, "x"),
        P(DP_ROW, "x"),
        P("x"),
        P("x", row),
        P(row, "x"),
        P("x"),
        P("x", row),
        P("x", row),
        P(row, "x"),
    )
    return jax.shard_map(per_device, mesh=finer, in_specs=in_specs, out_specs=out_specs, check_vma=False)
```

```python
import functools
import math

import jax
import jax.numpy as jnp
import numpy as np
from jax import lax
from jax.experimental import pallas as pl
from jax.experimental.pallas import tpu as pltpu
from jax.sharding import Mesh
from jax.sharding import PartitionSpec as P

D = 1536
HD = 96
AXES = ("zl", "core", "y", "zh", "x")
DP_ROW = ("zl", "core", "y", "zh")
bf16 = jnp.bfloat16
f32 = jnp.float32
i32 = jnp.int32
MESH = pl.DeviceIdType.MESH
VM = pl.BlockSpec(memory_space=pltpu.VMEM)
ANY = pl.BlockSpec(memory_space=pl.ANY)

epsilon = 1e-05
rope_base = 100000.0
masked_score = -1e30
score_scale = math.log2(math.e) / math.sqrt(HD)
H0, H1 = pl.ds(0, 256), pl.ds(256, 256)


def dot(a, b):
    return lax.dot_general(a, b, (((1,), (0,)), ((), ())), preferred_element_type=f32)


def dot_t(a, b):
    return lax.dot_general(a, b, (((1,), (1,)), ((), ())), preferred_element_type=f32)


def lanes(index, width):
    return pl.ds(pl.multiple_of(index * width, 128), width)


class Place:
    def __init__(self):
        self.x, self.y = lax.axis_index("x"), lax.axis_index("y")
        self.zl, self.zh, self.core = lax.axis_index("zl"), lax.axis_index("zh"), lax.axis_index("core")
        self.quarter = self.zl * 2 + self.core
        self.ahead, self.behind, self.across = [(self.x + k) % 4 for k in (1, 3, 2)]
        self.right, self.left, self.far = {"x": self.ahead}, {"x": self.behind}, {"x": self.across}
        self.ys = [{"y": (self.y + k) % 4} for k in (1, 3, 2)]
        self.zs = [{"zl": 1 - self.zl}, {"zl": 1 - self.zl, "zh": 1 - self.zh}, {"zh": 1 - self.zh}]
        self.twin = {"core": 1 - self.core}
        self.mirror = {"x": self.y, "y": self.x}
        y, zl, zh = self.y, self.zl, self.zh
        beside, opposite = y + 1 - y % 2 * 2, 3 - y
        self.cube = {
            "ya": ({"y": beside}, (beside, zl, zh)),
            "yb": ({"y": opposite}, (opposite, zl, zh)),
            "za": ({"zl": 1 - zl}, (y, 1 - zl, zh)),
            "zb": ({"zl": 1 - zl, "zh": 1 - zh}, (y, 1 - zl, 1 - zh)),
        }

    def across_link(self, name):
        return self.cube[name]

    def enter(self):
        barrier = pltpu.get_barrier_semaphore()
        peers = [self.right, self.left, self.far, *self.ys, *self.zs, self.twin]
        for peer in peers:
            pl.semaphore_signal(barrier, inc=1, device_id=peer, device_id_type=MESH)

        @pl.when(self.x != self.y)
        def _():
            pl.semaphore_signal(barrier, inc=1, device_id=self.mirror, device_id_type=MESH)
            pl.semaphore_wait(barrier, len(peers) + 1)

        @pl.when(self.x == self.y)
        def _():
            pl.semaphore_wait(barrier, len(peers))


class Links:
    def __init__(self, send, recv, local):
        self.send, self.recv, self.local, self.count, self.local_count = send, recv, local, 0, 0
        self.open = []

    def make(self, src, dst, device):
        i = self.count
        self.count += 1
        return pltpu.make_async_remote_copy(
            src, dst, self.send.at[i], self.recv.at[i], device_id=device, device_id_type=MESH
        )

    def start(self, src, dst, device):
        copy = self.make(src, dst, device)
        copy.start()
        self.open.append(copy)
        return copy

    def spread(self, ref, devices):
        return [self.start(ref, ref, device) for device in devices]

    def keep(self, src, dst):
        copy = pltpu.make_async_copy(src, dst, self.local.at[self.local_count])
        self.local_count += 1
        copy.start()
        return copy

    def settle(self, copies):
        for copy in copies:
            copy.wait_send()
        self.open = [copy for copy in self.open if all(copy is not done for done in copies)]

    def close(self):
        self.settle(list(self.open))


def arrive(copies):
    for copy in copies:
        copy.wait_recv()


class RingGather:
    def __init__(self, links, here, src, buf):
        cols = lanes(here.x, 384)
        self.links, self.here, self.buf = links, here, buf
        self.first = [
            links.start(src(H0), buf.at[H0, cols], here.right),
            links.start(src(H1), buf.at[H1, cols], here.left),
        ]
        self.second = [
            links.start(src(H1), buf.at[H1, cols], here.right),
            links.start(src(H0), buf.at[H0, cols], here.left),
        ]

    def forward(self):
        here, buf = self.here, self.buf
        self.first[0].wait_recv()
        a = buf.at[H0, lanes(here.behind, 384)]
        self.third = [self.links.start(a, a, here.right)]
        self.first[1].wait_recv()
        b = buf.at[H1, lanes(here.ahead, 384)]
        self.third += [self.links.start(b, b, here.left)]

    def finish(self):
        arrive(self.second)
        arrive(self.third)

    def settle(self):
        self.links.settle(self.first + self.second + self.third)


class RingScatter:
    def __init__(self, links, here, part, slots):
        self.links, self.here, self.part, self.slots = links, here, part, slots

    def send_far(self):
        h, p, s = self.here, self.part, self.slots
        self.r0 = self.links.start(p.at[h.across, H0], s.at[0], h.right)
        self.l0 = self.links.start(p.at[h.across, H1], s.at[1], h.left)

    def send_near(self):
        h, p, s = self.here, self.part, self.slots
        self.r1 = self.links.start(p.at[h.ahead, H1], s.at[2], h.right)
        self.l1 = self.links.start(p.at[h.behind, H0], s.at[3], h.left)

    def forward(self):
        h, p, s = self.here, self.part, self.slots
        self.r0.wait_recv()
        p[h.ahead, H0] = (p[h.ahead, H0].astype(f32) + s[0].astype(f32)).astype(bf16)
        self.r2 = self.links.start(p.at[h.ahead, H0], s.at[4], h.right)
        self.l0.wait_recv()
        p[h.behind, H1] = (p[h.behind, H1].astype(f32) + s[1].astype(f32)).astype(bf16)
        self.l2 = self.links.start(p.at[h.behind, H1], s.at[5], h.left)

    def finish(self):
        arrive([self.r1, self.l1, self.r2, self.l2])

    def settle(self):
        self.links.settle([self.r0, self.l0, self.r1, self.l1, self.r2, self.l2])

    def received(self, half):
        s = self.slots
        pair = (4, 3) if half == 0 else (2, 5)
        return s[pair[0]].astype(f32) + s[pair[1]].astype(f32)


ORDERS = (("ya", "yb", "za", "zb"), ("za", "zb", "ya", "yb"), ("yb", "ya", "zb", "za"), ("zb", "za", "yb", "ya"))


def part_of(order):
    y_state = {(): "own", ("ya",): "pair", ("yb",): "cross"}.get(tuple(d for d in order if d[0] == "y"), "all")
    z_state = {(): "own", ("za",): "low", ("zb",): "cross"}.get(tuple(d for d in order if d[0] == "z"), "all")
    return y_state, z_state


def y_cells(state, y):
    return {"own": [(y, 1)], "pair": [(y // 2 * 2, 2)], "cross": [(y, 1), (3 - y, 1)], "all": [(0, 4)]}[state]


def z_cells(state, zl, zh, joined):
    if state == "all" and not joined:
        return [(None, 0), (None, 1)]
    cells = {"own": [(zl, zh)], "low": [(None, zh)], "cross": [(zl, zh), (1 - zl, 1 - zh)], "all": [(None, None)]}
    return cells[state]


def either(index):
    return slice(None) if index is None else index


class UnitColumns:
    def __init__(self, core, start, size):
        self.core, self.start, self.size = core, start, size

    def cells(self, state, y, zl, zh):
        rows = pl.ds(self.start, self.size)
        return [
            (slice(None), either(l), self.core, rows, pl.ds(pl.multiple_of(h * 512 + first * 128, 128), count * 128))
            for l, h in z_cells(state[1], zl, zh, False)
            for first, count in y_cells(state[0], y)
        ]

    def shapes(self, state):
        return [
            (4,) + ((2,) if l is None else ()) + (self.size, count * 128)
            for l, _ in z_cells(state[1], 0, 0, False)
            for _, count in y_cells(state[0], 0)
        ]


class Blocks:
    def __init__(self, core, start, size, width):
        self.core, self.start, self.size, self.width = core, start, size, width

    def cells(self, state, y, zl, zh):
        rows = pl.ds(self.start, self.size)
        pick = lambda first, count: first if count == 1 else (slice(None) if count == 4 else pl.ds(first, count))
        return [
            (either(h), pick(first, count), either(l), self.core, rows)
            for l, h in z_cells(state[1], zl, zh, True)
            for first, count in y_cells(state[0], y)
        ]

    def shapes(self, state):
        return [
            ((2,) if h is None else ()) + ((count,) if count > 1 else ()) + ((2,) if l is None else ()) + (self.size, self.width)
            for l, h in z_cells(state[1], 0, 0, True)
            for _, count in y_cells(state[0], 0)
        ]


class OutputRows:
    def __init__(self, core, start, size, place):
        self.core, self.start, self.size, self.place = core, start, size, place

    def cells(self, state, y, zl, zh):
        rows = pl.ds(self.start, self.size)
        return [
            (either(h), self.place, either(l), self.core, rows, pl.ds(pl.multiple_of(first * 384, 128), count * 384))
            for l, h in z_cells(state[1], zl, zh, True)
            for first, count in y_cells(state[0], y)
        ]

    def shapes(self, state):
        return [
            ((2,) if h is None else ()) + ((2,) if l is None else ()) + (self.size, count * 384)
            for l, h in z_cells(state[1], 0, 0, True)
            for _, count in y_cells(state[0], 0)
        ]


class CubeGather:
    def __init__(self, links, here, ref, layout, order):
        self.links, self.here, self.ref, self.layout, self.order, self.step = links, here, ref, layout, order, 0
        self.launch()

    def launch(self):
        here, ref = self.here, self.ref
        device, _ = here.across_link(self.order[self.step])
        cells = self.layout.cells(part_of(self.order[: self.step]), here.y, here.zl, here.zh)
        self.copies = [self.links.start(ref.at[cell], ref.at[cell], device) for cell in cells]

    def advance(self):
        arrive(self.copies)
        self.step += 1
        if self.step < 4:
            self.launch()


class CubeReduce:
    def __init__(self, links, here, ref, layout, order, slots):
        self.links, self.here, self.ref, self.layout, self.order, self.step = links, here, ref, layout, order, 3
        self.slots = slots
        self.launch()

    def launch(self):
        here, ref = self.here, self.ref
        device, coordinates = here.across_link(self.order[self.step])
        cells = self.layout.cells(part_of(self.order[: self.step]), *coordinates)
        pairs = zip(cells, self.slots[self.step])
        self.copies = [self.links.start(ref.at[cell], slot, device) for cell, slot in pairs]

    def advance(self):
        here, ref = self.here, self.ref
        arrive(self.copies)
        cells = self.layout.cells(part_of(self.order[: self.step]), here.y, here.zl, here.zh)
        for cell, slot in zip(cells, self.slots[self.step]):
            ref[cell] = (ref[cell].astype(f32) + slot[...].astype(f32)).astype(bf16)
        self.step -= 1
        if self.step >= 0:
            self.launch()


def advance(cubes):
    for cube in cubes:
        cube.advance()


def grad_layouts(core, place):
    return [
        ("d", Blocks(core, 0, 16, D), 0),
        ("d", Blocks(core, 16, 16, D), 3),
        ("g", UnitColumns(core, 0, 48), 0),
        ("g", UnitColumns(core, 48, 48), 1),
        ("u", UnitColumns(core, 0, 48), 2),
        ("u", UnitColumns(core, 48, 48), 3),
        ("o", OutputRows(core, 0, 16, place), 1),
        ("o", OutputRows(core, 16, 16, place), 2),
        ("o", OutputRows(core, 32, 16, place), 3),
        ("q", Blocks(core, 0, 32, 384), 0),
        ("q", Blocks(core, 32, 32, 384), 1),
        ("q", Blocks(core, 64, 16, 384), 2),
        ("q", Blocks(core, 80, 16, 384), 3),
    ]


def slot_shapes():
    return [
        [layout.shapes(part_of(ORDERS[order][:step])) for step in range(4)] for _, layout, order in grad_layouts(0, 0)
    ]


def sine_cosine(angle):
    turns = jnp.floor(angle * (1.0 / (2.0 * math.pi)) + 0.5)
    r = angle - turns * 6.28125
    r = r - turns * 0.0019350051879882812
    r = r - turns * 3.0199159819185874e-07
    t = r * 0.5
    t2 = t * t
    s = 1.0 / 6227020800.0
    for c in (-1.0 / 39916800, 1.0 / 362880, -1.0 / 5040, 1.0 / 120, -1.0 / 6, 1.0):
        s = s * t2 + c
    s = s * t
    c_ = 1.0 / 479001600.0
    for c in (-1.0 / 3628800, 1.0 / 40320, -1.0 / 720, 1.0 / 24, -0.5, 1.0):
        c_ = c_ * t2 + c
    return 2.0 * s * c_, 1.0 - 2.0 * s * s


def turn(head, cosine, sine):
    return head * cosine + pltpu.roll(head, 64, 1) * sine


def dot_first(a, b):
    return lax.dot_general(a, b, (((0,), (0,)), ((), ())), preferred_element_type=f32)


def column_to_rows(column, ref):
    for c in range(4):
        block = jnp.broadcast_to(column[c * 128 : c * 128 + 128], (128, 128)).T
        ref[c : c + 1] = block[0:1]


def rows_to_column(rows):
    return jnp.concatenate([jnp.broadcast_to(rows[c : c + 1], (128, 128)).T for c in range(4)], 0)


def layer_kernel(
    tokens, pos, gain_a, gain_f, qkvw, ow, gw, uw, dw, cot, freq, perm, permo,
    mixed, tgrad, dgain, fin_q, fin_o, fin_g, fin_u, fin_d,
    xf, a1, a2, cotf, stats, qkv, kvr, att, cosb, sinb, middle, gn, posb, packed,
    wqkv, wo, wg, wu, wd, hdd, part, partd, slots, wide, dzf, dmid,
    dq, dkv, dkr, dkin, dproj, small, sums, gsum, rc_g, rc_u, rc_d, rc_q, rc_o,
    send, recv, local, *slot_refs,
):
    here = Place()
    links = Links(send, recv, local)
    x, y, zl, zh, core, quarter = here.x, here.y, here.zl, here.zh, here.core, here.quarter
    hid = zh * 4 + y
    other = 1 - core
    own, y_cols = lanes(x, 384), lanes(y, 384)
    a, b, da, db, oa, ob = pl.ds(0, 48), pl.ds(48, 48), pl.ds(0, 16), pl.ds(16, 16), pl.ds(0, 32), pl.ds(32, 16)
    refs = iter(slot_refs)
    layouts = [
        (name, layout, ORDERS[order], [[next(refs) for _ in shapes] for shapes in steps])
        for (name, layout, order), steps in zip(grad_layouts(core, x), slot_shapes())
    ]
    x_peers = (here.right, here.left, here.far)
    here.enter()

    own_qkv, src_qkv = wqkv.at[zh, x, zl, core], qkvw.at[pl.ds(quarter * 96, 96)]
    own_o, src_o = wo.at[zh, y, zl, core, :, own], ow.at[pl.ds(quarter * 48, 48)]
    mirror = [links.make(src_qkv, own_qkv, here.mirror)]
    stay = [pltpu.make_async_copy(src_qkv, own_qkv, local.at[0])]
    links.local_count = 2

    @pl.when(x != y)
    def _():
        for copy in mirror:
            copy.start()

    @pl.when(x == y)
    def _():
        for copy in stay:
            copy.start()

    def hidden_slices(target):
        rows = pl.ds(quarter * 96, 96)
        return [
            (gw.at[rows, lanes(target, 128)], wg.at[x, zl, core, :, lanes(hid, 128)]),
            (uw.at[rows, lanes(target, 128)], wu.at[x, zl, core, :, lanes(hid, 128)]),
            (dw.at[pl.ds(target * 128 + quarter * 32, 32)], wd.at[zh, y, zl, core, :, own]),
        ]

    swaps = []
    for peer, target in ((here.right, here.ahead), (here.left, here.behind), (here.far, here.across)):
        swaps += [links.start(src, dst, peer) for src, dst in hidden_slices(target)]
    swap_kept = [links.keep(src, dst) for src, dst in hidden_slices(x)]
    swaps_o = [links.start(src_o, own_o, peer) for peer in x_peers]
    swap_kept_o = links.keep(src_o, own_o)

    ring_x = RingGather(links, here, lambda half: tokens.at[half], xf)
    kept = [links.keep(tokens, xf.at[:, own])]
    small_sends = []
    for peer in x_peers:
        small_sends.append(links.start(pos, posb.at[x], peer))
        small_sends.append(links.start(gain_a, gn.at[0, :, own], peer))
        small_sends.append(links.start(gain_f, gn.at[1, :, own], peer))
    kept += [links.keep(pos, posb.at[x]), links.keep(gain_a, gn.at[0, :, own]), links.keep(gain_f, gn.at[1, :, own])]

    @pl.when(x != y)
    def _():
        for copy in mirror:
            copy.wait()

    @pl.when(x == y)
    def _():
        for copy in stay:
            copy.wait()

    pieces = ((0, 32), (32, 32), (64, 16), (80, 16))
    cube_q = [
        CubeGather(links, here, wqkv, Blocks(core, start, size, 384), ORDERS[k]) for k, (start, size) in enumerate(pieces)
    ]
    for copy in swap_kept:
        copy.wait()
    arrive(swaps)
    advance(cube_q)
    cube_g = [CubeGather(links, here, wg, UnitColumns(core, 48 * k, 48), ORDERS[k]) for k in range(2)]
    cube_u = [CubeGather(links, here, wu, UnitColumns(core, 48 * k, 48), ORDERS[2 + k]) for k in range(2)]
    cube_d = [CubeGather(links, here, wd, Blocks(core, 16 * k, 16, D), ORDERS[3 * k]) for k in range(2)]
    ring_x.forward()
    advance(cube_q)
    swap_kept_o.wait()
    arrive(swaps_o)
    cube_o = [CubeGather(links, here, wo, Blocks(core, 16 * k, 16, D), ORDERS[1 + k]) for k in range(3)]
    advance(cube_q)
    advance(cube_o)

    for copy in kept:
        copy.wait()
    arrive(small_sends)
    mine = posb[y]
    mine = jnp.where(zh == 0, mine[0:4], mine[4:8]).astype(f32)
    lane = lax.broadcasted_iota(i32, (128, 128), 1)
    for c in range(4):
        column = jnp.broadcast_to(mine[c : c + 1], (128, 128)).T
        sine, cosine = sine_cosine(column * freq[0:1])
        cosb[pl.ds(c * 128, 128)] = cosine
        sinb[pl.ds(c * 128, 128)] = jnp.where(lane < 64, -sine, sine)

    ring_x.finish()
    ring_c = RingGather(links, here, lambda half: cot.at[half], cotf)
    cot_kept = links.keep(cot, cotf.at[:, own])

    def norm_tokens(i, _):
        rows = pl.ds(pl.multiple_of(i * 64, 64), 64)
        value = xf[rows].astype(f32)
        inverse = lax.rsqrt(jnp.sum(value * value, axis=1, keepdims=True) * (1.0 / D) + epsilon)
        a1[rows] = (value * gn[0]).astype(bf16)
        stats[rows] = jnp.broadcast_to(inverse, (64, 128))
        return 0

    lax.fori_loop(0, 8, norm_tokens, 0)

    advance(cube_q)
    core_qkv = links.spread(wqkv.at[:, :, :, core], [here.twin])
    advance(cube_g)
    advance(cube_u)
    advance(cube_o)
    advance(cube_d)

    arrive(core_qkv)
    advance(cube_g)
    advance(cube_u)

    def widen(i, _):
        w = wqkv[i].reshape(D, 384)
        for j in range(3):
            hdd[j, :, lanes(i, 512)] = dot(w[j * 512 : j * 512 + 512], perm[...]).astype(bf16)
        return 0

    lax.fori_loop(0, 2, widen, 0)

    def keys_values(g, _):
        pair = dot(a1[...], hdd[:, :, lanes(g * 2 + 1, 256)].reshape(D, 256))
        inverse = stats[...]
        qkv[:, lanes(g * 4 + 2, 128)] = turn(pair[:, :128] * inverse, cosb[...], sinb[...]).astype(bf16)
        qkv[:, lanes(g * 4 + 3, 128)] = (pair[:, 128:] * inverse).astype(bf16)
        return 0

    lax.fori_loop(0, 2, keys_values, 0)
    over = [links.make(qkv.at[:, pl.ds(g * 512 + 256, 256)], kvr.at[g], here.zs[2]) for g in range(2)]

    @pl.when(zh == 0)
    def _():
        for copy in over:
            copy.start()

    def queries(g, _):
        pair = dot(a1[...], hdd[:, :, lanes(g * 2, 256)].reshape(D, 256))
        inverse = stats[...]
        for h in range(2):
            head = pair[:, h * 128 : h * 128 + 128] * inverse
            qkv[:, lanes(g * 4 + h, 128)] = turn(head, cosb[...], sinb[...]).astype(bf16)
        return 0

    lax.fori_loop(0, 2, queries, 0)
    ring_c.forward()
    advance(cube_o)
    advance(cube_d)
    advance(cube_g)

    def own_scores(i, _):
        g = i // 2
        for qb in range(2):
            rows, keys = pl.ds(qb * 256, 256), pl.ds(0, qb * 256 + 256)
            q = qkv[rows, lanes(g * 4 + i % 2, 128)]
            s = dot_t(q, qkv[keys, lanes(g * 4 + 2, 128)]) * score_scale
            index = lax.broadcasted_iota(i32, s.shape, 0) + qb * 256
            s = jnp.where(lax.broadcasted_iota(i32, s.shape, 1) <= index, s, masked_score)
            m = jnp.max(s, axis=1, keepdims=True)
            e = jnp.exp2(s - m)
            dq[i, rows] = dot(e.astype(bf16), qkv[keys, lanes(g * 4 + 3, 128)])
            dkv[i, rows] = jnp.broadcast_to(m, (256, 128))
            dkr[i, rows] = jnp.broadcast_to(jnp.sum(e, axis=1, keepdims=True), (256, 128))
        return 0

    lax.fori_loop(0, 4, own_scores, 0)
    advance(cube_u)
    advance(cube_o)
    core_o = links.spread(wo.at[:, :, :, core], [here.twin])
    advance(cube_d)

    @pl.when(zh == 1)
    def _():
        for copy in over:
            copy.wait_recv()

        def first_scores(i, _):
            g = i // 2
            for qb in range(2):
                rows = pl.ds(qb * 256, 256)
                q = qkv[rows, lanes(g * 4 + i % 2, 128)]
                s = dot_t(q, kvr[g, :, 0:128]) * score_scale
                old = dkv[i, rows][:, 0:1]
                m = jnp.maximum(old, jnp.max(s, axis=1, keepdims=True))
                e = jnp.exp2(s - m)
                shrink = jnp.exp2(old - m)
                dq[i, rows] = dq[i, rows] * shrink + dot(e.astype(bf16), kvr[g, :, 128:256])
                dkr[i, rows] = dkr[i, rows] * shrink + jnp.sum(e, axis=1, keepdims=True)
                dkv[i, rows] = jnp.broadcast_to(m, (256, 128))
            return 0

        lax.fori_loop(0, 4, first_scores, 0)

    @pl.when(zh == 0)
    def _():
        for copy in over:
            copy.wait_send()

    lane = lax.broadcasted_iota(i32, (512, 128), 1)
    for i in range(4):
        att[:, i * 128 : i * 128 + 128] = (dq[i] / dkr[i]).astype(bf16)
        stats[...] = jnp.where(lane == i, dkv[i] + jnp.log2(dkr[i]), stats[...])

    packed[...] = dot(att[...], permo[...]).astype(bf16)
    ring_a = RingGather(links, here, lambda half: packed.at[half], dzf)
    dzf[:, own] = packed[...]
    advance(cube_g)
    cores = [links.start(wg.at[:, :, core], wg.at[:, :, core], here.twin)]
    ring_a.forward()
    advance(cube_u)
    cores.append(links.start(wu.at[:, :, core], wu.at[:, :, core], here.twin))
    advance(cube_d)
    cores.append(links.start(wd.at[:, :, :, core], wd.at[:, :, :, core], here.twin))
    cot_kept.wait()
    ring_c.finish()
    arrive(core_o)
    ring_a.finish()
    sums[...] = jnp.zeros_like(sums)
    for rows in (H0, H1):
        for c in range(4):
            cols = pl.ds(c * 384, 384)
            value = xf[rows, cols].astype(f32)
            for k in range(4):
                value = value + dot(dzf[rows, k * 384 : k * 384 + 384], wo[:, k, :, :, :, cols].reshape(384, 384))
            a2[rows, cols] = value.astype(bf16)
            sums[rows] = sums[rows] + jnp.sum(value * value, axis=1, keepdims=True)

            @pl.when(x == c)
            def _(rows=rows, value=value):
                middle[rows] = value

    def norm_middle(i, _):
        rows = pl.ds(pl.multiple_of(i * 64, 64), 64)
        inverse = lax.rsqrt(sums[rows] * (1.0 / D) + epsilon)
        a2[rows] = (a2[rows].astype(f32) * inverse * gn[1]).astype(bf16)
        wide[rows] = jnp.broadcast_to(inverse, (64, 128))
        return 0

    lax.fori_loop(0, 8, norm_middle, 0)
    links.close()
    arrive(cores)

    sums[...] = jnp.zeros_like(sums)

    def units(n, _):
        cols = lanes(n, 256)
        w_g = wg[:, :, :, :, cols].reshape(D, 256)
        w_u = wu[:, :, :, :, cols].reshape(D, 256)
        w_d = wd[n // 2, pl.ds((n % 2) * 2, 2)].reshape(256, D)
        for rows in (H0, H1):
            gate = dot(a2[rows], w_g)
            up = dot(a2[rows], w_u)
            dh = dot_t(cotf[rows], w_d)
            sg = 1.0 / (1.0 + jnp.exp(-gate))
            silu = gate * sg
            dg = (dh * up * (sg + silu * (1.0 - sg))).astype(bf16)
            du = (dh * silu).astype(bf16)
            hdd[0, rows, cols] = (silu * up).astype(bf16)
            hdd[1, rows, cols] = dg
            hdd[2, rows, cols] = du
            inner = jnp.sum(dg.astype(f32) * gate + du.astype(f32) * up, axis=1, keepdims=True)
            sums[rows] = sums[rows] + inner
        return 0

    lax.fori_loop(0, 4, units, 0)

    def back_block(block):
        return dot_t(hdd[1], wg[block].reshape(384, 1024)) + dot_t(hdd[2], wu[block].reshape(384, 1024))

    scatter = RingScatter(links, here, part, slots.at[0])
    part[here.across] = back_block(here.across).astype(bf16)
    scatter.send_far()
    part[here.ahead] = back_block(here.ahead).astype(bf16)
    part[here.behind] = back_block(here.behind).astype(bf16)
    scatter.send_near()
    column_to_rows(sums[...], small.at[0, x])
    inner_sums = [links.start(small.at[0, x], small.at[0, x], p) for p in x_peers]
    dmid[...] = back_block(x)
    scatter.forward()

    def down_block(block, _):
        cols = lanes(block, 384)
        partd[block] = dot(hdd[0], wd[:, :, :, :, :, cols].reshape(1024, 384)).astype(bf16)
        return 0

    lax.fori_loop(0, 4, down_block, 0)

    def down_grad(n, _):
        rows = hdd[0, :, lanes(n, 256)].T
        for c in range(3):
            cols = pl.ds(c * 512, 512)
            value = dot(rows, cotf[:, cols]).astype(bf16)
            wd[n // 2, pl.ds((n % 2) * 2, 2), :, :, :, cols] = value.reshape(2, 2, 2, 32, 512)
        return 0

    lax.fori_loop(0, 4, down_grad, 0)
    cores = [links.start(wd.at[:, :, :, other], rc_d, here.twin)]

    def up_grads(block, _):
        rows = a2[:, lanes(block, 384)].T
        for source, target in ((1, wg), (2, wu)):
            for c in range(2):
                cols = pl.ds(c * 512, 512)
                target[block, :, :, :, cols] = dot(rows, hdd[source, :, cols]).astype(bf16).reshape(2, 2, 96, 512)
        return 0

    lax.fori_loop(0, 4, up_grads, 0)
    cores.append(links.start(wg.at[:, :, other], rc_g, here.twin))
    cores.append(links.start(wu.at[:, :, other], rc_u, here.twin))

    buffers = {"d": wd, "g": wg, "u": wu, "o": wo, "q": wqkv}
    reduces = {}

    def start_reduce(name):
        reduces[name] = [
            CubeReduce(links, here, buffers[name], layout, order, slots_)
            for piece, layout, order, slots_ in layouts
            if piece == name
        ]

    def core_sum_down(i, _):
        for k in range(2):
            for j in range(2):
                value = wd[k, i, j, core].astype(f32) + rc_d[k, i, j].astype(f32)
                wd[k, i, j, core] = value.astype(bf16)
        return 0

    arrive(cores[0:1])
    lax.fori_loop(0, 4, core_sum_down, 0)
    start_reduce("d")

    arrive(inner_sums)
    inner = rows_to_column(jnp.sum(small[0], axis=0)[0:4])[:, 0:1]
    scatter.finish()
    gsum[...] = jnp.zeros_like(gsum)
    for half, rows in enumerate((H0, H1)):
        da2 = dmid[rows] + scatter.received(half)
        m, inverse = middle[rows], wide[rows][:, 0:1]
        gsum[1:2] = gsum[1:2] + jnp.sum(da2 * m * inverse, axis=0, keepdims=True)
        factor = inner[half * 256 : half * 256 + 256] * inverse * inverse * (1.0 / D)
        value = cotf[rows, own].astype(f32) + inverse * gn[1, :, own] * da2 - m * factor
        dmid[rows] = value
        dzf[rows, own] = value.astype(bf16)
    ring_z = RingGather(links, here, lambda half: dzf.at[half, own], dzf)
    ring_z.forward()

    for matrix, (name, source) in enumerate((("g", rc_g), ("u", rc_u))):
        arrive(cores[matrix + 1 : matrix + 2])

        def core_sum(i, _, target=buffers[name], source=source):
            for j in range(2):
                target[i, j, core] = (target[i, j, core].astype(f32) + source[i, j].astype(f32)).astype(bf16)
            return 0

        lax.fori_loop(0, 4, core_sum, 0)
        start_reduce(name)

    ring_z.finish()

    scatter_d = RingScatter(links, here, partd, slots.at[1])
    scatter_d.send_far()
    scatter_d.send_near()

    packed[...] = dot_t(dzf[...], wo[:, x].reshape(384, D)).astype(bf16)
    hdd[1, :, 0:512] = dot_t(packed[...], permo[...]).astype(bf16)
    packed[...] = dot(att[...], permo[...]).astype(bf16)
    for c in range(3):
        cols = pl.ds(c * 512, 512)
        value = dot_first(packed[...], dzf[:, cols]).astype(bf16)
        wo[:, x, :, :, :, cols] = value.reshape(2, 2, 2, 48, 512)
    cores = [links.start(wo.at[:, x, :, other], rc_o, here.twin)]

    dq[...] = jnp.zeros_like(dq)
    dkv[...] = jnp.zeros_like(dkv)

    def pair(i, rows, k, v, visible):
        g = i // 2
        head = lanes(i, 128)
        q, grad = qkv[rows, lanes(g * 4 + i % 2, 128)], hdd[1, rows, head]
        delta = jnp.sum(grad.astype(f32) * att[rows, head].astype(f32), axis=1, keepdims=True)
        lane = lax.broadcasted_iota(i32, (256, 128), 1)
        lse = jnp.sum(jnp.where(lane == i, stats[rows], 0.0), axis=1, keepdims=True)
        s = dot_t(q, k) * score_scale
        if visible is not None:
            s = jnp.where(visible(s.shape), s, masked_score)
        p = jnp.exp2(s - lse)
        ds = (p * (dot_t(grad, v) - delta) * (1.0 / math.sqrt(HD))).astype(bf16)
        dq[i, rows] = dq[i, rows] + dot(ds, k)
        return dot_first(ds, q), dot_first(p.astype(bf16), grad)

    give = [links.make(kvr.at[g], dkin.at[g], here.zs[2]) for g in range(2)]

    @pl.when(zh == 1)
    def _():
        dkr[...] = jnp.zeros_like(dkr)

        def first_half(i, _):
            g = i // 2
            for qb in range(2):
                dk, dv = pair(i, pl.ds(qb * 256, 256), kvr[g, :, 0:128], kvr[g, :, 128:256], None)
                dkr[2 * g] = dkr[2 * g] + dk
                dkr[2 * g + 1] = dkr[2 * g + 1] + dv
            return 0

        for g in range(2):
            lax.fori_loop(2 * g, 2 * g + 2, first_half, 0)
            kvr[g, :, 0:128] = dkr[2 * g].astype(bf16)
            kvr[g, :, 128:256] = dkr[2 * g + 1].astype(bf16)
            give[g].start()

    scatter_d.forward()

    def own_keys(i, _):
        g = i // 2
        for qb in range(2):
            keys = pl.ds(0, qb * 256 + 256)

            def visible(shape):
                rows = lax.broadcasted_iota(i32, shape, 0) + qb * 256
                return lax.broadcasted_iota(i32, shape, 1) <= rows

            k, v = qkv[keys, lanes(g * 4 + 2, 128)], qkv[keys, lanes(g * 4 + 3, 128)]
            dk, dv = pair(i, pl.ds(qb * 256, 256), k, v, visible)
            dkv[2 * g, keys] = dkv[2 * g, keys] + dk
            dkv[2 * g + 1, keys] = dkv[2 * g + 1, keys] + dv
        return 0

    lax.fori_loop(0, 4, own_keys, 0)

    @pl.when(zh == 0)
    def _():
        for g in range(2):
            give[g].wait_recv()
            dkv[2 * g] = dkv[2 * g] + dkin[g, :, 0:128].astype(f32)
            dkv[2 * g + 1] = dkv[2 * g + 1] + dkin[g, :, 128:256].astype(f32)

    @pl.when(zh == 1)
    def _():
        for g in range(2):
            give[g].wait_send()

    arrive(cores)
    for g in range(2):
        for j in range(2):
            wo[g, x, j, core] = (wo[g, x, j, core].astype(f32) + rc_o[g, j].astype(f32)).astype(bf16)
    start_reduce("o")

    sums[...] = jnp.zeros_like(sums)
    inverse = stats[:, 4:5]
    for i in range(8):
        cols = pl.ds(i * 128, 128)
        g, place = i // 4, i % 4
        value = dq[2 * g + place] if place < 2 else dkv[2 * g + place - 2]
        sums[...] = sums[...] + jnp.sum(value * qkv[:, cols].astype(f32), axis=1, keepdims=True)
        if place < 3:
            value = turn(value, cosb[...], -sinb[...])
        hdd[0, :, cols] = (value * inverse).astype(bf16)
    column_to_rows(sums[...], small.at[1, x])
    inner_sums = [links.start(small.at[1, x], small.at[1, x], p) for p in x_peers]
    for g in range(2):
        dproj[g] = dot_t(hdd[0, :, g * 512 : g * 512 + 512], perm[...]).astype(bf16)

    def back_input(block):
        return sum(dot_t(dproj[g], wqkv[g, block].reshape(384, 384)) for g in range(2))

    scatter.settle()
    scatter = RingScatter(links, here, part, slots.at[2])
    part[here.across] = back_input(here.across).astype(bf16)
    scatter.send_far()
    part[here.ahead] = back_input(here.ahead).astype(bf16)
    part[here.behind] = back_input(here.behind).astype(bf16)
    scatter.send_near()
    tgrad[...] = back_input(x)

    def qkv_grads(block, _):
        rows = a1[:, lanes(block, 384)].T
        for g in range(2):
            wqkv[g, block] = dot(rows, dproj[g]).astype(bf16).reshape(2, 2, 96, 384)
        return 0

    lax.fori_loop(0, 4, qkv_grads, 0)
    cores.append(links.start(wqkv.at[:, :, :, other], rc_q, here.twin))
    scatter.forward()

    scatter_d.finish()
    for half, rows in enumerate((H0, H1)):
        mixed[rows] = middle[rows] + partd[x, rows].astype(f32) + scatter_d.received(half)

    advance(reduces["d"])
    advance(reduces["g"])
    advance(reduces["u"])

    arrive(cores[1:])
    for g in range(2):

        def core_heads(i, _, g=g):
            for j in range(2):
                value = wqkv[g, i, j, core].astype(f32) + rc_q[g, i, j].astype(f32)
                wqkv[g, i, j, core] = value.astype(bf16)
            return 0

        lax.fori_loop(0, 4, core_heads, 0)
    start_reduce("q")
    advance(reduces["o"])
    advance(reduces["d"])
    advance(reduces["g"])
    advance(reduces["u"])

    arrive(inner_sums)
    inner = rows_to_column(jnp.sum(small[1], axis=0)[0:4])[:, 0:1]
    scatter.finish()
    for half, rows in enumerate((H0, H1)):
        da1 = tgrad[rows] + scatter.received(half)
        source, rinv = xf[rows, own].astype(f32), stats[rows][:, 4:5]
        gsum[0:1] = gsum[0:1] + jnp.sum(da1 * source, axis=0, keepdims=True)
        factor = inner[half * 256 : half * 256 + 256] * rinv * rinv * (1.0 / D)
        tgrad[rows] = dmid[rows] + gn[0, :, own] * da1 - source * factor
    dgain[0] = gsum[...]
    gain_y = [links.start(dgain.at[0], dgain.at[1 + j], here.ys[j]) for j in range(3)]

    advance(reduces["q"])
    for _ in range(2):
        advance(reduces["d"])
        advance(reduces["g"])
        advance(reduces["u"])
    advance(reduces["o"])

    def hidden_blocks(target):
        return [
            (wg.at[target, zl, core, :, lanes(hid, 128)], fin_g.at[zl, core, :, lanes(x, 128)]),
            (wu.at[target, zl, core, :, lanes(hid, 128)], fin_u.at[zl, core, :, lanes(x, 128)]),
            (wd.at[zh, y, zl, core, :, lanes(target, 384)], fin_d.at[x, zl, core]),
        ]

    swaps = []
    for peer, target in ((here.right, here.ahead), (here.left, here.behind), (here.far, here.across)):
        swaps += [links.start(src, dst, peer) for src, dst in hidden_blocks(target)]
    swap_kept = [links.keep(src, dst) for src, dst in hidden_blocks(x)]

    advance(reduces["q"])
    advance(reduces["o"])

    for copy in swap_kept:
        copy.wait()
    arrive(swaps)
    fins = ((fin_g, 0), (fin_u, 0), (fin_d, 1))
    pick = lambda ref, lead, index: ref.at[(slice(None),) * lead + index]
    across_zl = [links.start(v, v, here.zs[0]) for v in (pick(ref, lead, (zl, core)) for ref, lead in fins)]

    arrive(gain_y)
    gsum[...] = dgain[0] + dgain[1] + dgain[2] + dgain[3]
    dgain[4] = gsum[...]
    gain_z = [links.start(dgain.at[4], dgain.at[5 + j], here.zs[j]) for j in range(3)]

    for _ in range(2):
        advance(reduces["q"])
    advance(reduces["o"])
    src_q, src_o = wqkv.at[zh, y, zl, core], wo.at[zh, x, zl, core, :, y_cols]
    dst_q, dst_o = fin_q.at[zl, core], fin_o.at[zl, core]
    mirror = [links.make(src_q, dst_q, here.mirror), links.make(src_o, dst_o, here.mirror)]
    first = links.local_count
    stay = [pltpu.make_async_copy(src_q, dst_q, local.at[first]), pltpu.make_async_copy(src_o, dst_o, local.at[first + 1])]

    @pl.when(x != y)
    def _():
        for copy in mirror:
            copy.start()
        for copy in mirror:
            copy.wait()

    @pl.when(x == y)
    def _():
        for copy in stay:
            copy.start()
        for copy in stay:
            copy.wait()

    head_zl = [links.start(v, v, here.zs[0]) for v in (fin_q.at[zl, core], fin_o.at[zl, core])]
    arrive(across_zl)
    to_core = [links.start(v, v, here.twin) for v in (pick(ref, lead, (slice(None), core)) for ref, lead in fins)]
    arrive(gain_z)
    gsum[...] = dgain[4] + dgain[5] + dgain[6] + dgain[7]
    dgain[8] = gsum[...]
    gain_c = links.start(dgain.at[8], dgain.at[9], here.twin)
    arrive(head_zl)
    head_core = [links.start(v, v, here.twin) for v in (fin_q.at[:, core], fin_o.at[:, core])]
    arrive([gain_c])
    arrive(to_core)
    arrive(head_core)
    links.close()


def run_layer(tokens, pos, gain_a, gain_f, qkvw, ow, gw, uw, dw, cot):
    s = jax.ShapeDtypeStruct
    v = pltpu.VMEM
    outs = [
        s((512, 384), f32),
        s((512, 384), f32),
        s((10, 8, 384), f32),
        s((2, 2, 96, 384), bf16),
        s((2, 2, 48, 384), bf16),
        s((2, 2, 96, 512), bf16),
        s((2, 2, 96, 512), bf16),
        s((4, 2, 2, 32, 384), bf16),
    ]
    scratch = [
        v((512, D), bf16),
        v((512, D), bf16),
        v((512, D), bf16),
        v((512, D), bf16),
        v((512, 128), f32),
        v((512, 1024), bf16),
        v((2, 512, 256), bf16),
        v((512, 512), bf16),
        v((512, 128), f32),
        v((512, 128), f32),
        v((512, 384), f32),
        v((2, 1, D), f32),
        v((4, 8, 128), i32),
        v((512, 384), bf16),
        v((2, 4, 2, 2, 96, 384), bf16),
        v((2, 4, 2, 2, 48, D), bf16),
        v((4, 2, 2, 96, 1024), bf16),
        v((4, 2, 2, 96, 1024), bf16),
        v((2, 4, 2, 2, 32, D), bf16),
        v((3, 512, 1024), bf16),
        v((4, 512, 384), bf16),
        v((4, 512, 384), bf16),
        v((3, 6, 256, 384), bf16),
        v((512, 128), f32),
        v((512, D), bf16),
        v((512, 384), f32),
        v((4, 512, 128), f32),
        v((4, 512, 128), f32),
        v((4, 512, 128), f32),
        v((2, 512, 256), bf16),
        v((2, 512, 384), bf16),
        v((2, 4, 8, 128), f32),
        v((512, 1), f32),
        v((8, 384), f32),
        v((4, 2, 96, 1024), bf16),
        v((4, 2, 96, 1024), bf16),
        v((2, 4, 2, 32, D), bf16),
        v((2, 4, 2, 96, 384), bf16),
        v((2, 2, 48, D), bf16),
        pltpu.SemaphoreType.DMA((270,)),
        pltpu.SemaphoreType.DMA((270,)),
        pltpu.SemaphoreType.DMA((20,)),
    ]
    scratch += [v(shape, bf16) for piece in slot_shapes() for step in piece for shape in step]
    return pl.pallas_call(
        layer_kernel,
        out_shape=outs,
        in_specs=[ANY] * 10 + [VM] * 3,
        out_specs=[VM] * len(outs),
        scratch_shapes=scratch,
        compiler_params=pltpu.CompilerParams(
            collective_id=0, has_side_effects=True, vmem_limit_bytes=63 * 1024 * 1024
        ),
        name="layer",
    )(tokens, pos, gain_a, gain_f, qkvw, ow, gw, uw, dw, cot, *constants())


def constants():
    half = HD // 2
    freq = np.zeros((8, 128), np.float32)
    rates = rope_base ** (-(np.arange(half) * 2.0 / HD))
    freq[:, :half] = rates
    freq[:, 64 : 64 + half] = rates
    perm = np.zeros((384, 512), np.float32)
    permo = np.zeros((512, 384), np.float32)
    for h in range(4):
        for d in range(HD):
            wide = d if (h == 3 or d < half) else d - half + 64
            perm[h * HD + d, h * 128 + wide] = 1
            permo[h * 128 + d, h * HD + d] = 1
    return jnp.asarray(freq), jnp.asarray(perm, bf16), jnp.asarray(permo, bf16)


def per_device(
    tokens,
    positions,
    attn_gain,
    qkv_weight,
    output_weight,
    ffn_gain,
    gate_weight,
    up_weight,
    down_weight,
    cotangent,
):
    mixed, tgrad, dgain, g_q, g_o, g_g, g_u, g_d = run_layer(
        tokens, positions.reshape(8, 128), attn_gain[None], ffn_gain[None], qkv_weight, output_weight,
        gate_weight, up_weight, down_weight, cotangent,
    )
    dgain = dgain[8] + dgain[9]
    return (
        mixed,
        tgrad,
        dgain[0],
        g_q.reshape(384, 384).astype(f32),
        g_o.reshape(192, 384).astype(f32),
        dgain[1],
        g_g.reshape(384, 512).astype(f32),
        g_u.reshape(384, 512).astype(f32),
        g_d.reshape(512, 384).astype(f32),
    )


def solution(mesh):
    finer = Mesh(mesh.devices.reshape(2, 2, 4, 2, 4), AXES)
    row = ("y", "zh")
    in_specs = (
        P(DP_ROW, "x"),
        P(("zl", "core", "x")),
        P("x"),
        P("x", row),
        P(row, "x"),
        P("x"),
        P("x", row),
        P("x", row),
        P(row, "x"),
        P(DP_ROW, "x"),
    )
    out_specs = (
        P(DP_ROW, "x"),
        P(DP_ROW, "x"),
        P("x"),
        P("x", row),
        P(row, "x"),
        P("x"),
        P("x", row),
        P("x", row),
        P(row, "x"),
    )
    return jax.shard_map(per_device, mesh=finer, in_specs=in_specs, out_specs=out_specs, check_vma=False)
```

```python
import functools
import math

import jax
import jax.numpy as jnp
import numpy as np
from jax import lax
from jax.experimental import pallas as pl
from jax.experimental.pallas import tpu as pltpu
from jax.sharding import Mesh
from jax.sharding import PartitionSpec as P

D = 1536
HD = 96
AXES = ("zl", "core", "y", "zh", "x")
DP_ROW = ("zl", "core", "y", "zh")
bf16 = jnp.bfloat16
f32 = jnp.float32
i32 = jnp.int32
MESH = pl.DeviceIdType.MESH
VM = pl.BlockSpec(memory_space=pltpu.VMEM)
ANY = pl.BlockSpec(memory_space=pl.ANY)

epsilon = 1e-05
rope_base = 100000.0
masked_score = -1e30
score_scale = math.log2(math.e) / math.sqrt(HD)
H0, H1 = pl.ds(0, 256), pl.ds(256, 256)


def dot(a, b):
    return lax.dot_general(a, b, (((1,), (0,)), ((), ())), preferred_element_type=f32)


def dot_t(a, b):
    return lax.dot_general(a, b, (((1,), (1,)), ((), ())), preferred_element_type=f32)


def lanes(index, width):
    return pl.ds(pl.multiple_of(index * width, 128), width)


class Place:
    def __init__(self):
        self.x, self.y = lax.axis_index("x"), lax.axis_index("y")
        self.zl, self.zh, self.core = lax.axis_index("zl"), lax.axis_index("zh"), lax.axis_index("core")
        self.quarter = self.zl * 2 + self.core
        self.ahead, self.behind, self.across = [(self.x + k) % 4 for k in (1, 3, 2)]
        self.right, self.left, self.far = {"x": self.ahead}, {"x": self.behind}, {"x": self.across}
        self.ys = [{"y": (self.y + k) % 4} for k in (1, 3, 2)]
        self.zs = [{"zl": 1 - self.zl}, {"zl": 1 - self.zl, "zh": 1 - self.zh}, {"zh": 1 - self.zh}]
        self.twin = {"core": 1 - self.core}
        self.mirror = {"x": self.y, "y": self.x}
        y, zl, zh = self.y, self.zl, self.zh
        beside, opposite = y + 1 - y % 2 * 2, 3 - y
        self.cube = {
            "ya": ({"y": beside}, (beside, zl, zh)),
            "yb": ({"y": opposite}, (opposite, zl, zh)),
            "za": ({"zl": 1 - zl}, (y, 1 - zl, zh)),
            "zb": ({"zl": 1 - zl, "zh": 1 - zh}, (y, 1 - zl, 1 - zh)),
        }

    def across_link(self, name):
        return self.cube[name]

    def enter(self):
        barrier = pltpu.get_barrier_semaphore()
        peers = [self.right, self.left, self.far, *self.ys, *self.zs, self.twin]
        for peer in peers:
            pl.semaphore_signal(barrier, inc=1, device_id=peer, device_id_type=MESH)

        @pl.when(self.x != self.y)
        def _():
            pl.semaphore_signal(barrier, inc=1, device_id=self.mirror, device_id_type=MESH)
            pl.semaphore_wait(barrier, len(peers) + 1)

        @pl.when(self.x == self.y)
        def _():
            pl.semaphore_wait(barrier, len(peers))


class Links:
    def __init__(self, send, recv, local):
        self.send, self.recv, self.local, self.count, self.local_count = send, recv, local, 0, 0
        self.open = []

    def make(self, src, dst, device):
        i = self.count
        self.count += 1
        return pltpu.make_async_remote_copy(
            src, dst, self.send.at[i], self.recv.at[i], device_id=device, device_id_type=MESH
        )

    def start(self, src, dst, device):
        copy = self.make(src, dst, device)
        copy.start()
        self.open.append(copy)
        return copy

    def spread(self, ref, devices):
        return [self.start(ref, ref, device) for device in devices]

    def keep(self, src, dst):
        copy = pltpu.make_async_copy(src, dst, self.local.at[self.local_count])
        self.local_count += 1
        copy.start()
        return copy

    def settle(self, copies):
        for copy in copies:
            copy.wait_send()
        self.open = [copy for copy in self.open if all(copy is not done for done in copies)]

    def close(self):
        self.settle(list(self.open))


def arrive(copies):
    for copy in copies:
        copy.wait_recv()


class RingGather:
    def __init__(self, links, here, src, buf):
        cols = lanes(here.x, 384)
        self.links, self.here, self.buf = links, here, buf
        self.first = [
            links.start(src(H0), buf.at[H0, cols], here.right),
            links.start(src(H1), buf.at[H1, cols], here.left),
        ]
        self.second = [
            links.start(src(H1), buf.at[H1, cols], here.right),
            links.start(src(H0), buf.at[H0, cols], here.left),
        ]

    def forward(self):
        here, buf = self.here, self.buf
        self.first[0].wait_recv()
        a = buf.at[H0, lanes(here.behind, 384)]
        self.third = [self.links.start(a, a, here.right)]
        self.first[1].wait_recv()
        b = buf.at[H1, lanes(here.ahead, 384)]
        self.third += [self.links.start(b, b, here.left)]

    def near(self):
        arrive(self.second)

    def finish(self):
        arrive(self.third)

    def settle(self):
        self.links.settle(self.first + self.second + self.third)


class RingScatter:
    def __init__(self, links, here, part, slots):
        self.links, self.here, self.part, self.slots = links, here, part, slots

    def send_far(self):
        h, p, s = self.here, self.part, self.slots
        self.r0 = self.links.start(p.at[h.across, H0], s.at[0], h.right)
        self.l0 = self.links.start(p.at[h.across, H1], s.at[1], h.left)

    def send_near(self):
        h, p, s = self.here, self.part, self.slots
        self.r1 = self.links.start(p.at[h.ahead, H1], s.at[2], h.right)
        self.l1 = self.links.start(p.at[h.behind, H0], s.at[3], h.left)

    def forward(self):
        h, p, s = self.here, self.part, self.slots
        self.r0.wait_recv()
        p[h.ahead, H0] = (p[h.ahead, H0].astype(f32) + s[0].astype(f32)).astype(bf16)
        self.r2 = self.links.start(p.at[h.ahead, H0], s.at[4], h.right)
        self.l0.wait_recv()
        p[h.behind, H1] = (p[h.behind, H1].astype(f32) + s[1].astype(f32)).astype(bf16)
        self.l2 = self.links.start(p.at[h.behind, H1], s.at[5], h.left)

    def finish(self):
        arrive([self.r1, self.l1, self.r2, self.l2])

    def settle(self):
        self.links.settle([self.r0, self.l0, self.r1, self.l1, self.r2, self.l2])

    def received(self, half):
        s = self.slots
        pair = (4, 3) if half == 0 else (2, 5)
        return s[pair[0]].astype(f32) + s[pair[1]].astype(f32)


ORDERS = (("ya", "yb", "za", "zb"), ("za", "zb", "ya", "yb"), ("yb", "ya", "zb", "za"), ("zb", "za", "yb", "ya"))


def part_of(order):
    y_state = {(): "own", ("ya",): "pair", ("yb",): "cross"}.get(tuple(d for d in order if d[0] == "y"), "all")
    z_state = {(): "own", ("za",): "low", ("zb",): "cross"}.get(tuple(d for d in order if d[0] == "z"), "all")
    return y_state, z_state


def y_cells(state, y):
    return {"own": [(y, 1)], "pair": [(y // 2 * 2, 2)], "cross": [(y, 1), (3 - y, 1)], "all": [(0, 4)]}[state]


def z_cells(state, zl, zh, joined):
    if state == "all" and not joined:
        return [(None, 0), (None, 1)]
    cells = {"own": [(zl, zh)], "low": [(None, zh)], "cross": [(zl, zh), (1 - zl, 1 - zh)], "all": [(None, None)]}
    return cells[state]


def either(index):
    return slice(None) if index is None else index


class UnitColumns:
    def __init__(self, core, start, size):
        self.core, self.start, self.size = core, start, size

    def cells(self, state, y, zl, zh):
        rows = pl.ds(self.start, self.size)
        return [
            (slice(None), either(l), self.core, rows, pl.ds(pl.multiple_of(h * 512 + first * 128, 128), count * 128))
            for l, h in z_cells(state[1], zl, zh, False)
            for first, count in y_cells(state[0], y)
        ]

    def shapes(self, state):
        return [
            (4,) + ((2,) if l is None else ()) + (self.size, count * 128)
            for l, _ in z_cells(state[1], 0, 0, False)
            for _, count in y_cells(state[0], 0)
        ]


class Blocks:
    def __init__(self, core, start, size, width, left=None):
        self.core, self.start, self.size, self.width = core, start, size, width
        self.columns = () if left is None else (pl.ds(left, width),)

    def cells(self, state, y, zl, zh):
        rows = pl.ds(self.start, self.size)
        pick = lambda first, count: first if count == 1 else (slice(None) if count == 4 else pl.ds(first, count))
        return [
            (either(h), pick(first, count), either(l), self.core, rows, *self.columns)
            for l, h in z_cells(state[1], zl, zh, True)
            for first, count in y_cells(state[0], y)
        ]

    def shapes(self, state):
        return [
            ((2,) if h is None else ()) + ((count,) if count > 1 else ()) + ((2,) if l is None else ()) + (self.size, self.width)
            for l, h in z_cells(state[1], 0, 0, True)
            for _, count in y_cells(state[0], 0)
        ]


class OutputRows:
    def __init__(self, core, start, size, place):
        self.core, self.start, self.size, self.place = core, start, size, place

    def cells(self, state, y, zl, zh):
        rows = pl.ds(self.start, self.size)
        return [
            (either(h), self.place, either(l), self.core, rows, pl.ds(pl.multiple_of(first * 384, 128), count * 384))
            for l, h in z_cells(state[1], zl, zh, True)
            for first, count in y_cells(state[0], y)
        ]

    def shapes(self, state):
        return [
            ((2,) if h is None else ()) + ((2,) if l is None else ()) + (self.size, count * 384)
            for l, h in z_cells(state[1], 0, 0, True)
            for _, count in y_cells(state[0], 0)
        ]


class CubeGather:
    def __init__(self, links, here, ref, layout, order):
        self.links, self.here, self.ref, self.layout, self.order, self.step = links, here, ref, layout, order, 0
        self.launch()

    def launch(self):
        here, ref = self.here, self.ref
        device, _ = here.across_link(self.order[self.step])
        cells = self.layout.cells(part_of(self.order[: self.step]), here.y, here.zl, here.zh)
        self.copies = [self.links.start(ref.at[cell], ref.at[cell], device) for cell in cells]

    def advance(self):
        arrive(self.copies)
        self.step += 1
        if self.step < 4:
            self.launch()


class CubeReduce:
    def __init__(self, links, here, ref, layout, order, slots):
        self.links, self.here, self.ref, self.layout, self.order, self.step = links, here, ref, layout, order, 3
        self.slots = slots
        self.launch()

    def launch(self):
        here, ref = self.here, self.ref
        device, coordinates = here.across_link(self.order[self.step])
        cells = self.layout.cells(part_of(self.order[: self.step]), *coordinates)
        pairs = zip(cells, self.slots[self.step])
        self.copies = [self.links.start(ref.at[cell], slot, device) for cell, slot in pairs]

    def advance(self):
        here, ref = self.here, self.ref
        arrive(self.copies)
        cells = self.layout.cells(part_of(self.order[: self.step]), here.y, here.zl, here.zh)
        for cell, slot in zip(cells, self.slots[self.step]):
            ref[cell] = (ref[cell].astype(f32) + slot[...].astype(f32)).astype(bf16)
        self.step -= 1
        if self.step >= 0:
            self.launch()


def advance(cubes):
    for cube in cubes:
        cube.advance()


def grad_layouts(core, place):
    return [
        ("d", Blocks(core, 0, 16, 768, 0), 0),
        ("d", Blocks(core, 0, 16, 768, 768), 1),
        ("d", Blocks(core, 16, 16, 768, 0), 2),
        ("d", Blocks(core, 16, 16, 768, 768), 3),
        ("g", UnitColumns(core, 0, 48), 0),
        ("g", UnitColumns(core, 48, 48), 1),
        ("u", UnitColumns(core, 0, 48), 2),
        ("u", UnitColumns(core, 48, 48), 3),
        ("o", OutputRows(core, 0, 16, place), 1),
        ("o", OutputRows(core, 16, 16, place), 2),
        ("o", OutputRows(core, 32, 16, place), 3),
        ("q", Blocks(core, 0, 32, 384), 0),
        ("q", Blocks(core, 32, 32, 384), 1),
        ("q", Blocks(core, 64, 16, 384), 2),
        ("q", Blocks(core, 80, 16, 384), 3),
    ]


def slot_shapes():
    return [
        [layout.shapes(part_of(ORDERS[order][:step])) for step in range(4)] for _, layout, order in grad_layouts(0, 0)
    ]


def sine_cosine(angle):
    turns = jnp.floor(angle * (1.0 / (2.0 * math.pi)) + 0.5)
    r = angle - turns * 6.28125
    r = r - turns * 0.0019350051879882812
    r = r - turns * 3.0199159819185874e-07
    t = r * 0.5
    t2 = t * t
    s = 1.0 / 6227020800.0
    for c in (-1.0 / 39916800, 1.0 / 362880, -1.0 / 5040, 1.0 / 120, -1.0 / 6, 1.0):
        s = s * t2 + c
    s = s * t
    c_ = 1.0 / 479001600.0
    for c in (-1.0 / 3628800, 1.0 / 40320, -1.0 / 720, 1.0 / 24, -0.5, 1.0):
        c_ = c_ * t2 + c
    return 2.0 * s * c_, 1.0 - 2.0 * s * s


def causal(scores):
    last = scores[:, -256:]
    seen = lax.broadcasted_iota(i32, (256, 256), 1) <= lax.broadcasted_iota(i32, (256, 256), 0)
    last = jnp.where(seen, last, masked_score)
    return last if scores.shape[1] == 256 else jnp.concatenate([scores[:, :-256], last], axis=1)


def turn(head, cosine, sine):
    return head * cosine + pltpu.roll(head, 64, 1) * sine


def dot_first(a, b):
    return lax.dot_general(a, b, (((0,), (0,)), ((), ())), preferred_element_type=f32)


def column_to_rows(column, ref):
    for c in range(4):
        block = jnp.broadcast_to(column[c * 128 : c * 128 + 128], (128, 128)).T
        ref[c : c + 1] = block[0:1]


def rows_to_column(rows):
    return jnp.concatenate([jnp.broadcast_to(rows[c : c + 1], (128, 128)).T for c in range(4)], 0)


def layer_kernel(
    tokens, pos, gain_a, gain_f, qkvw, ow, gw, uw, dw, cot, freq, perm, permo,
    mixed, tgrad, dgain, fin_q, fin_o, fin_g, fin_u, fin_d,
    xf, a1, a2, cotf, stats, qkv, kvr, att, cosb, sinb, middle, gn, posb, packed,
    wqkv, wo, wg, wu, wd, hdd, part, partd, slots, wide, dzf, dmid,
    dq, dkv, dkr, dkin, dproj, small, sums, gsum, rc_g, rc_u, rc_d, rc_q, rc_o,
    send, recv, local, *slot_refs,
):
    here = Place()
    links = Links(send, recv, local)
    x, y, zl, zh, core, quarter = here.x, here.y, here.zl, here.zh, here.core, here.quarter
    hid = zh * 4 + y
    other = 1 - core
    own, y_cols = lanes(x, 384), lanes(y, 384)
    a, b, da, db, oa, ob = pl.ds(0, 48), pl.ds(48, 48), pl.ds(0, 16), pl.ds(16, 16), pl.ds(0, 32), pl.ds(32, 16)
    refs = iter(slot_refs)
    layouts = [
        (name, layout, ORDERS[order], [[next(refs) for _ in shapes] for shapes in steps])
        for (name, layout, order), steps in zip(grad_layouts(core, x), slot_shapes())
    ]
    x_peers = (here.right, here.left, here.far)
    here.enter()

    own_qkv, src_qkv = wqkv.at[zh, x, zl, core], qkvw.at[pl.ds(quarter * 96, 96)]
    own_o, src_o = wo.at[zh, y, zl, core, :, own], ow.at[pl.ds(quarter * 48, 48)]
    mirror = [links.make(src_qkv, own_qkv, here.mirror)]
    stay = [pltpu.make_async_copy(src_qkv, own_qkv, local.at[0])]
    links.local_count = 2

    @pl.when(x != y)
    def _():
        for copy in mirror:
            copy.start()

    @pl.when(x == y)
    def _():
        for copy in stay:
            copy.start()

    @pl.when(x != y)
    def _():
        for copy in mirror:
            copy.wait()

    @pl.when(x == y)
    def _():
        for copy in stay:
            copy.wait()

    pieces = ((0, 32), (32, 32), (64, 16), (80, 16))
    cube_q = [
        CubeGather(links, here, wqkv, Blocks(core, start, size, 384), ORDERS[k]) for k, (start, size) in enumerate(pieces)
    ]
    def hidden_slices(target):
        rows = pl.ds(quarter * 96, 96)
        return [
            (gw.at[rows, lanes(target, 128)], wg.at[x, zl, core, :, lanes(hid, 128)]),
            (uw.at[rows, lanes(target, 128)], wu.at[x, zl, core, :, lanes(hid, 128)]),
            (dw.at[pl.ds(target * 128 + quarter * 32, 32)], wd.at[zh, y, zl, core, :, own]),
        ]

    swaps = []
    for peer, target in ((here.right, here.ahead), (here.left, here.behind), (here.far, here.across)):
        swaps += [links.start(src, dst, peer) for src, dst in hidden_slices(target)]
    swap_kept = [links.keep(src, dst) for src, dst in hidden_slices(x)]
    swaps_o = [links.start(src_o, own_o, peer) for peer in x_peers]
    swap_kept_o = links.keep(src_o, own_o)

    ring_x = RingGather(links, here, lambda half: tokens.at[half], xf)
    kept = [links.keep(tokens, xf.at[:, own])]
    small_sends = []
    for peer in x_peers:
        small_sends.append(links.start(pos, posb.at[x], peer))
        small_sends.append(links.start(gain_a, gn.at[0, :, own], peer))
        small_sends.append(links.start(gain_f, gn.at[1, :, own], peer))
    kept += [links.keep(pos, posb.at[x]), links.keep(gain_a, gn.at[0, :, own]), links.keep(gain_f, gn.at[1, :, own])]

    advance(cube_q)
    for copy in swap_kept:
        copy.wait()
    arrive(swaps)
    cube_g = [CubeGather(links, here, wg, UnitColumns(core, 48 * k, 48), ORDERS[k]) for k in range(2)]
    cube_u = [CubeGather(links, here, wu, UnitColumns(core, 48 * k, 48), ORDERS[2 + k]) for k in range(2)]
    cube_d = [
        CubeGather(links, here, wd, Blocks(core, 16 * (k // 2), 16, 768, 768 * (k % 2)), ORDERS[k]) for k in range(4)
    ]
    ring_x.forward()
    advance(cube_q)
    swap_kept_o.wait()
    arrive(swaps_o)
    cube_o = [CubeGather(links, here, wo, Blocks(core, 16 * k, 16, D), ORDERS[1 + k]) for k in range(3)]
    advance(cube_g)
    advance(cube_u)
    advance(cube_d)
    advance(cube_q)
    advance(cube_o)

    for copy in kept:
        copy.wait()
    arrive(small_sends)
    mine = posb[y]
    mine = jnp.where(zh == 0, mine[0:4], mine[4:8]).astype(f32)
    lane = lax.broadcasted_iota(i32, (128, 128), 1)
    for c in range(4):
        column = jnp.broadcast_to(mine[c : c + 1], (128, 128)).T
        sine, cosine = sine_cosine(column * freq[0:1])
        cosb[pl.ds(c * 128, 128)] = cosine
        sinb[pl.ds(c * 128, 128)] = jnp.where(lane < 64, -sine, sine)

    ring_x.near()
    ring_x.finish()
    ring_c = RingGather(links, here, lambda half: cot.at[half], cotf)
    cot_kept = links.keep(cot, cotf.at[:, own])

    def norm_tokens(i, _):
        rows = pl.ds(pl.multiple_of(i * 64, 64), 64)
        value = xf[rows].astype(f32)
        inverse = lax.rsqrt(jnp.sum(value * value, axis=1, keepdims=True) * (1.0 / D) + epsilon)
        a1[rows] = (value * gn[0]).astype(bf16)
        stats[rows] = jnp.broadcast_to(inverse, (64, 128))
        return 0

    lax.fori_loop(0, 8, norm_tokens, 0)

    advance(cube_q)
    core_qkv = links.spread(wqkv.at[:, :, :, core], [here.twin])
    advance(cube_g)
    advance(cube_u)
    advance(cube_d)
    advance(cube_o)

    arrive(core_qkv)

    def widen(i, _):
        w = wqkv[i].reshape(D, 384)
        for j in range(3):
            hdd[j, :, lanes(i, 512)] = dot(w[j * 512 : j * 512 + 512], perm[...]).astype(bf16)
        return 0

    lax.fori_loop(0, 2, widen, 0)

    def keys_values(g, _):
        pair = dot(a1[...], hdd[:, :, lanes(g * 2 + 1, 256)].reshape(D, 256))
        inverse = stats[...]
        qkv[:, lanes(g * 4 + 2, 128)] = turn(pair[:, :128] * inverse, cosb[...], sinb[...]).astype(bf16)
        qkv[:, lanes(g * 4 + 3, 128)] = (pair[:, 128:] * inverse).astype(bf16)
        return 0

    lax.fori_loop(0, 2, keys_values, 0)
    over = [links.make(qkv.at[:, pl.ds(g * 512 + 256, 256)], kvr.at[g], here.zs[2]) for g in range(2)]

    @pl.when(zh == 0)
    def _():
        for copy in over:
            copy.start()

    advance(cube_g)
    advance(cube_u)
    advance(cube_d)
    advance(cube_o)

    def queries(g, _):
        pair = dot(a1[...], hdd[:, :, lanes(g * 2, 256)].reshape(D, 256))
        inverse = stats[...]
        for h in range(2):
            head = pair[:, h * 128 : h * 128 + 128] * inverse
            qkv[:, lanes(g * 4 + h, 128)] = (turn(head, cosb[...], sinb[...]) * score_scale).astype(bf16)
        return 0

    lax.fori_loop(0, 2, queries, 0)
    ring_c.forward()

    def own_scores(i, _):
        g = i // 2
        for qb in range(2):
            rows, keys = pl.ds(qb * 256, 256), pl.ds(0, qb * 256 + 256)
            q = qkv[rows, lanes(g * 4 + i % 2, 128)]
            s = causal(dot_t(q, qkv[keys, lanes(g * 4 + 2, 128)]))
            m = jnp.max(s, axis=1, keepdims=True)
            e = jnp.exp2(s - m)
            dq[i, rows] = dot(e.astype(bf16), qkv[keys, lanes(g * 4 + 3, 128)])
            dkv[i, rows] = jnp.broadcast_to(m, (256, 128))
            dkr[i, rows] = jnp.broadcast_to(jnp.sum(e, axis=1, keepdims=True), (256, 128))
        return 0

    lax.fori_loop(0, 4, own_scores, 0)

    @pl.when(zh == 1)
    def _():
        for copy in over:
            copy.wait_recv()

        def first_scores(i, _):
            g = i // 2
            for qb in range(2):
                rows = pl.ds(qb * 256, 256)
                q = qkv[rows, lanes(g * 4 + i % 2, 128)]
                s = dot_t(q, kvr[g, :, 0:128])
                old = dkv[i, rows][:, 0:1]
                m = jnp.maximum(old, jnp.max(s, axis=1, keepdims=True))
                e = jnp.exp2(s - m)
                shrink = jnp.exp2(old - m)
                dq[i, rows] = dq[i, rows] * shrink + dot(e.astype(bf16), kvr[g, :, 128:256])
                dkr[i, rows] = dkr[i, rows] * shrink + jnp.sum(e, axis=1, keepdims=True)
                dkv[i, rows] = jnp.broadcast_to(m, (256, 128))
            return 0

        lax.fori_loop(0, 4, first_scores, 0)

    @pl.when(zh == 0)
    def _():
        for copy in over:
            copy.wait_send()

    advance(cube_o)
    core_o = links.spread(wo.at[:, :, :, core], [here.twin])
    lane = lax.broadcasted_iota(i32, (512, 128), 1)
    for i in range(4):
        att[:, i * 128 : i * 128 + 128] = (dq[i] / dkr[i]).astype(bf16)
        stats[...] = jnp.where(lane == i, dkv[i] + jnp.log2(dkr[i]), stats[...])

    packed[...] = dot(att[...], permo[...]).astype(bf16)
    ring_a = RingGather(links, here, lambda half: packed.at[half], dzf)
    dzf[:, own] = packed[...]
    thirds = (dq, dkv, dkr)

    def output_part(block, c):
        return dot(dzf[:, lanes(block, 384)], wo[:, block, :, :, :, lanes(c, 384)].reshape(384, 384))

    def output_first(c, _):
        value = xf[:, lanes(c, 384)].astype(f32) + output_part(x, c)
        for k, ref in enumerate(thirds):
            ref[c] = value[:, k * 128 : k * 128 + 128]
        return 0

    def output_near(c, _):
        value = output_part(here.ahead, c) + output_part(here.behind, c)
        for k, ref in enumerate(thirds):
            ref[c] = ref[c] + value[:, k * 128 : k * 128 + 128]
        return 0

    def output_last(c, _):
        value = output_part(here.across, c)
        for k, ref in enumerate(thirds):
            m = ref[c] + value[:, k * 128 : k * 128 + 128]
            ref[c] = m
            a2[:, lanes(c * 3 + k, 128)] = (m * gn[1, :, lanes(c * 3 + k, 128)]).astype(bf16)
            sums[...] = sums[...] + jnp.sum(m * m, axis=1, keepdims=True)
        return 0

    arrive(core_o)
    lax.fori_loop(0, 4, output_first, 0)
    ring_a.forward()
    advance(cube_g)
    cores = [links.start(wg.at[:, :, core], wg.at[:, :, core], here.twin)]
    advance(cube_u)
    cores.append(links.start(wu.at[:, :, core], wu.at[:, :, core], here.twin))
    advance(cube_d)
    cores.append(links.start(wd.at[:, :, :, core], wd.at[:, :, :, core], here.twin))
    ring_a.near()
    lax.fori_loop(0, 4, output_near, 0)
    cot_kept.wait()
    ring_c.near()
    ring_c.finish()
    sums[...] = jnp.zeros_like(sums)
    ring_a.finish()
    lax.fori_loop(0, 4, output_last, 0)
    wide[...] = jnp.broadcast_to(lax.rsqrt(sums[...] * (1.0 / D) + epsilon), (512, 128))
    for k, ref in enumerate(thirds):
        middle[:, k * 128 : k * 128 + 128] = ref[x]
    links.close()
    arrive(cores)

    sums[...] = jnp.zeros_like(sums)

    def units(n, _):
        cols = lanes(n, 256)
        w_g = wg[:, :, :, :, cols].reshape(D, 256)
        w_u = wu[:, :, :, :, cols].reshape(D, 256)
        w_d = wd[n // 2, pl.ds((n % 2) * 2, 2)].reshape(256, D)
        for rows in (H0, H1):
            inverse = wide[rows][:, 0:1]
            gate = dot(a2[rows], w_g) * inverse
            up = dot(a2[rows], w_u) * inverse
            dh = dot_t(cotf[rows], w_d)
            sg = 1.0 / (1.0 + jnp.exp(-gate))
            silu = gate * sg
            dg = dh * up * (sg + silu * (1.0 - sg))
            du = dh * silu
            hdd[0, rows, cols] = (silu * up).astype(bf16)
            hdd[1, rows, cols] = (dg * inverse).astype(bf16)
            hdd[2, rows, cols] = (du * inverse).astype(bf16)
            inner = jnp.sum(dg * gate + du * up, axis=1, keepdims=True)
            sums[rows] = sums[rows] + inner
        return 0

    lax.fori_loop(0, 4, units, 0)

    def back_block(block):
        return dot_t(hdd[1], wg[block].reshape(384, 1024)) + dot_t(hdd[2], wu[block].reshape(384, 1024))

    scatter = RingScatter(links, here, part, slots.at[0])
    part[here.across] = back_block(here.across).astype(bf16)
    scatter.send_far()
    part[here.ahead] = back_block(here.ahead).astype(bf16)
    part[here.behind] = back_block(here.behind).astype(bf16)
    scatter.send_near()
    column_to_rows(sums[...], small.at[0, x])
    inner_sums = [links.start(small.at[0, x], small.at[0, x], p) for p in x_peers]
    dmid[...] = back_block(x)
    scatter.forward()

    def down_block(block, _):
        cols = lanes(block, 384)
        partd[block] = dot(hdd[0], wd[:, :, :, :, :, cols].reshape(1024, 384)).astype(bf16)
        return 0

    lax.fori_loop(0, 4, down_block, 0)

    def down_grad(n, _):
        rows = hdd[0, :, lanes(n, 256)].T
        for c in range(3):
            cols = pl.ds(c * 512, 512)
            value = dot(rows, cotf[:, cols]).astype(bf16)
            wd[n // 2, pl.ds((n % 2) * 2, 2), :, :, :, cols] = value.reshape(2, 2, 2, 32, 512)
        return 0

    lax.fori_loop(0, 4, down_grad, 0)
    cores = [links.start(wd.at[:, :, :, other], rc_d, here.twin)]

    def up_grads(block, _):
        rows = a2[:, lanes(block, 384)].T
        for source, target in ((1, wg), (2, wu)):
            for c in range(2):
                cols = pl.ds(c * 512, 512)
                target[block, :, :, :, cols] = dot(rows, hdd[source, :, cols]).astype(bf16).reshape(2, 2, 96, 512)
        return 0

    lax.fori_loop(0, 4, up_grads, 0)
    cores.append(links.start(wg.at[:, :, other], rc_g, here.twin))
    cores.append(links.start(wu.at[:, :, other], rc_u, here.twin))

    buffers = {"d": wd, "g": wg, "u": wu, "o": wo, "q": wqkv}
    reduces = {}

    def start_reduce(name):
        reduces[name] = [
            CubeReduce(links, here, buffers[name], layout, order, slots_)
            for piece, layout, order, slots_ in layouts
            if piece == name
        ]

    def core_sum_down(i, _):
        for k in range(2):
            for j in range(2):
                value = wd[k, i, j, core].astype(f32) + rc_d[k, i, j].astype(f32)
                wd[k, i, j, core] = value.astype(bf16)
        return 0

    arrive(cores[0:1])
    lax.fori_loop(0, 4, core_sum_down, 0)
    start_reduce("d")

    arrive(inner_sums)
    inner = rows_to_column(jnp.sum(small[0], axis=0)[0:4])[:, 0:1]
    scatter.finish()
    gsum[...] = jnp.zeros_like(gsum)
    for half, rows in enumerate((H0, H1)):
        da2 = dmid[rows] + scatter.received(half)
        m, inverse = middle[rows], wide[rows][:, 0:1]
        gsum[1:2] = gsum[1:2] + jnp.sum(da2 * m, axis=0, keepdims=True)
        factor = inner[half * 256 : half * 256 + 256] * inverse * inverse * (1.0 / D)
        value = cotf[rows, own].astype(f32) + gn[1, :, own] * da2 - m * factor
        dmid[rows] = value
        dzf[rows, own] = value.astype(bf16)
    ring_z = RingGather(links, here, lambda half: dzf.at[half, own], dzf)
    ring_z.forward()

    for matrix, (name, source) in enumerate((("g", rc_g), ("u", rc_u))):
        arrive(cores[matrix + 1 : matrix + 2])

        def core_sum(i, _, target=buffers[name], source=source):
            for j in range(2):
                target[i, j, core] = (target[i, j, core].astype(f32) + source[i, j].astype(f32)).astype(bf16)
            return 0

        lax.fori_loop(0, 4, core_sum, 0)
        start_reduce(name)

    ring_z.near()
    ring_z.finish()

    scatter_d = RingScatter(links, here, partd, slots.at[1])
    scatter_d.send_far()
    scatter_d.send_near()

    packed[...] = dot_t(dzf[...], wo[:, x].reshape(384, D)).astype(bf16)
    hdd[1, :, 0:512] = dot_t(packed[...], permo[...]).astype(bf16)
    packed[...] = dot(att[...], permo[...]).astype(bf16)
    for c in range(3):
        cols = pl.ds(c * 512, 512)
        value = dot_first(packed[...], dzf[:, cols]).astype(bf16)
        wo[:, x, :, :, :, cols] = value.reshape(2, 2, 2, 48, 512)
    cores = [links.start(wo.at[:, x, :, other], rc_o, here.twin)]

    dq[...] = jnp.zeros_like(dq)
    dkv[...] = jnp.zeros_like(dkv)

    def pair(i, rows, k, v, masked):
        g = i // 2
        head = lanes(i, 128)
        q, grad = qkv[rows, lanes(g * 4 + i % 2, 128)], hdd[1, rows, head]
        delta = jnp.sum(grad.astype(f32) * att[rows, head].astype(f32), axis=1, keepdims=True)
        lane = lax.broadcasted_iota(i32, (256, 128), 1)
        lse = jnp.sum(jnp.where(lane == i, stats[rows], 0.0), axis=1, keepdims=True)
        s = dot_t(q, k)
        if masked:
            s = causal(s)
        p = jnp.exp2(s - lse)
        ds = (p * (dot_t(grad, v) - delta)).astype(bf16)
        dq[i, rows] = dq[i, rows] + dot(ds, k)
        return dot_first(ds, q), dot_first(p.astype(bf16), grad)

    give = [links.make(kvr.at[g], dkin.at[g], here.zs[2]) for g in range(2)]

    @pl.when(zh == 1)
    def _():
        dkr[...] = jnp.zeros_like(dkr)

        def first_half(i, _):
            g = i // 2
            for qb in range(2):
                dk, dv = pair(i, pl.ds(qb * 256, 256), kvr[g, :, 0:128], kvr[g, :, 128:256], False)
                dkr[2 * g] = dkr[2 * g] + dk
                dkr[2 * g + 1] = dkr[2 * g + 1] + dv
            return 0

        for g in range(2):
            lax.fori_loop(2 * g, 2 * g + 2, first_half, 0)
            kvr[g, :, 0:128] = dkr[2 * g].astype(bf16)
            kvr[g, :, 128:256] = dkr[2 * g + 1].astype(bf16)
            give[g].start()

    scatter_d.forward()

    def own_keys(i, _):
        g = i // 2
        for qb in range(2):
            keys = pl.ds(0, qb * 256 + 256)
            k, v = qkv[keys, lanes(g * 4 + 2, 128)], qkv[keys, lanes(g * 4 + 3, 128)]
            dk, dv = pair(i, pl.ds(qb * 256, 256), k, v, True)
            dkv[2 * g, keys] = dkv[2 * g, keys] + dk
            dkv[2 * g + 1, keys] = dkv[2 * g + 1, keys] + dv
        return 0

    lax.fori_loop(0, 4, own_keys, 0)

    @pl.when(zh == 0)
    def _():
        for g in range(2):
            give[g].wait_recv()
            dkv[2 * g] = dkv[2 * g] + dkin[g, :, 0:128].astype(f32)
            dkv[2 * g + 1] = dkv[2 * g + 1] + dkin[g, :, 128:256].astype(f32)

    @pl.when(zh == 1)
    def _():
        for g in range(2):
            give[g].wait_send()

    for name in "dgu":
        advance(reduces[name])
    arrive(cores)
    for g in range(2):
        for j in range(2):
            wo[g, x, j, core] = (wo[g, x, j, core].astype(f32) + rc_o[g, j].astype(f32)).astype(bf16)
    start_reduce("o")

    sums[...] = jnp.zeros_like(sums)
    inverse = stats[:, 4:5]
    for i in range(8):
        cols = pl.ds(i * 128, 128)
        g, place = i // 4, i % 4
        value = dq[2 * g + place] if place < 2 else dkv[2 * g + place - 2]
        if place == 2:
            value = value * math.log(2.0)
        inside = jnp.sum(value * qkv[:, cols].astype(f32), axis=1, keepdims=True)
        if place < 2:
            inside = inside * math.log(2.0)
            value = value * (1.0 / math.sqrt(HD))
        sums[...] = sums[...] + inside
        if place < 3:
            value = turn(value, cosb[...], -sinb[...])
        hdd[0, :, cols] = (value * inverse).astype(bf16)
    column_to_rows(sums[...], small.at[1, x])
    inner_sums = [links.start(small.at[1, x], small.at[1, x], p) for p in x_peers]
    for g in range(2):
        dproj[g] = dot_t(hdd[0, :, g * 512 : g * 512 + 512], perm[...]).astype(bf16)

    def back_input(block):
        return sum(dot_t(dproj[g], wqkv[g, block].reshape(384, 384)) for g in range(2))

    scatter.settle()
    scatter = RingScatter(links, here, part, slots.at[2])
    part[here.across] = back_input(here.across).astype(bf16)
    scatter.send_far()
    part[here.ahead] = back_input(here.ahead).astype(bf16)
    part[here.behind] = back_input(here.behind).astype(bf16)
    scatter.send_near()
    tgrad[...] = back_input(x)

    def qkv_grads(block, _):
        rows = a1[:, lanes(block, 384)].T
        for g in range(2):
            wqkv[g, block] = dot(rows, dproj[g]).astype(bf16).reshape(2, 2, 96, 384)
        return 0

    lax.fori_loop(0, 4, qkv_grads, 0)
    cores.append(links.start(wqkv.at[:, :, :, other], rc_q, here.twin))
    scatter.forward()

    for name in "dgu":
        advance(reduces[name])

    scatter_d.finish()
    for half, rows in enumerate((H0, H1)):
        mixed[rows] = middle[rows] + partd[x, rows].astype(f32) + scatter_d.received(half)

    arrive(cores[1:])
    for g in range(2):

        def core_heads(i, _, g=g):
            for j in range(2):
                value = wqkv[g, i, j, core].astype(f32) + rc_q[g, i, j].astype(f32)
                wqkv[g, i, j, core] = value.astype(bf16)
            return 0

        lax.fori_loop(0, 4, core_heads, 0)
    start_reduce("q")
    advance(reduces["o"])
    for name in "dgu":
        advance(reduces[name])

    arrive(inner_sums)
    inner = rows_to_column(jnp.sum(small[1], axis=0)[0:4])[:, 0:1]
    scatter.finish()
    for half, rows in enumerate((H0, H1)):
        da1 = tgrad[rows] + scatter.received(half)
        source, rinv = xf[rows, own].astype(f32), stats[rows][:, 4:5]
        gsum[0:1] = gsum[0:1] + jnp.sum(da1 * source, axis=0, keepdims=True)
        factor = inner[half * 256 : half * 256 + 256] * rinv * rinv * (1.0 / D)
        tgrad[rows] = dmid[rows] + gn[0, :, own] * da1 - source * factor
    dgain[0] = gsum[...]
    gain_y = [links.start(dgain.at[0], dgain.at[1 + j], here.ys[j]) for j in range(3)]

    for name in "dgu":
        advance(reduces[name])

    def hidden_blocks(target):
        return [
            (wg.at[target, zl, core, :, lanes(hid, 128)], fin_g.at[zl, core, :, lanes(x, 128)]),
            (wu.at[target, zl, core, :, lanes(hid, 128)], fin_u.at[zl, core, :, lanes(x, 128)]),
            (wd.at[zh, y, zl, core, :, lanes(target, 384)], fin_d.at[x, zl, core]),
        ]

    swaps = []
    for peer, target in ((here.right, here.ahead), (here.left, here.behind), (here.far, here.across)):
        swaps += [links.start(src, dst, peer) for src, dst in hidden_blocks(target)]
    swap_kept = [links.keep(src, dst) for src, dst in hidden_blocks(x)]

    for _ in range(2):
        advance(reduces["q"])
        advance(reduces["o"])

    for copy in swap_kept:
        copy.wait()
    arrive(swaps)
    fins = ((fin_g, 0), (fin_u, 0), (fin_d, 1))
    pick = lambda ref, lead, index: ref.at[(slice(None),) * lead + index]
    across_zl = [links.start(v, v, here.zs[0]) for v in (pick(ref, lead, (zl, core)) for ref, lead in fins)]

    arrive(gain_y)
    gsum[...] = dgain[0] + dgain[1] + dgain[2] + dgain[3]
    dgain[4] = gsum[...]
    gain_z = [links.start(dgain.at[4], dgain.at[5 + j], here.zs[j]) for j in range(3)]

    for _ in range(2):
        advance(reduces["q"])
    advance(reduces["o"])
    src_q, src_o = wqkv.at[zh, y, zl, core], wo.at[zh, x, zl, core, :, y_cols]
    dst_q, dst_o = fin_q.at[zl, core], fin_o.at[zl, core]
    mirror = [links.make(src_q, dst_q, here.mirror), links.make(src_o, dst_o, here.mirror)]
    first = links.local_count
    stay = [pltpu.make_async_copy(src_q, dst_q, local.at[first]), pltpu.make_async_copy(src_o, dst_o, local.at[first + 1])]

    @pl.when(x != y)
    def _():
        for copy in mirror:
            copy.start()
        for copy in mirror:
            copy.wait()

    @pl.when(x == y)
    def _():
        for copy in stay:
            copy.start()
        for copy in stay:
            copy.wait()

    head_zl = [links.start(v, v, here.zs[0]) for v in (fin_q.at[zl, core], fin_o.at[zl, core])]
    arrive(across_zl)
    to_core = [links.start(v, v, here.twin) for v in (pick(ref, lead, (slice(None), core)) for ref, lead in fins)]
    arrive(gain_z)
    gsum[...] = dgain[4] + dgain[5] + dgain[6] + dgain[7]
    dgain[8] = gsum[...]
    gain_c = links.start(dgain.at[8], dgain.at[9], here.twin)
    arrive(head_zl)
    head_core = [links.start(v, v, here.twin) for v in (fin_q.at[:, core], fin_o.at[:, core])]
    arrive([gain_c])
    arrive(to_core)
    arrive(head_core)
    links.close()


def outputs_kernel(mixed, tgrad, dgain, g_q, g_o, g_g, g_u, g_d, *outs):
    gains = dgain[8] + dgain[9]
    outs[0][...] = mixed[...]
    outs[1][...] = tgrad[...]
    outs[2][...] = gains[0:1]
    outs[5][...] = gains[1:2]
    for out, source in zip((outs[3], outs[4], outs[6], outs[7], outs[8]), (g_q, g_o, g_g, g_u, g_d)):
        out[...] = source[...].reshape(out.shape).astype(f32)


def run_layer(tokens, pos, gain_a, gain_f, qkvw, ow, gw, uw, dw, cot):
    s = jax.ShapeDtypeStruct
    v = pltpu.VMEM
    outs = [
        s((512, 384), f32),
        s((512, 384), f32),
        s((10, 8, 384), f32),
        s((2, 2, 96, 384), bf16),
        s((2, 2, 48, 384), bf16),
        s((2, 2, 96, 512), bf16),
        s((2, 2, 96, 512), bf16),
        s((4, 2, 2, 32, 384), bf16),
    ]
    scratch = [
        v((512, D), bf16),
        v((512, D), bf16),
        v((512, D), bf16),
        v((512, D), bf16),
        v((512, 128), f32),
        v((512, 1024), bf16),
        v((2, 512, 256), bf16),
        v((512, 512), bf16),
        v((512, 128), f32),
        v((512, 128), f32),
        v((512, 384), f32),
        v((2, 1, D), f32),
        v((4, 8, 128), i32),
        v((512, 384), bf16),
        v((2, 4, 2, 2, 96, 384), bf16),
        v((2, 4, 2, 2, 48, D), bf16),
        v((4, 2, 2, 96, 1024), bf16),
        v((4, 2, 2, 96, 1024), bf16),
        v((2, 4, 2, 2, 32, D), bf16),
        v((3, 512, 1024), bf16),
        v((4, 512, 384), bf16),
        v((4, 512, 384), bf16),
        v((3, 6, 256, 384), bf16),
        v((512, 128), f32),
        v((512, D), bf16),
        v((512, 384), f32),
        v((4, 512, 128), f32),
        v((4, 512, 128), f32),
        v((4, 512, 128), f32),
        v((2, 512, 256), bf16),
        v((2, 512, 384), bf16),
        v((2, 4, 8, 128), f32),
        v((512, 1), f32),
        v((8, 384), f32),
        v((4, 2, 96, 1024), bf16),
        v((4, 2, 96, 1024), bf16),
        v((2, 4, 2, 32, D), bf16),
        v((2, 4, 2, 96, 384), bf16),
        v((2, 2, 48, D), bf16),
        pltpu.SemaphoreType.DMA((340,)),
        pltpu.SemaphoreType.DMA((340,)),
        pltpu.SemaphoreType.DMA((20,)),
    ]
    scratch += [v(shape, bf16) for piece in slot_shapes() for step in piece for shape in step]
    return pl.pallas_call(
        layer_kernel,
        out_shape=outs,
        in_specs=[ANY] * 10 + [VM] * 3,
        out_specs=[VM] * len(outs),
        scratch_shapes=scratch,
        compiler_params=pltpu.CompilerParams(
            collective_id=0, has_side_effects=True, vmem_limit_bytes=63 * 1024 * 1024
        ),
        name="layer",
    )(tokens, pos, gain_a, gain_f, qkvw, ow, gw, uw, dw, cot, *constants())


def constants():
    half = HD // 2
    freq = np.zeros((8, 128), np.float32)
    rates = rope_base ** (-(np.arange(half) * 2.0 / HD))
    freq[:, :half] = rates
    freq[:, 64 : 64 + half] = rates
    perm = np.zeros((384, 512), np.float32)
    permo = np.zeros((512, 384), np.float32)
    for h in range(4):
        for d in range(HD):
            wide = d if (h == 3 or d < half) else d - half + 64
            perm[h * HD + d, h * 128 + wide] = 1
            permo[h * 128 + d, h * HD + d] = 1
    return jnp.asarray(freq), jnp.asarray(perm, bf16), jnp.asarray(permo, bf16)


def per_device(
    tokens,
    positions,
    attn_gain,
    qkv_weight,
    output_weight,
    ffn_gain,
    gate_weight,
    up_weight,
    down_weight,
    cotangent,
):
    parts = run_layer(
        tokens, positions.reshape(8, 128), attn_gain[None], ffn_gain[None], qkv_weight, output_weight,
        gate_weight, up_weight, down_weight, cotangent,
    )
    s = jax.ShapeDtypeStruct
    shapes = [(512, 384), (512, 384), (1, 384), (384, 384), (192, 384), (1, 384), (384, 512), (384, 512), (512, 384)]
    outs = pl.pallas_call(
        outputs_kernel,
        out_shape=[s(shape, f32) for shape in shapes],
        in_specs=[VM] * 8,
        out_specs=[VM] * 9,
        compiler_params=pltpu.CompilerParams(vmem_limit_bytes=32 * 1024 * 1024),
        name="outputs",
    )(*parts)
    return tuple(out.reshape(384) if out.shape == (1, 384) else out for out in outs)


def solution(mesh):
    finer = Mesh(mesh.devices.reshape(2, 2, 4, 2, 4), AXES)
    row = ("y", "zh")
    in_specs = (
        P(DP_ROW, "x"),
        P(("zl", "core", "x")),
        P("x"),
        P("x", row),
        P(row, "x"),
        P("x"),
        P("x", row),
        P("x", row),
        P(row, "x"),
        P(DP_ROW, "x"),
    )
    out_specs = (
        P(DP_ROW, "x"),
        P(DP_ROW, "x"),
        P("x"),
        P("x", row),
        P(row, "x"),
        P("x"),
        P("x", row),
        P("x", row),
        P(row, "x"),
    )
    return jax.shard_map(per_device, mesh=finer, in_specs=in_specs, out_specs=out_specs, check_vma=False)
```

```python
import functools
import math

import jax
import jax.numpy as jnp
import numpy as np
from jax import lax
from jax.experimental import pallas as pl
from jax.experimental.pallas import tpu as pltpu
from jax.sharding import Mesh
from jax.sharding import PartitionSpec as P

D = 1536
HD = 96
AXES = ("zl", "core", "y", "zh", "x")
DP_ROW = ("zl", "core", "y", "zh")
bf16 = jnp.bfloat16
f32 = jnp.float32
i32 = jnp.int32
MESH = pl.DeviceIdType.MESH
VM = pl.BlockSpec(memory_space=pltpu.VMEM)
ANY = pl.BlockSpec(memory_space=pl.ANY)

epsilon = 1e-05
rope_base = 100000.0
masked_score = -1e30
score_scale = math.log2(math.e) / math.sqrt(HD)
H0, H1 = pl.ds(0, 256), pl.ds(256, 256)


def dot(a, b):
    return lax.dot_general(a, b, (((1,), (0,)), ((), ())), preferred_element_type=f32)


def dot_t(a, b):
    return lax.dot_general(a, b, (((1,), (1,)), ((), ())), preferred_element_type=f32)


def lanes(index, width):
    return pl.ds(pl.multiple_of(index * width, 128), width)


class Place:
    def __init__(self):
        self.x, self.y = lax.axis_index("x"), lax.axis_index("y")
        self.zl, self.zh, self.core = lax.axis_index("zl"), lax.axis_index("zh"), lax.axis_index("core")
        self.quarter = self.zl * 2 + self.core
        self.ahead, self.behind, self.across = [(self.x + k) % 4 for k in (1, 3, 2)]
        self.right, self.left, self.far = {"x": self.ahead}, {"x": self.behind}, {"x": self.across}
        self.ys = [{"y": (self.y + k) % 4} for k in (1, 3, 2)]
        self.zs = [{"zl": 1 - self.zl}, {"zl": 1 - self.zl, "zh": 1 - self.zh}, {"zh": 1 - self.zh}]
        self.twin = {"core": 1 - self.core}
        self.mirror = {"x": self.y, "y": self.x}
        y, zl, zh = self.y, self.zl, self.zh
        beside, opposite = y + 1 - y % 2 * 2, 3 - y
        self.cube = {
            "ya": ({"y": beside}, (beside, zl, zh)),
            "yb": ({"y": opposite}, (opposite, zl, zh)),
            "za": ({"zl": 1 - zl}, (y, 1 - zl, zh)),
            "zb": ({"zl": 1 - zl, "zh": 1 - zh}, (y, 1 - zl, 1 - zh)),
        }

    def across_link(self, name):
        return self.cube[name]

    def enter(self):
        barrier = pltpu.get_barrier_semaphore()
        peers = [self.right, self.left, self.far, *self.ys, *self.zs, self.twin]
        for peer in peers:
            pl.semaphore_signal(barrier, inc=1, device_id=peer, device_id_type=MESH)

        @pl.when(self.x != self.y)
        def _():
            pl.semaphore_signal(barrier, inc=1, device_id=self.mirror, device_id_type=MESH)
            pl.semaphore_wait(barrier, len(peers) + 1)

        @pl.when(self.x == self.y)
        def _():
            pl.semaphore_wait(barrier, len(peers))


class Links:
    def __init__(self, send, recv, local):
        self.send, self.recv, self.local, self.count, self.local_count = send, recv, local, 0, 0
        self.open = []

    def make(self, src, dst, device):
        i = self.count
        self.count += 1
        return pltpu.make_async_remote_copy(
            src, dst, self.send.at[i], self.recv.at[i], device_id=device, device_id_type=MESH
        )

    def start(self, src, dst, device):
        copy = self.make(src, dst, device)
        copy.start()
        self.open.append(copy)
        return copy

    def spread(self, ref, devices):
        return [self.start(ref, ref, device) for device in devices]

    def keep(self, src, dst):
        copy = pltpu.make_async_copy(src, dst, self.local.at[self.local_count])
        self.local_count += 1
        copy.start()
        return copy

    def settle(self, copies):
        for copy in copies:
            copy.wait_send()
        self.open = [copy for copy in self.open if all(copy is not done for done in copies)]

    def close(self):
        self.settle(list(self.open))


def arrive(copies):
    for copy in copies:
        copy.wait_recv()


class RingGather:
    def __init__(self, links, here, src, buf):
        cols = lanes(here.x, 384)
        self.links, self.here, self.buf = links, here, buf
        self.first = [
            links.start(src(H0), buf.at[H0, cols], here.right),
            links.start(src(H1), buf.at[H1, cols], here.left),
        ]
        self.second = [
            links.start(src(H1), buf.at[H1, cols], here.right),
            links.start(src(H0), buf.at[H0, cols], here.left),
        ]

    def forward(self):
        here, buf = self.here, self.buf
        self.first[0].wait_recv()
        a = buf.at[H0, lanes(here.behind, 384)]
        self.third = [self.links.start(a, a, here.right)]
        self.first[1].wait_recv()
        b = buf.at[H1, lanes(here.ahead, 384)]
        self.third += [self.links.start(b, b, here.left)]

    def near(self):
        arrive(self.second)

    def finish(self):
        arrive(self.third)

    def settle(self):
        self.links.settle(self.first + self.second + self.third)


class RingScatter:
    def __init__(self, links, here, part, slots):
        self.links, self.here, self.part, self.slots = links, here, part, slots

    def send_far(self):
        h, p, s = self.here, self.part, self.slots
        self.r0 = self.links.start(p.at[h.across, H0], s.at[0], h.right)
        self.l0 = self.links.start(p.at[h.across, H1], s.at[1], h.left)

    def send_near(self):
        h, p, s = self.here, self.part, self.slots
        self.r1 = self.links.start(p.at[h.ahead, H1], s.at[2], h.right)
        self.l1 = self.links.start(p.at[h.behind, H0], s.at[3], h.left)

    def forward(self):
        h, p, s = self.here, self.part, self.slots
        self.r0.wait_recv()
        p[h.ahead, H0] = (p[h.ahead, H0].astype(f32) + s[0].astype(f32)).astype(bf16)
        self.r2 = self.links.start(p.at[h.ahead, H0], s.at[4], h.right)
        self.l0.wait_recv()
        p[h.behind, H1] = (p[h.behind, H1].astype(f32) + s[1].astype(f32)).astype(bf16)
        self.l2 = self.links.start(p.at[h.behind, H1], s.at[5], h.left)

    def finish(self):
        arrive([self.r1, self.l1, self.r2, self.l2])

    def settle(self):
        self.links.settle([self.r0, self.l0, self.r1, self.l1, self.r2, self.l2])

    def received(self, half):
        s = self.slots
        pair = (4, 3) if half == 0 else (2, 5)
        return s[pair[0]].astype(f32) + s[pair[1]].astype(f32)


ORDERS = (("ya", "yb", "za", "zb"), ("za", "zb", "ya", "yb"), ("yb", "ya", "zb", "za"), ("zb", "za", "yb", "ya"))


def part_of(order):
    y_state = {(): "own", ("ya",): "pair", ("yb",): "cross"}.get(tuple(d for d in order if d[0] == "y"), "all")
    z_state = {(): "own", ("za",): "low", ("zb",): "cross"}.get(tuple(d for d in order if d[0] == "z"), "all")
    return y_state, z_state


def y_cells(state, y):
    return {"own": [(y, 1)], "pair": [(y // 2 * 2, 2)], "cross": [(y, 1), (3 - y, 1)], "all": [(0, 4)]}[state]


def z_cells(state, zl, zh, joined):
    if state == "all" and not joined:
        return [(None, 0), (None, 1)]
    cells = {"own": [(zl, zh)], "low": [(None, zh)], "cross": [(zl, zh), (1 - zl, 1 - zh)], "all": [(None, None)]}
    return cells[state]


def either(index):
    return slice(None) if index is None else index


class UnitColumns:
    def __init__(self, core, start, size):
        self.core, self.start, self.size = core, start, size

    def cells(self, state, y, zl, zh):
        rows = pl.ds(self.start, self.size)
        return [
            (slice(None), either(l), self.core, rows, pl.ds(pl.multiple_of(h * 512 + first * 128, 128), count * 128))
            for l, h in z_cells(state[1], zl, zh, False)
            for first, count in y_cells(state[0], y)
        ]

    def shapes(self, state):
        return [
            (4,) + ((2,) if l is None else ()) + (self.size, count * 128)
            for l, _ in z_cells(state[1], 0, 0, False)
            for _, count in y_cells(state[0], 0)
        ]


class Blocks:
    def __init__(self, core, start, size, width):
        self.core, self.start, self.size, self.width = core, start, size, width

    def cells(self, state, y, zl, zh):
        rows = pl.ds(self.start, self.size)
        pick = lambda first, count: first if count == 1 else (slice(None) if count == 4 else pl.ds(first, count))
        return [
            (either(h), pick(first, count), either(l), self.core, rows)
            for l, h in z_cells(state[1], zl, zh, True)
            for first, count in y_cells(state[0], y)
        ]

    def shapes(self, state):
        return [
            ((2,) if h is None else ()) + ((count,) if count > 1 else ()) + ((2,) if l is None else ()) + (self.size, self.width)
            for l, h in z_cells(state[1], 0, 0, True)
            for _, count in y_cells(state[0], 0)
        ]


class OutputRows:
    def __init__(self, core, start, size, place):
        self.core, self.start, self.size, self.place = core, start, size, place

    def cells(self, state, y, zl, zh):
        rows = pl.ds(self.start, self.size)
        return [
            (either(h), self.place, either(l), self.core, rows, pl.ds(pl.multiple_of(first * 384, 128), count * 384))
            for l, h in z_cells(state[1], zl, zh, True)
            for first, count in y_cells(state[0], y)
        ]

    def shapes(self, state):
        return [
            ((2,) if h is None else ()) + ((2,) if l is None else ()) + (self.size, count * 384)
            for l, h in z_cells(state[1], 0, 0, True)
            for _, count in y_cells(state[0], 0)
        ]


class CubeGather:
    def __init__(self, links, here, ref, layout, order):
        self.links, self.here, self.ref, self.layout, self.order, self.step = links, here, ref, layout, order, 0
        self.launch()

    def launch(self):
        here, ref = self.here, self.ref
        device, _ = here.across_link(self.order[self.step])
        cells = self.layout.cells(part_of(self.order[: self.step]), here.y, here.zl, here.zh)
        self.copies = [self.links.start(ref.at[cell], ref.at[cell], device) for cell in cells]

    def advance(self):
        arrive(self.copies)
        self.step += 1
        if self.step < 4:
            self.launch()


class CubeReduce:
    def __init__(self, links, here, ref, layout, order, slots):
        self.links, self.here, self.ref, self.layout, self.order, self.step = links, here, ref, layout, order, 3
        self.slots = slots
        self.launch()

    def launch(self):
        here, ref = self.here, self.ref
        device, coordinates = here.across_link(self.order[self.step])
        cells = self.layout.cells(part_of(self.order[: self.step]), *coordinates)
        pairs = zip(cells, self.slots[self.step])
        self.copies = [self.links.start(ref.at[cell], slot, device) for cell, slot in pairs]

    def advance(self):
        here, ref = self.here, self.ref
        arrive(self.copies)
        cells = self.layout.cells(part_of(self.order[: self.step]), here.y, here.zl, here.zh)
        for cell, slot in zip(cells, self.slots[self.step]):
            ref[cell] = (ref[cell].astype(f32) + slot[...].astype(f32)).astype(bf16)
        self.step -= 1
        if self.step >= 0:
            self.launch()


def advance(cubes):
    for cube in cubes:
        cube.advance()


def grad_layouts(core, place):
    return [
        ("d", Blocks(core, 0, 16, D), 0),
        ("d", Blocks(core, 16, 16, D), 3),
        ("g", UnitColumns(core, 0, 48), 0),
        ("g", UnitColumns(core, 48, 48), 1),
        ("u", UnitColumns(core, 0, 48), 2),
        ("u", UnitColumns(core, 48, 48), 3),
        ("o", OutputRows(core, 0, 16, place), 1),
        ("o", OutputRows(core, 16, 16, place), 2),
        ("o", OutputRows(core, 32, 16, place), 3),
        ("q", Blocks(core, 0, 32, 384), 0),
        ("q", Blocks(core, 32, 32, 384), 1),
        ("q", Blocks(core, 64, 16, 384), 2),
        ("q", Blocks(core, 80, 16, 384), 3),
    ]


def slot_shapes():
    return [
        [layout.shapes(part_of(ORDERS[order][:step])) for step in range(4)] for _, layout, order in grad_layouts(0, 0)
    ]


def sine_cosine(angle):
    turns = jnp.floor(angle * (1.0 / (2.0 * math.pi)) + 0.5)
    r = angle - turns * 6.28125
    r = r - turns * 0.0019350051879882812
    r = r - turns * 3.0199159819185874e-07
    t = r * 0.5
    t2 = t * t
    s = 1.0 / 6227020800.0
    for c in (-1.0 / 39916800, 1.0 / 362880, -1.0 / 5040, 1.0 / 120, -1.0 / 6, 1.0):
        s = s * t2 + c
    s = s * t
    c_ = 1.0 / 479001600.0
    for c in (-1.0 / 3628800, 1.0 / 40320, -1.0 / 720, 1.0 / 24, -0.5, 1.0):
        c_ = c_ * t2 + c
    return 2.0 * s * c_, 1.0 - 2.0 * s * s


def causal(scores):
    last = scores[:, -256:]
    seen = lax.broadcasted_iota(i32, (256, 256), 1) <= lax.broadcasted_iota(i32, (256, 256), 0)
    last = jnp.where(seen, last, masked_score)
    return last if scores.shape[1] == 256 else jnp.concatenate([scores[:, :-256], last], axis=1)


def turn(head, cosine, sine):
    return head * cosine + pltpu.roll(head, 64, 1) * sine


def dot_first(a, b):
    return lax.dot_general(a, b, (((0,), (0,)), ((), ())), preferred_element_type=f32)


def column_to_rows(column, ref):
    for c in range(4):
        block = jnp.broadcast_to(column[c * 128 : c * 128 + 128], (128, 128)).T
        ref[c : c + 1] = block[0:1]


def rows_to_column(rows):
    return jnp.concatenate([jnp.broadcast_to(rows[c : c + 1], (128, 128)).T for c in range(4)], 0)


def layer_kernel(
    tokens, pos, gain_a, gain_f, qkvw, ow, gw, uw, dw, cot, freq, perm, permo,
    mixed, tgrad, dgain, fin_q, fin_o, fin_g, fin_u, fin_d,
    xf, a1, a2, cotf, stats, qkv, kvr, att, cosb, sinb, middle, gn, posb, packed,
    wqkv, wo, wg, wu, wd, hdd, part, partd, slots, wide, dzf, dmid,
    dq, dkv, dkr, dkin, dproj, small, sums, gsum, rc_g, rc_u, rc_d, rc_q, rc_o,
    send, recv, local, *slot_refs,
):
    here = Place()
    links = Links(send, recv, local)
    x, y, zl, zh, core, quarter = here.x, here.y, here.zl, here.zh, here.core, here.quarter
    hid = zh * 4 + y
    other = 1 - core
    own, y_cols = lanes(x, 384), lanes(y, 384)
    a, b, da, db, oa, ob = pl.ds(0, 48), pl.ds(48, 48), pl.ds(0, 16), pl.ds(16, 16), pl.ds(0, 32), pl.ds(32, 16)
    refs = iter(slot_refs)
    layouts = [
        (name, layout, ORDERS[order], [[next(refs) for _ in shapes] for shapes in steps])
        for (name, layout, order), steps in zip(grad_layouts(core, x), slot_shapes())
    ]
    x_peers = (here.right, here.left, here.far)
    here.enter()

    own_qkv, src_qkv = wqkv.at[zh, x, zl, core], qkvw.at[pl.ds(quarter * 96, 96)]
    own_o, src_o = wo.at[zh, y, zl, core, :, own], ow.at[pl.ds(quarter * 48, 48)]
    mirror = [links.make(src_qkv, own_qkv, here.mirror)]
    stay = [pltpu.make_async_copy(src_qkv, own_qkv, local.at[0])]
    links.local_count = 2

    @pl.when(x != y)
    def _():
        for copy in mirror:
            copy.start()

    @pl.when(x == y)
    def _():
        for copy in stay:
            copy.start()

    def hidden_slices(target):
        rows = pl.ds(quarter * 96, 96)
        return [
            (gw.at[rows, lanes(target, 128)], wg.at[x, zl, core, :, lanes(hid, 128)]),
            (uw.at[rows, lanes(target, 128)], wu.at[x, zl, core, :, lanes(hid, 128)]),
            (dw.at[pl.ds(target * 128 + quarter * 32, 32)], wd.at[zh, y, zl, core, :, own]),
        ]

    swaps = []
    for peer, target in ((here.right, here.ahead), (here.left, here.behind), (here.far, here.across)):
        swaps += [links.start(src, dst, peer) for src, dst in hidden_slices(target)]
    swap_kept = [links.keep(src, dst) for src, dst in hidden_slices(x)]
    swaps_o = [links.start(src_o, own_o, peer) for peer in x_peers]
    swap_kept_o = links.keep(src_o, own_o)

    ring_x = RingGather(links, here, lambda half: tokens.at[half], xf)
    kept = [links.keep(tokens, xf.at[:, own])]
    small_sends = []
    for peer in x_peers:
        small_sends.append(links.start(pos, posb.at[x], peer))
        small_sends.append(links.start(gain_a, gn.at[0, :, own], peer))
        small_sends.append(links.start(gain_f, gn.at[1, :, own], peer))
    kept += [links.keep(pos, posb.at[x]), links.keep(gain_a, gn.at[0, :, own]), links.keep(gain_f, gn.at[1, :, own])]

    @pl.when(x != y)
    def _():
        for copy in mirror:
            copy.wait()

    @pl.when(x == y)
    def _():
        for copy in stay:
            copy.wait()

    pieces = ((0, 32), (32, 32), (64, 16), (80, 16))
    cube_q = [
        CubeGather(links, here, wqkv, Blocks(core, start, size, 384), ORDERS[k]) for k, (start, size) in enumerate(pieces)
    ]
    advance(cube_q)
    for copy in swap_kept:
        copy.wait()
    arrive(swaps)
    cube_g = [CubeGather(links, here, wg, UnitColumns(core, 48 * k, 48), ORDERS[k]) for k in range(2)]
    cube_u = [CubeGather(links, here, wu, UnitColumns(core, 48 * k, 48), ORDERS[2 + k]) for k in range(2)]
    cube_d = [CubeGather(links, here, wd, Blocks(core, 16 * k, 16, D), ORDERS[3 * k]) for k in range(2)]
    ring_x.forward()
    advance(cube_q)
    swap_kept_o.wait()
    arrive(swaps_o)
    cube_o = [CubeGather(links, here, wo, Blocks(core, 16 * k, 16, D), ORDERS[1 + k]) for k in range(3)]
    advance(cube_g)
    advance(cube_u)
    advance(cube_d)
    advance(cube_q)
    advance(cube_o)

    for copy in kept:
        copy.wait()
    arrive(small_sends)
    mine = posb[y]
    mine = jnp.where(zh == 0, mine[0:4], mine[4:8]).astype(f32)
    lane = lax.broadcasted_iota(i32, (128, 128), 1)
    for c in range(4):
        column = jnp.broadcast_to(mine[c : c + 1], (128, 128)).T
        sine, cosine = sine_cosine(column * freq[0:1])
        cosb[pl.ds(c * 128, 128)] = cosine
        sinb[pl.ds(c * 128, 128)] = jnp.where(lane < 64, -sine, sine)

    ring_x.near()
    ring_x.finish()
    ring_c = RingGather(links, here, lambda half: cot.at[half], cotf)
    cot_kept = links.keep(cot, cotf.at[:, own])

    def norm_tokens(i, _):
        rows = pl.ds(pl.multiple_of(i * 64, 64), 64)
        value = xf[rows].astype(f32)
        inverse = lax.rsqrt(jnp.sum(value * value, axis=1, keepdims=True) * (1.0 / D) + epsilon)
        a1[rows] = (value * gn[0]).astype(bf16)
        stats[rows] = jnp.broadcast_to(inverse, (64, 128))
        return 0

    lax.fori_loop(0, 8, norm_tokens, 0)

    advance(cube_q)
    core_qkv = links.spread(wqkv.at[:, :, :, core], [here.twin])
    advance(cube_g)
    advance(cube_u)
    advance(cube_d)
    advance(cube_o)

    arrive(core_qkv)

    def widen(i, _):
        w = wqkv[i].reshape(D, 384)
        for j in range(3):
            hdd[j, :, lanes(i, 512)] = dot(w[j * 512 : j * 512 + 512], perm[...]).astype(bf16)
        return 0

    lax.fori_loop(0, 2, widen, 0)

    def keys_values(g, _):
        pair = dot(a1[...], hdd[:, :, lanes(g * 2 + 1, 256)].reshape(D, 256))
        inverse = stats[...]
        qkv[:, lanes(g * 4 + 2, 128)] = turn(pair[:, :128] * inverse, cosb[...], sinb[...]).astype(bf16)
        qkv[:, lanes(g * 4 + 3, 128)] = (pair[:, 128:] * inverse).astype(bf16)
        return 0

    lax.fori_loop(0, 2, keys_values, 0)
    over = [links.make(qkv.at[:, pl.ds(g * 512 + 256, 256)], kvr.at[g], here.zs[2]) for g in range(2)]

    @pl.when(zh == 0)
    def _():
        for copy in over:
            copy.start()

    advance(cube_g)
    advance(cube_u)
    advance(cube_d)
    advance(cube_o)

    def queries(g, _):
        pair = dot(a1[...], hdd[:, :, lanes(g * 2, 256)].reshape(D, 256))
        inverse = stats[...]
        for h in range(2):
            head = pair[:, h * 128 : h * 128 + 128] * inverse
            qkv[:, lanes(g * 4 + h, 128)] = (turn(head, cosb[...], sinb[...]) * score_scale).astype(bf16)
        return 0

    lax.fori_loop(0, 2, queries, 0)
    ring_c.forward()

    def own_scores(i, _):
        g = i // 2
        for qb in range(2):
            rows, keys = pl.ds(qb * 256, 256), pl.ds(0, qb * 256 + 256)
            q = qkv[rows, lanes(g * 4 + i % 2, 128)]
            s = causal(dot_t(q, qkv[keys, lanes(g * 4 + 2, 128)]))
            m = jnp.max(s, axis=1, keepdims=True)
            e = jnp.exp2(s - m)
            dq[i, rows] = dot(e.astype(bf16), qkv[keys, lanes(g * 4 + 3, 128)])
            dkv[i, rows] = jnp.broadcast_to(m, (256, 128))
            dkr[i, rows] = jnp.broadcast_to(jnp.sum(e, axis=1, keepdims=True), (256, 128))
        return 0

    lax.fori_loop(0, 4, own_scores, 0)

    @pl.when(zh == 1)
    def _():
        for copy in over:
            copy.wait_recv()

        def first_scores(i, _):
            g = i // 2
            for qb in range(2):
                rows = pl.ds(qb * 256, 256)
                q = qkv[rows, lanes(g * 4 + i % 2, 128)]
                s = dot_t(q, kvr[g, :, 0:128])
                old = dkv[i, rows][:, 0:1]
                m = jnp.maximum(old, jnp.max(s, axis=1, keepdims=True))
                e = jnp.exp2(s - m)
                shrink = jnp.exp2(old - m)
                dq[i, rows] = dq[i, rows] * shrink + dot(e.astype(bf16), kvr[g, :, 128:256])
                dkr[i, rows] = dkr[i, rows] * shrink + jnp.sum(e, axis=1, keepdims=True)
                dkv[i, rows] = jnp.broadcast_to(m, (256, 128))
            return 0

        lax.fori_loop(0, 4, first_scores, 0)

    @pl.when(zh == 0)
    def _():
        for copy in over:
            copy.wait_send()

    advance(cube_o)
    core_o = links.spread(wo.at[:, :, :, core], [here.twin])
    lane = lax.broadcasted_iota(i32, (512, 128), 1)
    for i in range(4):
        att[:, i * 128 : i * 128 + 128] = (dq[i] / dkr[i]).astype(bf16)
        stats[...] = jnp.where(lane == i, dkv[i] + jnp.log2(dkr[i]), stats[...])

    packed[...] = dot(att[...], permo[...]).astype(bf16)
    ring_a = RingGather(links, here, lambda half: packed.at[half], dzf)
    dzf[:, own] = packed[...]
    thirds = (dq, dkv, dkr)

    def output_part(block, c):
        return dot(dzf[:, lanes(block, 384)], wo[:, block, :, :, :, lanes(c, 384)].reshape(384, 384))

    def output_first(c, _):
        value = xf[:, lanes(c, 384)].astype(f32) + output_part(x, c)
        for k, ref in enumerate(thirds):
            ref[c] = value[:, k * 128 : k * 128 + 128]
        return 0

    def output_near(c, _):
        value = output_part(here.ahead, c) + output_part(here.behind, c)
        for k, ref in enumerate(thirds):
            ref[c] = ref[c] + value[:, k * 128 : k * 128 + 128]
        return 0

    def output_last(c, _):
        value = output_part(here.across, c)
        for k, ref in enumerate(thirds):
            m = ref[c] + value[:, k * 128 : k * 128 + 128]
            ref[c] = m
            a2[:, lanes(c * 3 + k, 128)] = (m * gn[1, :, lanes(c * 3 + k, 128)]).astype(bf16)
            sums[...] = sums[...] + jnp.sum(m * m, axis=1, keepdims=True)
        return 0

    arrive(core_o)
    lax.fori_loop(0, 4, output_first, 0)
    ring_a.forward()
    advance(cube_g)
    cores = [links.start(wg.at[:, :, core], wg.at[:, :, core], here.twin)]
    advance(cube_u)
    cores.append(links.start(wu.at[:, :, core], wu.at[:, :, core], here.twin))
    advance(cube_d)
    cores.append(links.start(wd.at[:, :, :, core], wd.at[:, :, :, core], here.twin))
    ring_a.near()
    lax.fori_loop(0, 4, output_near, 0)
    cot_kept.wait()
    ring_c.near()
    ring_c.finish()
    sums[...] = jnp.zeros_like(sums)
    ring_a.finish()
    lax.fori_loop(0, 4, output_last, 0)
    wide[...] = jnp.broadcast_to(lax.rsqrt(sums[...] * (1.0 / D) + epsilon), (512, 128))
    for k, ref in enumerate(thirds):
        middle[:, k * 128 : k * 128 + 128] = ref[x]
    links.close()
    arrive(cores)

    sums[...] = jnp.zeros_like(sums)

    def units(n, _):
        cols = lanes(n, 256)
        w_g = wg[:, :, :, :, cols].reshape(D, 256)
        w_u = wu[:, :, :, :, cols].reshape(D, 256)
        w_d = wd[n // 2, pl.ds((n % 2) * 2, 2)].reshape(256, D)
        for rows in (H0, H1):
            inverse = wide[rows][:, 0:1]
            gate = dot(a2[rows], w_g) * inverse
            up = dot(a2[rows], w_u) * inverse
            dh = dot_t(cotf[rows], w_d)
            sg = 1.0 / (1.0 + jnp.exp(-gate))
            silu = gate * sg
            dg = dh * up * (sg + silu * (1.0 - sg))
            du = dh * silu
            hdd[0, rows, cols] = (silu * up).astype(bf16)
            hdd[1, rows, cols] = (dg * inverse).astype(bf16)
            hdd[2, rows, cols] = (du * inverse).astype(bf16)
            inner = jnp.sum(dg * gate + du * up, axis=1, keepdims=True)
            sums[rows] = sums[rows] + inner
        return 0

    lax.fori_loop(0, 4, units, 0)

    def back_block(block):
        return dot_t(hdd[1], wg[block].reshape(384, 1024)) + dot_t(hdd[2], wu[block].reshape(384, 1024))

    scatter = RingScatter(links, here, part, slots.at[0])
    part[here.across] = back_block(here.across).astype(bf16)
    scatter.send_far()
    part[here.ahead] = back_block(here.ahead).astype(bf16)
    part[here.behind] = back_block(here.behind).astype(bf16)
    scatter.send_near()
    column_to_rows(sums[...], small.at[0, x])
    inner_sums = [links.start(small.at[0, x], small.at[0, x], p) for p in x_peers]
    dmid[...] = back_block(x)
    scatter.forward()

    def down_block(block, _):
        cols = lanes(block, 384)
        partd[block] = dot(hdd[0], wd[:, :, :, :, :, cols].reshape(1024, 384)).astype(bf16)
        return 0

    lax.fori_loop(0, 4, down_block, 0)

    def down_grad(n, _):
        rows = hdd[0, :, lanes(n, 256)].T
        for c in range(3):
            cols = pl.ds(c * 512, 512)
            value = dot(rows, cotf[:, cols]).astype(bf16)
            wd[n // 2, pl.ds((n % 2) * 2, 2), :, :, :, cols] = value.reshape(2, 2, 2, 32, 512)
        return 0

    lax.fori_loop(0, 4, down_grad, 0)
    cores = [links.start(wd.at[:, :, :, other], rc_d, here.twin)]

    def up_grads(block, _):
        rows = a2[:, lanes(block, 384)].T
        for source, target in ((1, wg), (2, wu)):
            for c in range(2):
                cols = pl.ds(c * 512, 512)
                target[block, :, :, :, cols] = dot(rows, hdd[source, :, cols]).astype(bf16).reshape(2, 2, 96, 512)
        return 0

    lax.fori_loop(0, 4, up_grads, 0)
    cores.append(links.start(wg.at[:, :, other], rc_g, here.twin))
    cores.append(links.start(wu.at[:, :, other], rc_u, here.twin))

    buffers = {"d": wd, "g": wg, "u": wu, "o": wo, "q": wqkv}
    reduces = {}

    def start_reduce(name):
        reduces[name] = [
            CubeReduce(links, here, buffers[name], layout, order, slots_)
            for piece, layout, order, slots_ in layouts
            if piece == name
        ]

    def core_sum_down(i, _):
        for k in range(2):
            for j in range(2):
                value = wd[k, i, j, core].astype(f32) + rc_d[k, i, j].astype(f32)
                wd[k, i, j, core] = value.astype(bf16)
        return 0

    arrive(cores[0:1])
    lax.fori_loop(0, 4, core_sum_down, 0)
    start_reduce("d")

    arrive(inner_sums)
    inner = rows_to_column(jnp.sum(small[0], axis=0)[0:4])[:, 0:1]
    scatter.finish()
    gsum[...] = jnp.zeros_like(gsum)
    for half, rows in enumerate((H0, H1)):
        da2 = dmid[rows] + scatter.received(half)
        m, inverse = middle[rows], wide[rows][:, 0:1]
        gsum[1:2] = gsum[1:2] + jnp.sum(da2 * m, axis=0, keepdims=True)
        factor = inner[half * 256 : half * 256 + 256] * inverse * inverse * (1.0 / D)
        value = cotf[rows, own].astype(f32) + gn[1, :, own] * da2 - m * factor
        dmid[rows] = value
        dzf[rows, own] = value.astype(bf16)
    ring_z = RingGather(links, here, lambda half: dzf.at[half, own], dzf)
    ring_z.forward()

    for matrix, (name, source) in enumerate((("g", rc_g), ("u", rc_u))):
        arrive(cores[matrix + 1 : matrix + 2])

        def core_sum(i, _, target=buffers[name], source=source):
            for j in range(2):
                target[i, j, core] = (target[i, j, core].astype(f32) + source[i, j].astype(f32)).astype(bf16)
            return 0

        lax.fori_loop(0, 4, core_sum, 0)
        start_reduce(name)

    ring_z.near()
    ring_z.finish()

    scatter_d = RingScatter(links, here, partd, slots.at[1])
    scatter_d.send_far()
    scatter_d.send_near()

    packed[...] = dot_t(dzf[...], wo[:, x].reshape(384, D)).astype(bf16)
    hdd[1, :, 0:512] = dot_t(packed[...], permo[...]).astype(bf16)
    packed[...] = dot(att[...], permo[...]).astype(bf16)
    for c in range(3):
        cols = pl.ds(c * 512, 512)
        value = dot_first(packed[...], dzf[:, cols]).astype(bf16)
        wo[:, x, :, :, :, cols] = value.reshape(2, 2, 2, 48, 512)
    cores = [links.start(wo.at[:, x, :, other], rc_o, here.twin)]

    dq[...] = jnp.zeros_like(dq)
    dkv[...] = jnp.zeros_like(dkv)

    def pair(i, rows, k, v, masked):
        g = i // 2
        head = lanes(i, 128)
        q, grad = qkv[rows, lanes(g * 4 + i % 2, 128)], hdd[1, rows, head]
        delta = jnp.sum(grad.astype(f32) * att[rows, head].astype(f32), axis=1, keepdims=True)
        lane = lax.broadcasted_iota(i32, (256, 128), 1)
        lse = jnp.sum(jnp.where(lane == i, stats[rows], 0.0), axis=1, keepdims=True)
        s = dot_t(q, k)
        if masked:
            s = causal(s)
        p = jnp.exp2(s - lse)
        ds = (p * (dot_t(grad, v) - delta)).astype(bf16)
        dq[i, rows] = dq[i, rows] + dot(ds, k)
        return dot_first(ds, q), dot_first(p.astype(bf16), grad)

    give = [links.make(kvr.at[g], dkin.at[g], here.zs[2]) for g in range(2)]

    @pl.when(zh == 1)
    def _():
        dkr[...] = jnp.zeros_like(dkr)

        def first_half(i, _):
            g = i // 2
            for qb in range(2):
                dk, dv = pair(i, pl.ds(qb * 256, 256), kvr[g, :, 0:128], kvr[g, :, 128:256], False)
                dkr[2 * g] = dkr[2 * g] + dk
                dkr[2 * g + 1] = dkr[2 * g + 1] + dv
            return 0

        for g in range(2):
            lax.fori_loop(2 * g, 2 * g + 2, first_half, 0)
            kvr[g, :, 0:128] = dkr[2 * g].astype(bf16)
            kvr[g, :, 128:256] = dkr[2 * g + 1].astype(bf16)
            give[g].start()

    scatter_d.forward()

    def own_keys(i, _):
        g = i // 2
        for qb in range(2):
            keys = pl.ds(0, qb * 256 + 256)
            k, v = qkv[keys, lanes(g * 4 + 2, 128)], qkv[keys, lanes(g * 4 + 3, 128)]
            dk, dv = pair(i, pl.ds(qb * 256, 256), k, v, True)
            dkv[2 * g, keys] = dkv[2 * g, keys] + dk
            dkv[2 * g + 1, keys] = dkv[2 * g + 1, keys] + dv
        return 0

    lax.fori_loop(0, 4, own_keys, 0)

    @pl.when(zh == 0)
    def _():
        for g in range(2):
            give[g].wait_recv()
            dkv[2 * g] = dkv[2 * g] + dkin[g, :, 0:128].astype(f32)
            dkv[2 * g + 1] = dkv[2 * g + 1] + dkin[g, :, 128:256].astype(f32)

    @pl.when(zh == 1)
    def _():
        for g in range(2):
            give[g].wait_send()

    for name in "dgu":
        advance(reduces[name])
    arrive(cores)
    for g in range(2):
        for j in range(2):
            wo[g, x, j, core] = (wo[g, x, j, core].astype(f32) + rc_o[g, j].astype(f32)).astype(bf16)
    start_reduce("o")

    sums[...] = jnp.zeros_like(sums)
    inverse = stats[:, 4:5]
    for i in range(8):
        cols = pl.ds(i * 128, 128)
        g, place = i // 4, i % 4
        value = dq[2 * g + place] if place < 2 else dkv[2 * g + place - 2]
        if place == 2:
            value = value * math.log(2.0)
        inside = jnp.sum(value * qkv[:, cols].astype(f32), axis=1, keepdims=True)
        if place < 2:
            inside = inside * math.log(2.0)
            value = value * (1.0 / math.sqrt(HD))
        sums[...] = sums[...] + inside
        if place < 3:
            value = turn(value, cosb[...], -sinb[...])
        hdd[0, :, cols] = (value * inverse).astype(bf16)
    column_to_rows(sums[...], small.at[1, x])
    inner_sums = [links.start(small.at[1, x], small.at[1, x], p) for p in x_peers]
    for g in range(2):
        dproj[g] = dot_t(hdd[0, :, g * 512 : g * 512 + 512], perm[...]).astype(bf16)

    def back_input(block):
        return sum(dot_t(dproj[g], wqkv[g, block].reshape(384, 384)) for g in range(2))

    scatter.settle()
    scatter = RingScatter(links, here, part, slots.at[2])
    part[here.across] = back_input(here.across).astype(bf16)
    scatter.send_far()
    part[here.ahead] = back_input(here.ahead).astype(bf16)
    part[here.behind] = back_input(here.behind).astype(bf16)
    scatter.send_near()
    tgrad[...] = back_input(x)

    def qkv_grads(block, _):
        rows = a1[:, lanes(block, 384)].T
        for g in range(2):
            wqkv[g, block] = dot(rows, dproj[g]).astype(bf16).reshape(2, 2, 96, 384)
        return 0

    lax.fori_loop(0, 4, qkv_grads, 0)
    cores.append(links.start(wqkv.at[:, :, :, other], rc_q, here.twin))
    scatter.forward()

    for name in "dgu":
        advance(reduces[name])

    scatter_d.finish()
    for half, rows in enumerate((H0, H1)):
        mixed[rows] = middle[rows] + partd[x, rows].astype(f32) + scatter_d.received(half)

    arrive(cores[1:])
    for g in range(2):

        def core_heads(i, _, g=g):
            for j in range(2):
                value = wqkv[g, i, j, core].astype(f32) + rc_q[g, i, j].astype(f32)
                wqkv[g, i, j, core] = value.astype(bf16)
            return 0

        lax.fori_loop(0, 4, core_heads, 0)
    start_reduce("q")
    advance(reduces["o"])
    for name in "dgu":
        advance(reduces[name])

    arrive(inner_sums)
    inner = rows_to_column(jnp.sum(small[1], axis=0)[0:4])[:, 0:1]
    scatter.finish()
    for half, rows in enumerate((H0, H1)):
        da1 = tgrad[rows] + scatter.received(half)
        source, rinv = xf[rows, own].astype(f32), stats[rows][:, 4:5]
        gsum[0:1] = gsum[0:1] + jnp.sum(da1 * source, axis=0, keepdims=True)
        factor = inner[half * 256 : half * 256 + 256] * rinv * rinv * (1.0 / D)
        tgrad[rows] = dmid[rows] + gn[0, :, own] * da1 - source * factor
    dgain[0] = gsum[...]
    gain_y = [links.start(dgain.at[0], dgain.at[1 + j], here.ys[j]) for j in range(3)]

    for name in "dgu":
        advance(reduces[name])

    def hidden_blocks(target):
        return [
            (wg.at[target, zl, core, :, lanes(hid, 128)], fin_g.at[zl, core, :, lanes(x, 128)]),
            (wu.at[target, zl, core, :, lanes(hid, 128)], fin_u.at[zl, core, :, lanes(x, 128)]),
            (wd.at[zh, y, zl, core, :, lanes(target, 384)], fin_d.at[x, zl, core]),
        ]

    swaps = []
    for peer, target in ((here.right, here.ahead), (here.left, here.behind), (here.far, here.across)):
        swaps += [links.start(src, dst, peer) for src, dst in hidden_blocks(target)]
    swap_kept = [links.keep(src, dst) for src, dst in hidden_blocks(x)]

    for _ in range(2):
        advance(reduces["q"])
        advance(reduces["o"])

    for copy in swap_kept:
        copy.wait()
    arrive(swaps)
    fins = ((fin_g, 0), (fin_u, 0), (fin_d, 1))
    pick = lambda ref, lead, index: ref.at[(slice(None),) * lead + index]
    across_zl = [links.start(v, v, here.zs[0]) for v in (pick(ref, lead, (zl, core)) for ref, lead in fins)]

    arrive(gain_y)
    gsum[...] = dgain[0] + dgain[1] + dgain[2] + dgain[3]
    dgain[4] = gsum[...]
    gain_z = [links.start(dgain.at[4], dgain.at[5 + j], here.zs[j]) for j in range(3)]

    for _ in range(2):
        advance(reduces["q"])
    advance(reduces["o"])
    src_q, src_o = wqkv.at[zh, y, zl, core], wo.at[zh, x, zl, core, :, y_cols]
    dst_q, dst_o = fin_q.at[zl, core], fin_o.at[zl, core]
    mirror = [links.make(src_q, dst_q, here.mirror), links.make(src_o, dst_o, here.mirror)]
    first = links.local_count
    stay = [pltpu.make_async_copy(src_q, dst_q, local.at[first]), pltpu.make_async_copy(src_o, dst_o, local.at[first + 1])]

    @pl.when(x != y)
    def _():
        for copy in mirror:
            copy.start()
        for copy in mirror:
            copy.wait()

    @pl.when(x == y)
    def _():
        for copy in stay:
            copy.start()
        for copy in stay:
            copy.wait()

    head_zl = [links.start(v, v, here.zs[0]) for v in (fin_q.at[zl, core], fin_o.at[zl, core])]
    arrive(across_zl)
    to_core = [links.start(v, v, here.twin) for v in (pick(ref, lead, (slice(None), core)) for ref, lead in fins)]
    arrive(gain_z)
    gsum[...] = dgain[4] + dgain[5] + dgain[6] + dgain[7]
    dgain[8] = gsum[...]
    gain_c = links.start(dgain.at[8], dgain.at[9], here.twin)
    arrive(head_zl)
    head_core = [links.start(v, v, here.twin) for v in (fin_q.at[:, core], fin_o.at[:, core])]
    arrive([gain_c])
    arrive(to_core)
    arrive(head_core)
    links.close()


def outputs_kernel(mixed, tgrad, dgain, g_q, g_o, g_g, g_u, g_d, *outs):
    gains = dgain[8] + dgain[9]
    outs[0][...] = mixed[...]
    outs[1][...] = tgrad[...]
    outs[2][...] = gains[0:1]
    outs[5][...] = gains[1:2]
    for out, source in zip((outs[3], outs[4], outs[6], outs[7], outs[8]), (g_q, g_o, g_g, g_u, g_d)):
        out[...] = source[...].reshape(out.shape).astype(f32)


def run_layer(tokens, pos, gain_a, gain_f, qkvw, ow, gw, uw, dw, cot):
    s = jax.ShapeDtypeStruct
    v = pltpu.VMEM
    outs = [
        s((512, 384), f32),
        s((512, 384), f32),
        s((10, 8, 384), f32),
        s((2, 2, 96, 384), bf16),
        s((2, 2, 48, 384), bf16),
        s((2, 2, 96, 512), bf16),
        s((2, 2, 96, 512), bf16),
        s((4, 2, 2, 32, 384), bf16),
    ]
    scratch = [
        v((512, D), bf16),
        v((512, D), bf16),
        v((512, D), bf16),
        v((512, D), bf16),
        v((512, 128), f32),
        v((512, 1024), bf16),
        v((2, 512, 256), bf16),
        v((512, 512), bf16),
        v((512, 128), f32),
        v((512, 128), f32),
        v((512, 384), f32),
        v((2, 1, D), f32),
        v((4, 8, 128), i32),
        v((512, 384), bf16),
        v((2, 4, 2, 2, 96, 384), bf16),
        v((2, 4, 2, 2, 48, D), bf16),
        v((4, 2, 2, 96, 1024), bf16),
        v((4, 2, 2, 96, 1024), bf16),
        v((2, 4, 2, 2, 32, D), bf16),
        v((3, 512, 1024), bf16),
        v((4, 512, 384), bf16),
        v((4, 512, 384), bf16),
        v((3, 6, 256, 384), bf16),
        v((512, 128), f32),
        v((512, D), bf16),
        v((512, 384), f32),
        v((4, 512, 128), f32),
        v((4, 512, 128), f32),
        v((4, 512, 128), f32),
        v((2, 512, 256), bf16),
        v((2, 512, 384), bf16),
        v((2, 4, 8, 128), f32),
        v((512, 1), f32),
        v((8, 384), f32),
        v((4, 2, 96, 1024), bf16),
        v((4, 2, 96, 1024), bf16),
        v((2, 4, 2, 32, D), bf16),
        v((2, 4, 2, 96, 384), bf16),
        v((2, 2, 48, D), bf16),
        pltpu.SemaphoreType.DMA((270,)),
        pltpu.SemaphoreType.DMA((270,)),
        pltpu.SemaphoreType.DMA((20,)),
    ]
    scratch += [v(shape, bf16) for piece in slot_shapes() for step in piece for shape in step]
    return pl.pallas_call(
        layer_kernel,
        out_shape=outs,
        in_specs=[ANY] * 10 + [VM] * 3,
        out_specs=[VM] * len(outs),
        scratch_shapes=scratch,
        compiler_params=pltpu.CompilerParams(
            collective_id=0, has_side_effects=True, vmem_limit_bytes=63 * 1024 * 1024
        ),
        name="layer",
    )(tokens, pos, gain_a, gain_f, qkvw, ow, gw, uw, dw, cot, *constants())


def constants():
    half = HD // 2
    freq = np.zeros((8, 128), np.float32)
    rates = rope_base ** (-(np.arange(half) * 2.0 / HD))
    freq[:, :half] = rates
    freq[:, 64 : 64 + half] = rates
    perm = np.zeros((384, 512), np.float32)
    permo = np.zeros((512, 384), np.float32)
    for h in range(4):
        for d in range(HD):
            wide = d if (h == 3 or d < half) else d - half + 64
            perm[h * HD + d, h * 128 + wide] = 1
            permo[h * 128 + d, h * HD + d] = 1
    return jnp.asarray(freq), jnp.asarray(perm, bf16), jnp.asarray(permo, bf16)


def per_device(
    tokens,
    positions,
    attn_gain,
    qkv_weight,
    output_weight,
    ffn_gain,
    gate_weight,
    up_weight,
    down_weight,
    cotangent,
):
    parts = run_layer(
        tokens, positions.reshape(8, 128), attn_gain[None], ffn_gain[None], qkv_weight, output_weight,
        gate_weight, up_weight, down_weight, cotangent,
    )
    s = jax.ShapeDtypeStruct
    shapes = [(512, 384), (512, 384), (1, 384), (384, 384), (192, 384), (1, 384), (384, 512), (384, 512), (512, 384)]
    outs = pl.pallas_call(
        outputs_kernel,
        out_shape=[s(shape, f32) for shape in shapes],
        in_specs=[VM] * 8,
        out_specs=[VM] * 9,
        compiler_params=pltpu.CompilerParams(vmem_limit_bytes=32 * 1024 * 1024),
        name="outputs",
    )(*parts)
    return tuple(out.reshape(384) if out.shape == (1, 384) else out for out in outs)


def solution(mesh):
    finer = Mesh(mesh.devices.reshape(2, 2, 4, 2, 4), AXES)
    row = ("y", "zh")
    in_specs = (
        P(DP_ROW, "x"),
        P(("zl", "core", "x")),
        P("x"),
        P("x", row),
        P(row, "x"),
        P("x"),
        P("x", row),
        P("x", row),
        P(row, "x"),
        P(DP_ROW, "x"),
    )
    out_specs = (
        P(DP_ROW, "x"),
        P(DP_ROW, "x"),
        P("x"),
        P("x", row),
        P(row, "x"),
        P("x"),
        P("x", row),
        P("x", row),
        P(row, "x"),
    )
    return jax.shard_map(per_device, mesh=finer, in_specs=in_specs, out_specs=out_specs, check_vma=False)
```

```python
import functools
import math

import jax
import jax.numpy as jnp
import numpy as np
from jax import lax
from jax.experimental import pallas as pl
from jax.experimental.pallas import tpu as pltpu
from jax.sharding import Mesh
from jax.sharding import PartitionSpec as P

D = 1536
HD = 96
AXES = ("zl", "core", "y", "zh", "x")
DP_ROW = ("zl", "core", "y", "zh")
bf16 = jnp.bfloat16
f32 = jnp.float32
i32 = jnp.int32
MESH = pl.DeviceIdType.MESH
VM = pl.BlockSpec(memory_space=pltpu.VMEM)
ANY = pl.BlockSpec(memory_space=pl.ANY)

epsilon = 1e-05
rope_base = 100000.0
masked_score = -1e30
score_scale = math.log2(math.e) / math.sqrt(HD)
H0, H1 = pl.ds(0, 256), pl.ds(256, 256)


def dot(a, b):
    return lax.dot_general(a, b, (((1,), (0,)), ((), ())), preferred_element_type=f32)


def dot_t(a, b):
    return lax.dot_general(a, b, (((1,), (1,)), ((), ())), preferred_element_type=f32)


def lanes(index, width):
    return pl.ds(pl.multiple_of(index * width, 128), width)


class Place:
    def __init__(self):
        self.x, self.y = lax.axis_index("x"), lax.axis_index("y")
        self.zl, self.zh, self.core = lax.axis_index("zl"), lax.axis_index("zh"), lax.axis_index("core")
        self.quarter = self.zl * 2 + self.core
        self.ahead, self.behind, self.across = [(self.x + k) % 4 for k in (1, 3, 2)]
        self.right, self.left, self.far = {"x": self.ahead}, {"x": self.behind}, {"x": self.across}
        self.ys = [{"y": (self.y + k) % 4} for k in (1, 3, 2)]
        self.zs = [{"zl": 1 - self.zl}, {"zl": 1 - self.zl, "zh": 1 - self.zh}, {"zh": 1 - self.zh}]
        self.twin = {"core": 1 - self.core}
        self.mirror = {"x": self.y, "y": self.x}
        y, zl, zh = self.y, self.zl, self.zh
        beside, opposite = y + 1 - y % 2 * 2, 3 - y
        self.cube = {
            "ya": ({"y": beside}, (beside, zl, zh)),
            "yb": ({"y": opposite}, (opposite, zl, zh)),
            "za": ({"zl": 1 - zl}, (y, 1 - zl, zh)),
            "zb": ({"zl": 1 - zl, "zh": 1 - zh}, (y, 1 - zl, 1 - zh)),
        }

    def across_link(self, name):
        return self.cube[name]

    def enter(self):
        barrier = pltpu.get_barrier_semaphore()
        peers = [self.right, self.left, self.far, *self.ys, *self.zs, self.twin]
        for peer in peers:
            pl.semaphore_signal(barrier, inc=1, device_id=peer, device_id_type=MESH)

        @pl.when(self.x != self.y)
        def _():
            pl.semaphore_signal(barrier, inc=1, device_id=self.mirror, device_id_type=MESH)
            pl.semaphore_wait(barrier, len(peers) + 1)

        @pl.when(self.x == self.y)
        def _():
            pl.semaphore_wait(barrier, len(peers))


class Links:
    def __init__(self, send, recv, local):
        self.send, self.recv, self.local, self.count, self.local_count = send, recv, local, 0, 0
        self.open = []

    def make(self, src, dst, device):
        i = self.count
        self.count += 1
        return pltpu.make_async_remote_copy(
            src, dst, self.send.at[i], self.recv.at[i], device_id=device, device_id_type=MESH
        )

    def start(self, src, dst, device):
        copy = self.make(src, dst, device)
        copy.start()
        self.open.append(copy)
        return copy

    def spread(self, ref, devices):
        return [self.start(ref, ref, device) for device in devices]

    def keep(self, src, dst):
        copy = pltpu.make_async_copy(src, dst, self.local.at[self.local_count])
        self.local_count += 1
        copy.start()
        return copy

    def settle(self, copies):
        for copy in copies:
            copy.wait_send()
        self.open = [copy for copy in self.open if all(copy is not done for done in copies)]

    def close(self):
        self.settle(list(self.open))


def arrive(copies):
    for copy in copies:
        copy.wait_recv()


class RingGather:
    def __init__(self, links, here, src, buf):
        cols = lanes(here.x, 384)
        self.links, self.here, self.buf = links, here, buf
        self.first = [
            links.start(src(H0), buf.at[H0, cols], here.right),
            links.start(src(H1), buf.at[H1, cols], here.left),
        ]
        self.second = [
            links.start(src(H1), buf.at[H1, cols], here.right),
            links.start(src(H0), buf.at[H0, cols], here.left),
        ]

    def forward(self):
        here, buf = self.here, self.buf
        self.first[0].wait_recv()
        a = buf.at[H0, lanes(here.behind, 384)]
        self.third = [self.links.start(a, a, here.right)]
        self.first[1].wait_recv()
        b = buf.at[H1, lanes(here.ahead, 384)]
        self.third += [self.links.start(b, b, here.left)]

    def near(self):
        arrive(self.second)

    def finish(self):
        arrive(self.third)

    def settle(self):
        self.links.settle(self.first + self.second + self.third)


class RingScatter:
    def __init__(self, links, here, part, slots):
        self.links, self.here, self.part, self.slots = links, here, part, slots

    def send_far(self):
        h, p, s = self.here, self.part, self.slots
        self.r0 = self.links.start(p.at[h.across, H0], s.at[0], h.right)
        self.l0 = self.links.start(p.at[h.across, H1], s.at[1], h.left)

    def send_near(self):
        h, p, s = self.here, self.part, self.slots
        self.r1 = self.links.start(p.at[h.ahead, H1], s.at[2], h.right)
        self.l1 = self.links.start(p.at[h.behind, H0], s.at[3], h.left)

    def forward(self):
        h, p, s = self.here, self.part, self.slots
        self.r0.wait_recv()
        p[h.ahead, H0] = (p[h.ahead, H0].astype(f32) + s[0].astype(f32)).astype(bf16)
        self.r2 = self.links.start(p.at[h.ahead, H0], s.at[4], h.right)
        self.l0.wait_recv()
        p[h.behind, H1] = (p[h.behind, H1].astype(f32) + s[1].astype(f32)).astype(bf16)
        self.l2 = self.links.start(p.at[h.behind, H1], s.at[5], h.left)

    def finish(self):
        arrive([self.r1, self.l1, self.r2, self.l2])

    def settle(self):
        self.links.settle([self.r0, self.l0, self.r1, self.l1, self.r2, self.l2])

    def received(self, half):
        s = self.slots
        pair = (4, 3) if half == 0 else (2, 5)
        return s[pair[0]].astype(f32) + s[pair[1]].astype(f32)


ORDERS = (("ya", "yb", "za", "zb"), ("za", "zb", "ya", "yb"), ("yb", "ya", "zb", "za"), ("zb", "za", "yb", "ya"))


def part_of(order):
    y_state = {(): "own", ("ya",): "pair", ("yb",): "cross"}.get(tuple(d for d in order if d[0] == "y"), "all")
    z_state = {(): "own", ("za",): "low", ("zb",): "cross"}.get(tuple(d for d in order if d[0] == "z"), "all")
    return y_state, z_state


def y_cells(state, y):
    return {"own": [(y, 1)], "pair": [(y // 2 * 2, 2)], "cross": [(y, 1), (3 - y, 1)], "all": [(0, 4)]}[state]


def z_cells(state, zl, zh, joined):
    if state == "all" and not joined:
        return [(None, 0), (None, 1)]
    cells = {"own": [(zl, zh)], "low": [(None, zh)], "cross": [(zl, zh), (1 - zl, 1 - zh)], "all": [(None, None)]}
    return cells[state]


def either(index):
    return slice(None) if index is None else index


class UnitColumns:
    def __init__(self, core, start, size):
        self.core, self.start, self.size = core, start, size

    def cells(self, state, y, zl, zh):
        rows = pl.ds(self.start, self.size)
        return [
            (slice(None), either(l), self.core, rows, pl.ds(pl.multiple_of(h * 512 + first * 128, 128), count * 128))
            for l, h in z_cells(state[1], zl, zh, False)
            for first, count in y_cells(state[0], y)
        ]

    def shapes(self, state):
        return [
            (4,) + ((2,) if l is None else ()) + (self.size, count * 128)
            for l, _ in z_cells(state[1], 0, 0, False)
            for _, count in y_cells(state[0], 0)
        ]


class Blocks:
    def __init__(self, core, start, size, width):
        self.core, self.start, self.size, self.width = core, start, size, width

    def cells(self, state, y, zl, zh):
        rows = pl.ds(self.start, self.size)
        pick = lambda first, count: first if count == 1 else (slice(None) if count == 4 else pl.ds(first, count))
        return [
            (either(h), pick(first, count), either(l), self.core, rows)
            for l, h in z_cells(state[1], zl, zh, True)
            for first, count in y_cells(state[0], y)
        ]

    def shapes(self, state):
        return [
            ((2,) if h is None else ()) + ((count,) if count > 1 else ()) + ((2,) if l is None else ()) + (self.size, self.width)
            for l, h in z_cells(state[1], 0, 0, True)
            for _, count in y_cells(state[0], 0)
        ]


class OutputRows:
    def __init__(self, core, start, size, place):
        self.core, self.start, self.size, self.place = core, start, size, place

    def cells(self, state, y, zl, zh):
        rows = pl.ds(self.start, self.size)
        return [
            (either(h), self.place, either(l), self.core, rows, pl.ds(pl.multiple_of(first * 384, 128), count * 384))
            for l, h in z_cells(state[1], zl, zh, True)
            for first, count in y_cells(state[0], y)
        ]

    def shapes(self, state):
        return [
            ((2,) if h is None else ()) + ((2,) if l is None else ()) + (self.size, count * 384)
            for l, h in z_cells(state[1], 0, 0, True)
            for _, count in y_cells(state[0], 0)
        ]


class CubeGather:
    def __init__(self, links, here, ref, layout, order):
        self.links, self.here, self.ref, self.layout, self.order, self.step = links, here, ref, layout, order, 0
        self.launch()

    def launch(self):
        here, ref = self.here, self.ref
        device, _ = here.across_link(self.order[self.step])
        cells = self.layout.cells(part_of(self.order[: self.step]), here.y, here.zl, here.zh)
        self.copies = [self.links.start(ref.at[cell], ref.at[cell], device) for cell in cells]

    def advance(self):
        arrive(self.copies)
        self.step += 1
        if self.step < 4:
            self.launch()


class CubeReduce:
    def __init__(self, links, here, ref, layout, order, slots):
        self.links, self.here, self.ref, self.layout, self.order, self.step = links, here, ref, layout, order, 3
        self.slots = slots
        self.launch()

    def launch(self):
        here, ref = self.here, self.ref
        device, coordinates = here.across_link(self.order[self.step])
        cells = self.layout.cells(part_of(self.order[: self.step]), *coordinates)
        pairs = zip(cells, self.slots[self.step])
        self.copies = [self.links.start(ref.at[cell], slot, device) for cell, slot in pairs]

    def advance(self):
        here, ref = self.here, self.ref
        arrive(self.copies)
        cells = self.layout.cells(part_of(self.order[: self.step]), here.y, here.zl, here.zh)
        for cell, slot in zip(cells, self.slots[self.step]):
            ref[cell] = (ref[cell].astype(f32) + slot[...].astype(f32)).astype(bf16)
        self.step -= 1
        if self.step >= 0:
            self.launch()


def advance(cubes):
    for cube in cubes:
        cube.advance()


def grad_layouts(core, place):
    return [
        ("d", Blocks(core, 0, 16, D), 0),
        ("d", Blocks(core, 16, 16, D), 3),
        ("g", UnitColumns(core, 0, 48), 0),
        ("g", UnitColumns(core, 48, 48), 1),
        ("u", UnitColumns(core, 0, 48), 2),
        ("u", UnitColumns(core, 48, 48), 3),
        ("o", OutputRows(core, 0, 16, place), 1),
        ("o", OutputRows(core, 16, 16, place), 2),
        ("o", OutputRows(core, 32, 16, place), 3),
        ("q", Blocks(core, 0, 32, 384), 0),
        ("q", Blocks(core, 32, 32, 384), 1),
        ("q", Blocks(core, 64, 16, 384), 2),
        ("q", Blocks(core, 80, 16, 384), 3),
    ]


def slot_shapes():
    return [
        [layout.shapes(part_of(ORDERS[order][:step])) for step in range(4)] for _, layout, order in grad_layouts(0, 0)
    ]


def sine_cosine(angle):
    turns = jnp.floor(angle * (1.0 / (2.0 * math.pi)) + 0.5)
    r = angle - turns * 6.28125
    r = r - turns * 0.0019350051879882812
    r = r - turns * 3.0199159819185874e-07
    t = r * 0.5
    t2 = t * t
    s = 1.0 / 6227020800.0
    for c in (-1.0 / 39916800, 1.0 / 362880, -1.0 / 5040, 1.0 / 120, -1.0 / 6, 1.0):
        s = s * t2 + c
    s = s * t
    c_ = 1.0 / 479001600.0
    for c in (-1.0 / 3628800, 1.0 / 40320, -1.0 / 720, 1.0 / 24, -0.5, 1.0):
        c_ = c_ * t2 + c
    return 2.0 * s * c_, 1.0 - 2.0 * s * s


def causal(scores):
    last = scores[:, -256:]
    seen = lax.broadcasted_iota(i32, (256, 256), 1) <= lax.broadcasted_iota(i32, (256, 256), 0)
    last = jnp.where(seen, last, masked_score)
    return last if scores.shape[1] == 256 else jnp.concatenate([scores[:, :-256], last], axis=1)


def turn(head, cosine, sine):
    return head * cosine + pltpu.roll(head, 64, 1) * sine


def dot_first(a, b):
    return lax.dot_general(a, b, (((0,), (0,)), ((), ())), preferred_element_type=f32)


def column_to_rows(column, ref):
    for c in range(4):
        block = jnp.broadcast_to(column[c * 128 : c * 128 + 128], (128, 128)).T
        ref[c : c + 1] = block[0:1]


def rows_to_column(rows):
    return jnp.concatenate([jnp.broadcast_to(rows[c : c + 1], (128, 128)).T for c in range(4)], 0)


def layer_kernel(
    tokens, pos, gain_a, gain_f, qkvw, ow, gw, uw, dw, cot, freq, perm, permo,
    mixed, tgrad, dgain, fin_q, fin_o, fin_g, fin_u, fin_d,
    xf, a1, a2, cotf, stats, qkv, kvr, att, cosb, sinb, middle, gn, posb, packed,
    wqkv, wo, wg, wu, wd, hdd, part, partd, slots, wide, dzf, dmid,
    dq, dkv, dkr, dkin, dproj, small, sums, gsum, rc_g, rc_u, rc_d, rc_q, rc_o,
    send, recv, local, *slot_refs,
):
    here = Place()
    links = Links(send, recv, local)
    x, y, zl, zh, core, quarter = here.x, here.y, here.zl, here.zh, here.core, here.quarter
    hid = zh * 4 + y
    other = 1 - core
    own, y_cols = lanes(x, 384), lanes(y, 384)
    a, b, da, db, oa, ob = pl.ds(0, 48), pl.ds(48, 48), pl.ds(0, 16), pl.ds(16, 16), pl.ds(0, 32), pl.ds(32, 16)
    refs = iter(slot_refs)
    layouts = [
        (name, layout, ORDERS[order], [[next(refs) for _ in shapes] for shapes in steps])
        for (name, layout, order), steps in zip(grad_layouts(core, x), slot_shapes())
    ]
    x_peers = (here.right, here.left, here.far)
    here.enter()

    own_qkv, src_qkv = wqkv.at[zh, x, zl, core], qkvw.at[pl.ds(quarter * 96, 96)]
    own_o, src_o = wo.at[zh, y, zl, core, :, own], ow.at[pl.ds(quarter * 48, 48)]
    mirror = [links.make(src_qkv, own_qkv, here.mirror)]
    stay = [pltpu.make_async_copy(src_qkv, own_qkv, local.at[0])]
    links.local_count = 2

    @pl.when(x != y)
    def _():
        for copy in mirror:
            copy.start()

    @pl.when(x == y)
    def _():
        for copy in stay:
            copy.start()

    def hidden_slices(target):
        rows = pl.ds(quarter * 96, 96)
        return [
            (gw.at[rows, lanes(target, 128)], wg.at[x, zl, core, :, lanes(hid, 128)]),
            (uw.at[rows, lanes(target, 128)], wu.at[x, zl, core, :, lanes(hid, 128)]),
            (dw.at[pl.ds(target * 128 + quarter * 32, 32)], wd.at[zh, y, zl, core, :, own]),
        ]

    swaps = []
    for peer, target in ((here.right, here.ahead), (here.left, here.behind), (here.far, here.across)):
        swaps += [links.start(src, dst, peer) for src, dst in hidden_slices(target)]
    swap_kept = [links.keep(src, dst) for src, dst in hidden_slices(x)]
    swaps_o = [links.start(src_o, own_o, peer) for peer in x_peers]
    swap_kept_o = links.keep(src_o, own_o)

    ring_x = RingGather(links, here, lambda half: tokens.at[half], xf)
    kept = [links.keep(tokens, xf.at[:, own])]
    small_sends = []
    for peer in x_peers:
        small_sends.append(links.start(pos, posb.at[x], peer))
        small_sends.append(links.start(gain_a, gn.at[0, :, own], peer))
        small_sends.append(links.start(gain_f, gn.at[1, :, own], peer))
    kept += [links.keep(pos, posb.at[x]), links.keep(gain_a, gn.at[0, :, own]), links.keep(gain_f, gn.at[1, :, own])]

    @pl.when(x != y)
    def _():
        for copy in mirror:
            copy.wait()

    @pl.when(x == y)
    def _():
        for copy in stay:
            copy.wait()

    pieces = ((0, 32), (32, 32), (64, 16), (80, 16))
    cube_q = [
        CubeGather(links, here, wqkv, Blocks(core, start, size, 384), ORDERS[k]) for k, (start, size) in enumerate(pieces)
    ]
    advance(cube_q)
    for copy in swap_kept:
        copy.wait()
    arrive(swaps)
    cube_g = [CubeGather(links, here, wg, UnitColumns(core, 48 * k, 48), ORDERS[k]) for k in range(2)]
    cube_u = [CubeGather(links, here, wu, UnitColumns(core, 48 * k, 48), ORDERS[2 + k]) for k in range(2)]
    cube_d = [CubeGather(links, here, wd, Blocks(core, 16 * k, 16, D), ORDERS[3 * k]) for k in range(2)]
    ring_x.forward()
    advance(cube_q)
    swap_kept_o.wait()
    arrive(swaps_o)
    cube_o = [CubeGather(links, here, wo, Blocks(core, 16 * k, 16, D), ORDERS[1 + k]) for k in range(3)]
    advance(cube_g)
    advance(cube_u)
    advance(cube_d)
    advance(cube_q)
    advance(cube_o)

    for copy in kept:
        copy.wait()
    arrive(small_sends)
    mine = posb[y]
    mine = jnp.where(zh == 0, mine[0:4], mine[4:8]).astype(f32)
    lane = lax.broadcasted_iota(i32, (128, 128), 1)
    for c in range(4):
        column = jnp.broadcast_to(mine[c : c + 1], (128, 128)).T
        sine, cosine = sine_cosine(column * freq[0:1])
        cosb[pl.ds(c * 128, 128)] = cosine
        sinb[pl.ds(c * 128, 128)] = jnp.where(lane < 64, -sine, sine)

    ring_x.near()
    ring_x.finish()
    ring_c = RingGather(links, here, lambda half: cot.at[half], cotf)
    cot_kept = links.keep(cot, cotf.at[:, own])

    def norm_tokens(i, _):
        rows = pl.ds(pl.multiple_of(i * 64, 64), 64)
        value = xf[rows].astype(f32)
        inverse = lax.rsqrt(jnp.sum(value * value, axis=1, keepdims=True) * (1.0 / D) + epsilon)
        a1[rows] = (value * gn[0]).astype(bf16)
        stats[rows] = jnp.broadcast_to(inverse, (64, 128))
        return 0

    lax.fori_loop(0, 8, norm_tokens, 0)

    advance(cube_q)
    core_qkv = links.spread(wqkv.at[:, :, :, core], [here.twin])
    advance(cube_g)
    advance(cube_u)
    advance(cube_d)
    advance(cube_o)

    arrive(core_qkv)

    def widen(i, _):
        w = wqkv[i].reshape(D, 384)
        for j in range(3):
            hdd[j, :, lanes(i, 512)] = dot(w[j * 512 : j * 512 + 512], perm[...]).astype(bf16)
        return 0

    lax.fori_loop(0, 2, widen, 0)

    def keys_values(g, _):
        pair = dot(a1[...], hdd[:, :, lanes(g * 2 + 1, 256)].reshape(D, 256))
        inverse = stats[...]
        qkv[:, lanes(g * 4 + 2, 128)] = turn(pair[:, :128] * inverse, cosb[...], sinb[...]).astype(bf16)
        qkv[:, lanes(g * 4 + 3, 128)] = (pair[:, 128:] * inverse).astype(bf16)
        return 0

    lax.fori_loop(0, 2, keys_values, 0)
    over = [links.make(qkv.at[:, pl.ds(g * 512 + 256, 256)], kvr.at[g], here.zs[2]) for g in range(2)]

    @pl.when(zh == 0)
    def _():
        for copy in over:
            copy.start()

    advance(cube_g)
    advance(cube_u)
    advance(cube_d)
    advance(cube_o)

    def queries(g, _):
        pair = dot(a1[...], hdd[:, :, lanes(g * 2, 256)].reshape(D, 256))
        inverse = stats[...]
        for h in range(2):
            head = pair[:, h * 128 : h * 128 + 128] * inverse
            qkv[:, lanes(g * 4 + h, 128)] = (turn(head, cosb[...], sinb[...]) * score_scale).astype(bf16)
        return 0

    lax.fori_loop(0, 2, queries, 0)
    ring_c.forward()

    def own_scores(i, _):
        g = i // 2
        for qb in range(2):
            rows, keys = pl.ds(qb * 256, 256), pl.ds(0, qb * 256 + 256)
            q = qkv[rows, lanes(g * 4 + i % 2, 128)]
            s = causal(dot_t(q, qkv[keys, lanes(g * 4 + 2, 128)]))
            m = jnp.max(s, axis=1, keepdims=True)
            e = jnp.exp2(s - m)
            dq[i, rows] = dot(e.astype(bf16), qkv[keys, lanes(g * 4 + 3, 128)])
            dkv[i, rows] = jnp.broadcast_to(m, (256, 128))
            dkr[i, rows] = jnp.broadcast_to(jnp.sum(e, axis=1, keepdims=True), (256, 128))
        return 0

    lax.fori_loop(0, 4, own_scores, 0)

    @pl.when(zh == 1)
    def _():
        for copy in over:
            copy.wait_recv()

        def first_scores(i, _):
            g = i // 2
            for qb in range(2):
                rows = pl.ds(qb * 256, 256)
                q = qkv[rows, lanes(g * 4 + i % 2, 128)]
                s = dot_t(q, kvr[g, :, 0:128])
                old = dkv[i, rows][:, 0:1]
                m = jnp.maximum(old, jnp.max(s, axis=1, keepdims=True))
                e = jnp.exp2(s - m)
                shrink = jnp.exp2(old - m)
                dq[i, rows] = dq[i, rows] * shrink + dot(e.astype(bf16), kvr[g, :, 128:256])
                dkr[i, rows] = dkr[i, rows] * shrink + jnp.sum(e, axis=1, keepdims=True)
                dkv[i, rows] = jnp.broadcast_to(m, (256, 128))
            return 0

        lax.fori_loop(0, 4, first_scores, 0)

    @pl.when(zh == 0)
    def _():
        for copy in over:
            copy.wait_send()

    advance(cube_o)
    core_o = links.spread(wo.at[:, :, :, core], [here.twin])
    lane = lax.broadcasted_iota(i32, (512, 128), 1)
    for i in range(4):
        att[:, i * 128 : i * 128 + 128] = (dq[i] / dkr[i]).astype(bf16)
        stats[...] = jnp.where(lane == i, dkv[i] + jnp.log2(dkr[i]), stats[...])

    packed[...] = dot(att[...], permo[...]).astype(bf16)
    ring_a = RingGather(links, here, lambda half: packed.at[half], dzf)
    dzf[:, own] = packed[...]
    thirds = (dq, dkv, dkr)

    def output_part(block, c):
        return dot(dzf[:, lanes(block, 384)], wo[:, block, :, :, :, lanes(c, 384)].reshape(384, 384))

    def output_first(c, _):
        value = xf[:, lanes(c, 384)].astype(f32) + output_part(x, c)
        for k, ref in enumerate(thirds):
            ref[c] = value[:, k * 128 : k * 128 + 128]
        return 0

    def output_near(c, _):
        value = output_part(here.ahead, c) + output_part(here.behind, c)
        for k, ref in enumerate(thirds):
            ref[c] = ref[c] + value[:, k * 128 : k * 128 + 128]
        return 0

    def output_last(c, _):
        value = output_part(here.across, c)
        for k, ref in enumerate(thirds):
            m = ref[c] + value[:, k * 128 : k * 128 + 128]
            ref[c] = m
            a2[:, lanes(c * 3 + k, 128)] = (m * gn[1, :, lanes(c * 3 + k, 128)]).astype(bf16)
            sums[...] = sums[...] + jnp.sum(m * m, axis=1, keepdims=True)
        return 0

    arrive(core_o)
    lax.fori_loop(0, 4, output_first, 0)
    ring_a.forward()
    advance(cube_g)
    cores = [links.start(wg.at[:, :, core], wg.at[:, :, core], here.twin)]
    advance(cube_u)
    cores.append(links.start(wu.at[:, :, core], wu.at[:, :, core], here.twin))
    advance(cube_d)
    cores.append(links.start(wd.at[:, :, :, core], wd.at[:, :, :, core], here.twin))
    ring_a.near()
    lax.fori_loop(0, 4, output_near, 0)
    cot_kept.wait()
    ring_c.near()
    ring_c.finish()
    sums[...] = jnp.zeros_like(sums)
    ring_a.finish()
    lax.fori_loop(0, 4, output_last, 0)
    wide[...] = jnp.broadcast_to(lax.rsqrt(sums[...] * (1.0 / D) + epsilon), (512, 128))
    for k, ref in enumerate(thirds):
        middle[:, k * 128 : k * 128 + 128] = ref[x]
    links.close()
    arrive(cores)

    sums[...] = jnp.zeros_like(sums)

    def units(n, _):
        cols = lanes(n, 256)
        w_g = wg[:, :, :, :, cols].reshape(D, 256)
        w_u = wu[:, :, :, :, cols].reshape(D, 256)
        w_d = wd[n // 2, pl.ds((n % 2) * 2, 2)].reshape(256, D)
        for rows in (H0, H1):
            inverse = wide[rows][:, 0:1]
            gate = dot(a2[rows], w_g) * inverse
            up = dot(a2[rows], w_u) * inverse
            dh = dot_t(cotf[rows], w_d)
            sg = 1.0 / (1.0 + jnp.exp(-gate))
            silu = gate * sg
            dg = dh * up * (sg + silu * (1.0 - sg))
            du = dh * silu
            hdd[0, rows, cols] = (silu * up).astype(bf16)
            hdd[1, rows, cols] = (dg * inverse).astype(bf16)
            hdd[2, rows, cols] = (du * inverse).astype(bf16)
            inner = jnp.sum(dg * gate + du * up, axis=1, keepdims=True)
            sums[rows] = sums[rows] + inner
        return 0

    lax.fori_loop(0, 4, units, 0)

    def back_block(block):
        return dot_t(hdd[1], wg[block].reshape(384, 1024)) + dot_t(hdd[2], wu[block].reshape(384, 1024))

    scatter = RingScatter(links, here, part, slots.at[0])
    part[here.across] = back_block(here.across).astype(bf16)
    scatter.send_far()
    part[here.ahead] = back_block(here.ahead).astype(bf16)
    part[here.behind] = back_block(here.behind).astype(bf16)
    scatter.send_near()
    column_to_rows(sums[...], small.at[0, x])
    inner_sums = [links.start(small.at[0, x], small.at[0, x], p) for p in x_peers]
    dmid[...] = back_block(x)
    scatter.forward()

    def down_block(block, _):
        cols = lanes(block, 384)
        partd[block] = dot(hdd[0], wd[:, :, :, :, :, cols].reshape(1024, 384)).astype(bf16)
        return 0

    lax.fori_loop(0, 4, down_block, 0)

    def down_grad(n, _):
        rows = hdd[0, :, lanes(n, 256)].T
        for c in range(3):
            cols = pl.ds(c * 512, 512)
            value = dot(rows, cotf[:, cols]).astype(bf16)
            wd[n // 2, pl.ds((n % 2) * 2, 2), :, :, :, cols] = value.reshape(2, 2, 2, 32, 512)
        return 0

    lax.fori_loop(0, 4, down_grad, 0)
    cores = [links.start(wd.at[:, :, :, other], rc_d, here.twin)]

    def up_grads(block, _):
        rows = a2[:, lanes(block, 384)].T
        for source, target in ((1, wg), (2, wu)):
            for c in range(2):
                cols = pl.ds(c * 512, 512)
                target[block, :, :, :, cols] = dot(rows, hdd[source, :, cols]).astype(bf16).reshape(2, 2, 96, 512)
        return 0

    lax.fori_loop(0, 4, up_grads, 0)
    cores.append(links.start(wg.at[:, :, other], rc_g, here.twin))
    cores.append(links.start(wu.at[:, :, other], rc_u, here.twin))

    buffers = {"d": wd, "g": wg, "u": wu, "o": wo, "q": wqkv}
    reduces = {}

    def start_reduce(name):
        reduces[name] = [
            CubeReduce(links, here, buffers[name], layout, order, slots_)
            for piece, layout, order, slots_ in layouts
            if piece == name
        ]

    def core_sum_down(i, _):
        for k in range(2):
            for j in range(2):
                value = wd[k, i, j, core].astype(f32) + rc_d[k, i, j].astype(f32)
                wd[k, i, j, core] = value.astype(bf16)
        return 0

    arrive(cores[0:1])
    lax.fori_loop(0, 4, core_sum_down, 0)
    start_reduce("d")

    arrive(inner_sums)
    inner = rows_to_column(jnp.sum(small[0], axis=0)[0:4])[:, 0:1]
    scatter.finish()
    gsum[...] = jnp.zeros_like(gsum)
    for half, rows in enumerate((H0, H1)):
        da2 = dmid[rows] + scatter.received(half)
        m, inverse = middle[rows], wide[rows][:, 0:1]
        gsum[1:2] = gsum[1:2] + jnp.sum(da2 * m, axis=0, keepdims=True)
        factor = inner[half * 256 : half * 256 + 256] * inverse * inverse * (1.0 / D)
        value = cotf[rows, own].astype(f32) + gn[1, :, own] * da2 - m * factor
        dmid[rows] = value
        dzf[rows, own] = value.astype(bf16)
    ring_z = RingGather(links, here, lambda half: dzf.at[half, own], dzf)
    ring_z.forward()

    for matrix, (name, source) in enumerate((("g", rc_g), ("u", rc_u))):
        arrive(cores[matrix + 1 : matrix + 2])

        def core_sum(i, _, target=buffers[name], source=source):
            for j in range(2):
                target[i, j, core] = (target[i, j, core].astype(f32) + source[i, j].astype(f32)).astype(bf16)
            return 0

        lax.fori_loop(0, 4, core_sum, 0)
        start_reduce(name)

    ring_z.near()
    ring_z.finish()

    scatter_d = RingScatter(links, here, partd, slots.at[1])
    scatter_d.send_far()
    scatter_d.send_near()

    packed[...] = dot_t(dzf[...], wo[:, x].reshape(384, D)).astype(bf16)
    hdd[1, :, 0:512] = dot_t(packed[...], permo[...]).astype(bf16)
    packed[...] = dot(att[...], permo[...]).astype(bf16)
    for c in range(3):
        cols = pl.ds(c * 512, 512)
        value = dot_first(packed[...], dzf[:, cols]).astype(bf16)
        wo[:, x, :, :, :, cols] = value.reshape(2, 2, 2, 48, 512)
    cores = [links.start(wo.at[:, x, :, other], rc_o, here.twin)]

    dq[...] = jnp.zeros_like(dq)
    dkv[...] = jnp.zeros_like(dkv)

    def pair(i, rows, k, v, masked):
        g = i // 2
        head = lanes(i, 128)
        q, grad = qkv[rows, lanes(g * 4 + i % 2, 128)], hdd[1, rows, head]
        delta = jnp.sum(grad.astype(f32) * att[rows, head].astype(f32), axis=1, keepdims=True)
        lane = lax.broadcasted_iota(i32, (256, 128), 1)
        lse = jnp.sum(jnp.where(lane == i, stats[rows], 0.0), axis=1, keepdims=True)
        s = dot_t(q, k)
        if masked:
            s = causal(s)
        p = jnp.exp2(s - lse)
        ds = (p * (dot_t(grad, v) - delta)).astype(bf16)
        dq[i, rows] = dq[i, rows] + dot(ds, k)
        return dot_first(ds, q), dot_first(p.astype(bf16), grad)

    give = [links.make(kvr.at[g], dkin.at[g], here.zs[2]) for g in range(2)]

    @pl.when(zh == 1)
    def _():
        dkr[...] = jnp.zeros_like(dkr)

        def first_half(i, _):
            g = i // 2
            for qb in range(2):
                dk, dv = pair(i, pl.ds(qb * 256, 256), kvr[g, :, 0:128], kvr[g, :, 128:256], False)
                dkr[2 * g] = dkr[2 * g] + dk
                dkr[2 * g + 1] = dkr[2 * g + 1] + dv
            return 0

        for g in range(2):
            lax.fori_loop(2 * g, 2 * g + 2, first_half, 0)
            kvr[g, :, 0:128] = dkr[2 * g].astype(bf16)
            kvr[g, :, 128:256] = dkr[2 * g + 1].astype(bf16)
            give[g].start()

    scatter_d.forward()

    def own_keys(i, _):
        g = i // 2
        for qb in range(2):
            keys = pl.ds(0, qb * 256 + 256)
            k, v = qkv[keys, lanes(g * 4 + 2, 128)], qkv[keys, lanes(g * 4 + 3, 128)]
            dk, dv = pair(i, pl.ds(qb * 256, 256), k, v, True)
            dkv[2 * g, keys] = dkv[2 * g, keys] + dk
            dkv[2 * g + 1, keys] = dkv[2 * g + 1, keys] + dv
        return 0

    lax.fori_loop(0, 4, own_keys, 0)

    @pl.when(zh == 0)
    def _():
        for g in range(2):
            give[g].wait_recv()
            dkv[2 * g] = dkv[2 * g] + dkin[g, :, 0:128].astype(f32)
            dkv[2 * g + 1] = dkv[2 * g + 1] + dkin[g, :, 128:256].astype(f32)

    @pl.when(zh == 1)
    def _():
        for g in range(2):
            give[g].wait_send()

    for name in "dgu":
        advance(reduces[name])
    arrive(cores)
    for g in range(2):
        for j in range(2):
            wo[g, x, j, core] = (wo[g, x, j, core].astype(f32) + rc_o[g, j].astype(f32)).astype(bf16)
    start_reduce("o")

    sums[...] = jnp.zeros_like(sums)
    inverse = stats[:, 4:5]
    for i in range(8):
        cols = pl.ds(i * 128, 128)
        g, place = i // 4, i % 4
        value = dq[2 * g + place] if place < 2 else dkv[2 * g + place - 2]
        if place == 2:
            value = value * math.log(2.0)
        inside = jnp.sum(value * qkv[:, cols].astype(f32), axis=1, keepdims=True)
        if place < 2:
            inside = inside * math.log(2.0)
            value = value * (1.0 / math.sqrt(HD))
        sums[...] = sums[...] + inside
        if place < 3:
            value = turn(value, cosb[...], -sinb[...])
        hdd[0, :, cols] = (value * inverse).astype(bf16)
    column_to_rows(sums[...], small.at[1, x])
    inner_sums = [links.start(small.at[1, x], small.at[1, x], p) for p in x_peers]
    for g in range(2):
        dproj[g] = dot_t(hdd[0, :, g * 512 : g * 512 + 512], perm[...]).astype(bf16)

    def back_input(block):
        return sum(dot_t(dproj[g], wqkv[g, block].reshape(384, 384)) for g in range(2))

    scatter.settle()
    scatter = RingScatter(links, here, part, slots.at[2])
    part[here.across] = back_input(here.across).astype(bf16)
    scatter.send_far()
    part[here.ahead] = back_input(here.ahead).astype(bf16)
    part[here.behind] = back_input(here.behind).astype(bf16)
    scatter.send_near()
    tgrad[...] = back_input(x)

    def qkv_grads(block, _):
        rows = a1[:, lanes(block, 384)].T
        for g in range(2):
            wqkv[g, block] = dot(rows, dproj[g]).astype(bf16).reshape(2, 2, 96, 384)
        return 0

    lax.fori_loop(0, 4, qkv_grads, 0)
    cores.append(links.start(wqkv.at[:, :, :, other], rc_q, here.twin))
    scatter.forward()

    for name in "dgu":
        advance(reduces[name])

    scatter_d.finish()
    for half, rows in enumerate((H0, H1)):
        mixed[rows] = middle[rows] + partd[x, rows].astype(f32) + scatter_d.received(half)

    arrive(cores[1:])
    for g in range(2):

        def core_heads(i, _, g=g):
            for j in range(2):
                value = wqkv[g, i, j, core].astype(f32) + rc_q[g, i, j].astype(f32)
                wqkv[g, i, j, core] = value.astype(bf16)
            return 0

        lax.fori_loop(0, 4, core_heads, 0)
    start_reduce("q")
    advance(reduces["o"])
    for name in "dgu":
        advance(reduces[name])

    arrive(inner_sums)
    inner = rows_to_column(jnp.sum(small[1], axis=0)[0:4])[:, 0:1]
    scatter.finish()
    for half, rows in enumerate((H0, H1)):
        da1 = tgrad[rows] + scatter.received(half)
        source, rinv = xf[rows, own].astype(f32), stats[rows][:, 4:5]
        gsum[0:1] = gsum[0:1] + jnp.sum(da1 * source, axis=0, keepdims=True)
        factor = inner[half * 256 : half * 256 + 256] * rinv * rinv * (1.0 / D)
        tgrad[rows] = dmid[rows] + gn[0, :, own] * da1 - source * factor
    dgain[0] = gsum[...]
    gain_y = [links.start(dgain.at[0], dgain.at[1 + j], here.ys[j]) for j in range(3)]

    for name in "dgu":
        advance(reduces[name])

    def hidden_blocks(target):
        return [
            (wg.at[target, zl, core, :, lanes(hid, 128)], fin_g.at[zl, core, :, lanes(x, 128)]),
            (wu.at[target, zl, core, :, lanes(hid, 128)], fin_u.at[zl, core, :, lanes(x, 128)]),
            (wd.at[zh, y, zl, core, :, lanes(target, 384)], fin_d.at[x, zl, core]),
        ]

    swaps = []
    for peer, target in ((here.right, here.ahead), (here.left, here.behind), (here.far, here.across)):
        swaps += [links.start(src, dst, peer) for src, dst in hidden_blocks(target)]
    swap_kept = [links.keep(src, dst) for src, dst in hidden_blocks(x)]

    for _ in range(2):
        advance(reduces["q"])
        advance(reduces["o"])

    for copy in swap_kept:
        copy.wait()
    arrive(swaps)
    fins = ((fin_g, 0), (fin_u, 0), (fin_d, 1))
    pick = lambda ref, lead, index: ref.at[(slice(None),) * lead + index]
    across_zl = [links.start(v, v, here.zs[0]) for v in (pick(ref, lead, (zl, core)) for ref, lead in fins)]

    arrive(gain_y)
    gsum[...] = dgain[0] + dgain[1] + dgain[2] + dgain[3]
    dgain[4] = gsum[...]
    gain_z = [links.start(dgain.at[4], dgain.at[5 + j], here.zs[j]) for j in range(3)]

    for _ in range(2):
        advance(reduces["q"])
    advance(reduces["o"])
    src_q, src_o = wqkv.at[zh, y, zl, core], wo.at[zh, x, zl, core, :, y_cols]
    dst_q, dst_o = fin_q.at[zl, core], fin_o.at[zl, core]
    mirror = [links.make(src_q, dst_q, here.mirror), links.make(src_o, dst_o, here.mirror)]
    first = links.local_count
    stay = [pltpu.make_async_copy(src_q, dst_q, local.at[first]), pltpu.make_async_copy(src_o, dst_o, local.at[first + 1])]

    @pl.when(x != y)
    def _():
        for copy in mirror:
            copy.start()
        for copy in mirror:
            copy.wait()

    @pl.when(x == y)
    def _():
        for copy in stay:
            copy.start()
        for copy in stay:
            copy.wait()

    head_zl = [links.start(v, v, here.zs[0]) for v in (fin_q.at[zl, core], fin_o.at[zl, core])]
    arrive(across_zl)
    to_core = [links.start(v, v, here.twin) for v in (pick(ref, lead, (slice(None), core)) for ref, lead in fins)]
    arrive(gain_z)
    gsum[...] = dgain[4] + dgain[5] + dgain[6] + dgain[7]
    dgain[8] = gsum[...]
    gain_c = links.start(dgain.at[8], dgain.at[9], here.twin)
    arrive(head_zl)
    head_core = [links.start(v, v, here.twin) for v in (fin_q.at[:, core], fin_o.at[:, core])]
    arrive([gain_c])
    arrive(to_core)
    arrive(head_core)
    links.close()


def outputs_kernel(mixed, tgrad, dgain, g_q, g_o, g_g, g_u, g_d, *outs):
    gains = dgain[8] + dgain[9]
    outs[0][...] = mixed[...]
    outs[1][...] = tgrad[...]
    outs[2][...] = gains[0]
    outs[5][...] = gains[1]
    for out, source in zip((outs[3], outs[4], outs[6], outs[7], outs[8]), (g_q, g_o, g_g, g_u, g_d)):
        out[...] = source[...].reshape(out.shape).astype(f32)


def run_layer(tokens, pos, gain_a, gain_f, qkvw, ow, gw, uw, dw, cot):
    s = jax.ShapeDtypeStruct
    v = pltpu.VMEM
    outs = [
        s((512, 384), f32),
        s((512, 384), f32),
        s((10, 8, 384), f32),
        s((2, 2, 96, 384), bf16),
        s((2, 2, 48, 384), bf16),
        s((2, 2, 96, 512), bf16),
        s((2, 2, 96, 512), bf16),
        s((4, 2, 2, 32, 384), bf16),
    ]
    scratch = [
        v((512, D), bf16),
        v((512, D), bf16),
        v((512, D), bf16),
        v((512, D), bf16),
        v((512, 128), f32),
        v((512, 1024), bf16),
        v((2, 512, 256), bf16),
        v((512, 512), bf16),
        v((512, 128), f32),
        v((512, 128), f32),
        v((512, 384), f32),
        v((2, 1, D), f32),
        v((4, 8, 128), i32),
        v((512, 384), bf16),
        v((2, 4, 2, 2, 96, 384), bf16),
        v((2, 4, 2, 2, 48, D), bf16),
        v((4, 2, 2, 96, 1024), bf16),
        v((4, 2, 2, 96, 1024), bf16),
        v((2, 4, 2, 2, 32, D), bf16),
        v((3, 512, 1024), bf16),
        v((4, 512, 384), bf16),
        v((4, 512, 384), bf16),
        v((3, 6, 256, 384), bf16),
        v((512, 128), f32),
        v((512, D), bf16),
        v((512, 384), f32),
        v((4, 512, 128), f32),
        v((4, 512, 128), f32),
        v((4, 512, 128), f32),
        v((2, 512, 256), bf16),
        v((2, 512, 384), bf16),
        v((2, 4, 8, 128), f32),
        v((512, 1), f32),
        v((8, 384), f32),
        v((4, 2, 96, 1024), bf16),
        v((4, 2, 96, 1024), bf16),
        v((2, 4, 2, 32, D), bf16),
        v((2, 4, 2, 96, 384), bf16),
        v((2, 2, 48, D), bf16),
        pltpu.SemaphoreType.DMA((270,)),
        pltpu.SemaphoreType.DMA((270,)),
        pltpu.SemaphoreType.DMA((20,)),
    ]
    scratch += [v(shape, bf16) for piece in slot_shapes() for step in piece for shape in step]
    return pl.pallas_call(
        layer_kernel,
        out_shape=outs,
        in_specs=[ANY] * 10 + [VM] * 3,
        out_specs=[VM] * len(outs),
        scratch_shapes=scratch,
        compiler_params=pltpu.CompilerParams(
            collective_id=0, has_side_effects=True, vmem_limit_bytes=63 * 1024 * 1024
        ),
        name="layer",
    )(tokens, pos, gain_a, gain_f, qkvw, ow, gw, uw, dw, cot, *constants())


def constants():
    half = HD // 2
    freq = np.zeros((8, 128), np.float32)
    rates = rope_base ** (-(np.arange(half) * 2.0 / HD))
    freq[:, :half] = rates
    freq[:, 64 : 64 + half] = rates
    perm = np.zeros((384, 512), np.float32)
    permo = np.zeros((512, 384), np.float32)
    for h in range(4):
        for d in range(HD):
            wide = d if (h == 3 or d < half) else d - half + 64
            perm[h * HD + d, h * 128 + wide] = 1
            permo[h * 128 + d, h * HD + d] = 1
    return jnp.asarray(freq), jnp.asarray(perm, bf16), jnp.asarray(permo, bf16)


def per_device(
    tokens,
    positions,
    attn_gain,
    qkv_weight,
    output_weight,
    ffn_gain,
    gate_weight,
    up_weight,
    down_weight,
    cotangent,
):
    parts = run_layer(
        tokens, positions.reshape(8, 128), attn_gain[None], ffn_gain[None], qkv_weight, output_weight,
        gate_weight, up_weight, down_weight, cotangent,
    )
    s = jax.ShapeDtypeStruct
    shapes = [(512, 384), (512, 384), (384,), (384, 384), (192, 384), (384,), (384, 512), (384, 512), (512, 384)]
    outs = pl.pallas_call(
        outputs_kernel,
        out_shape=[s(shape, f32) for shape in shapes],
        in_specs=[VM] * 8,
        out_specs=[VM] * 9,
        compiler_params=pltpu.CompilerParams(vmem_limit_bytes=63 * 1024 * 1024),
        name="outputs",
    )(*parts)
    return tuple(outs)


def solution(mesh):
    finer = Mesh(mesh.devices.reshape(2, 2, 4, 2, 4), AXES)
    row = ("y", "zh")
    in_specs = (
        P(DP_ROW, "x"),
        P(("zl", "core", "x")),
        P("x"),
        P("x", row),
        P(row, "x"),
        P("x"),
        P("x", row),
        P("x", row),
        P(row, "x"),
        P(DP_ROW, "x"),
    )
    out_specs = (
        P(DP_ROW, "x"),
        P(DP_ROW, "x"),
        P("x"),
        P("x", row),
        P(row, "x"),
        P("x"),
        P("x", row),
        P("x", row),
        P(row, "x"),
    )
    return jax.shard_map(per_device, mesh=finer, in_specs=in_specs, out_specs=out_specs, check_vma=False)
```

```python
import functools
import math

import jax
import jax.numpy as jnp
import numpy as np
from jax import lax
from jax.experimental import pallas as pl
from jax.experimental.pallas import tpu as pltpu
from jax.sharding import Mesh
from jax.sharding import PartitionSpec as P

D = 1536
HD = 96
AXES = ("zl", "core", "y", "zh", "x")
DP_ROW = ("zl", "core", "y", "zh")
bf16 = jnp.bfloat16
f32 = jnp.float32
i32 = jnp.int32
MESH = pl.DeviceIdType.MESH
VM = pl.BlockSpec(memory_space=pltpu.VMEM)
ANY = pl.BlockSpec(memory_space=pl.ANY)

epsilon = 1e-05
rope_base = 100000.0
masked_score = -1e30
score_scale = math.log2(math.e) / math.sqrt(HD)
H0, H1 = pl.ds(0, 256), pl.ds(256, 256)


def dot(a, b):
    return lax.dot_general(a, b, (((1,), (0,)), ((), ())), preferred_element_type=f32)


def dot_t(a, b):
    return lax.dot_general(a, b, (((1,), (1,)), ((), ())), preferred_element_type=f32)


def lanes(index, width):
    return pl.ds(pl.multiple_of(index * width, 128), width)


class Place:
    def __init__(self):
        self.x, self.y = lax.axis_index("x"), lax.axis_index("y")
        self.zl, self.zh, self.core = lax.axis_index("zl"), lax.axis_index("zh"), lax.axis_index("core")
        self.quarter = self.zl * 2 + self.core
        self.ahead, self.behind, self.across = [(self.x + k) % 4 for k in (1, 3, 2)]
        self.right, self.left, self.far = {"x": self.ahead}, {"x": self.behind}, {"x": self.across}
        self.ys = [{"y": (self.y + k) % 4} for k in (1, 3, 2)]
        self.zs = [{"zl": 1 - self.zl}, {"zl": 1 - self.zl, "zh": 1 - self.zh}, {"zh": 1 - self.zh}]
        self.twin = {"core": 1 - self.core}
        self.mirror = {"x": self.y, "y": self.x}
        y, zl, zh = self.y, self.zl, self.zh
        beside, opposite = y + 1 - y % 2 * 2, 3 - y
        self.cube = {
            "ya": ({"y": beside}, (beside, zl, zh)),
            "yb": ({"y": opposite}, (opposite, zl, zh)),
            "za": ({"zl": 1 - zl}, (y, 1 - zl, zh)),
            "zb": ({"zl": 1 - zl, "zh": 1 - zh}, (y, 1 - zl, 1 - zh)),
        }

    def across_link(self, name):
        return self.cube[name]

    def enter(self):
        barrier = pltpu.get_barrier_semaphore()
        peers = [self.right, self.left, self.far, *self.ys, *self.zs, self.twin]
        for peer in peers:
            pl.semaphore_signal(barrier, inc=1, device_id=peer, device_id_type=MESH)

        @pl.when(self.x != self.y)
        def _():
            pl.semaphore_signal(barrier, inc=1, device_id=self.mirror, device_id_type=MESH)
            pl.semaphore_wait(barrier, len(peers) + 1)

        @pl.when(self.x == self.y)
        def _():
            pl.semaphore_wait(barrier, len(peers))


class Links:
    def __init__(self, send, recv, local):
        self.send, self.recv, self.local, self.count, self.local_count = send, recv, local, 0, 0
        self.open = []

    def make(self, src, dst, device):
        i = self.count
        self.count += 1
        return pltpu.make_async_remote_copy(
            src, dst, self.send.at[i], self.recv.at[i], device_id=device, device_id_type=MESH
        )

    def start(self, src, dst, device):
        copy = self.make(src, dst, device)
        copy.start()
        self.open.append(copy)
        return copy

    def spread(self, ref, devices):
        return [self.start(ref, ref, device) for device in devices]

    def keep(self, src, dst):
        copy = pltpu.make_async_copy(src, dst, self.local.at[self.local_count])
        self.local_count += 1
        copy.start()
        return copy

    def settle(self, copies):
        for copy in copies:
            copy.wait_send()
        self.open = [copy for copy in self.open if all(copy is not done for done in copies)]

    def close(self):
        self.settle(list(self.open))


def arrive(copies):
    for copy in copies:
        copy.wait_recv()


class RingGather:
    def __init__(self, links, here, src, buf):
        cols = lanes(here.x, 384)
        self.links, self.here, self.buf = links, here, buf
        self.first = [
            links.start(src(H0), buf.at[H0, cols], here.right),
            links.start(src(H1), buf.at[H1, cols], here.left),
        ]
        self.second = [
            links.start(src(H1), buf.at[H1, cols], here.right),
            links.start(src(H0), buf.at[H0, cols], here.left),
        ]

    def forward(self):
        here, buf = self.here, self.buf
        self.first[0].wait_recv()
        a = buf.at[H0, lanes(here.behind, 384)]
        self.third = [self.links.start(a, a, here.right)]
        self.first[1].wait_recv()
        b = buf.at[H1, lanes(here.ahead, 384)]
        self.third += [self.links.start(b, b, here.left)]

    def near(self):
        arrive(self.second)

    def finish(self):
        arrive(self.third)

    def settle(self):
        self.links.settle(self.first + self.second + self.third)


class RingScatter:
    def __init__(self, links, here, part, slots):
        self.links, self.here, self.part, self.slots = links, here, part, slots

    def send_far(self):
        h, p, s = self.here, self.part, self.slots
        self.r0 = self.links.start(p.at[h.across, H0], s.at[0], h.right)
        self.l0 = self.links.start(p.at[h.across, H1], s.at[1], h.left)

    def send_near(self):
        h, p, s = self.here, self.part, self.slots
        self.r1 = self.links.start(p.at[h.ahead, H1], s.at[2], h.right)
        self.l1 = self.links.start(p.at[h.behind, H0], s.at[3], h.left)

    def forward(self):
        h, p, s = self.here, self.part, self.slots
        self.r0.wait_recv()
        p[h.ahead, H0] = (p[h.ahead, H0].astype(f32) + s[0].astype(f32)).astype(bf16)
        self.r2 = self.links.start(p.at[h.ahead, H0], s.at[4], h.right)
        self.l0.wait_recv()
        p[h.behind, H1] = (p[h.behind, H1].astype(f32) + s[1].astype(f32)).astype(bf16)
        self.l2 = self.links.start(p.at[h.behind, H1], s.at[5], h.left)

    def finish(self):
        arrive([self.r1, self.l1, self.r2, self.l2])

    def settle(self):
        self.links.settle([self.r0, self.l0, self.r1, self.l1, self.r2, self.l2])

    def received(self, half):
        s = self.slots
        pair = (4, 3) if half == 0 else (2, 5)
        return s[pair[0]].astype(f32) + s[pair[1]].astype(f32)


ORDERS = (("ya", "yb", "za", "zb"), ("za", "zb", "ya", "yb"), ("yb", "ya", "zb", "za"), ("zb", "za", "yb", "ya"))


def part_of(order):
    y_state = {(): "own", ("ya",): "pair", ("yb",): "cross"}.get(tuple(d for d in order if d[0] == "y"), "all")
    z_state = {(): "own", ("za",): "low", ("zb",): "cross"}.get(tuple(d for d in order if d[0] == "z"), "all")
    return y_state, z_state


def y_cells(state, y):
    return {"own": [(y, 1)], "pair": [(y // 2 * 2, 2)], "cross": [(y, 1), (3 - y, 1)], "all": [(0, 4)]}[state]


def z_cells(state, zl, zh, joined):
    if state == "all" and not joined:
        return [(None, 0), (None, 1)]
    cells = {"own": [(zl, zh)], "low": [(None, zh)], "cross": [(zl, zh), (1 - zl, 1 - zh)], "all": [(None, None)]}
    return cells[state]


def either(index):
    return slice(None) if index is None else index


class UnitColumns:
    def __init__(self, core, start, size):
        self.core, self.start, self.size = core, start, size

    def cells(self, state, y, zl, zh):
        rows = pl.ds(self.start, self.size)
        return [
            (slice(None), either(l), self.core, rows, pl.ds(pl.multiple_of(h * 512 + first * 128, 128), count * 128))
            for l, h in z_cells(state[1], zl, zh, False)
            for first, count in y_cells(state[0], y)
        ]

    def shapes(self, state):
        return [
            (4,) + ((2,) if l is None else ()) + (self.size, count * 128)
            for l, _ in z_cells(state[1], 0, 0, False)
            for _, count in y_cells(state[0], 0)
        ]


class Blocks:
    def __init__(self, core, start, size, width):
        self.core, self.start, self.size, self.width = core, start, size, width

    def cells(self, state, y, zl, zh):
        rows = pl.ds(self.start, self.size)
        pick = lambda first, count: first if count == 1 else (slice(None) if count == 4 else pl.ds(first, count))
        return [
            (either(h), pick(first, count), either(l), self.core, rows)
            for l, h in z_cells(state[1], zl, zh, True)
            for first, count in y_cells(state[0], y)
        ]

    def shapes(self, state):
        return [
            ((2,) if h is None else ()) + ((count,) if count > 1 else ()) + ((2,) if l is None else ()) + (self.size, self.width)
            for l, h in z_cells(state[1], 0, 0, True)
            for _, count in y_cells(state[0], 0)
        ]


class OutputRows:
    def __init__(self, core, start, size, place):
        self.core, self.start, self.size, self.place = core, start, size, place

    def cells(self, state, y, zl, zh):
        rows = pl.ds(self.start, self.size)
        return [
            (either(h), self.place, either(l), self.core, rows, pl.ds(pl.multiple_of(first * 384, 128), count * 384))
            for l, h in z_cells(state[1], zl, zh, True)
            for first, count in y_cells(state[0], y)
        ]

    def shapes(self, state):
        return [
            ((2,) if h is None else ()) + ((2,) if l is None else ()) + (self.size, count * 384)
            for l, h in z_cells(state[1], 0, 0, True)
            for _, count in y_cells(state[0], 0)
        ]


class CubeGather:
    def __init__(self, links, here, ref, layout, order):
        self.links, self.here, self.ref, self.layout, self.order, self.step = links, here, ref, layout, order, 0
        self.launch()

    def launch(self):
        here, ref = self.here, self.ref
        device, _ = here.across_link(self.order[self.step])
        cells = self.layout.cells(part_of(self.order[: self.step]), here.y, here.zl, here.zh)
        self.copies = [self.links.start(ref.at[cell], ref.at[cell], device) for cell in cells]

    def advance(self):
        arrive(self.copies)
        self.step += 1
        if self.step < 4:
            self.launch()


class CubeReduce:
    def __init__(self, links, here, ref, layout, order, slots):
        self.links, self.here, self.ref, self.layout, self.order, self.step = links, here, ref, layout, order, 3
        self.slots = slots
        self.launch()

    def launch(self):
        here, ref = self.here, self.ref
        device, coordinates = here.across_link(self.order[self.step])
        cells = self.layout.cells(part_of(self.order[: self.step]), *coordinates)
        pairs = zip(cells, self.slots[self.step])
        self.copies = [self.links.start(ref.at[cell], slot, device) for cell, slot in pairs]

    def advance(self):
        here, ref = self.here, self.ref
        arrive(self.copies)
        cells = self.layout.cells(part_of(self.order[: self.step]), here.y, here.zl, here.zh)
        for cell, slot in zip(cells, self.slots[self.step]):
            ref[cell] = (ref[cell].astype(f32) + slot[...].astype(f32)).astype(bf16)
        self.step -= 1
        if self.step >= 0:
            self.launch()


def advance(cubes):
    for cube in cubes:
        cube.advance()


def grad_layouts(core, place):
    return [
        ("d", Blocks(core, 0, 16, D), 0),
        ("d", Blocks(core, 16, 16, D), 3),
        ("g", UnitColumns(core, 0, 48), 0),
        ("g", UnitColumns(core, 48, 48), 1),
        ("u", UnitColumns(core, 0, 48), 2),
        ("u", UnitColumns(core, 48, 48), 3),
        ("o", OutputRows(core, 0, 16, place), 1),
        ("o", OutputRows(core, 16, 16, place), 2),
        ("o", OutputRows(core, 32, 16, place), 3),
        ("q", Blocks(core, 0, 32, 384), 0),
        ("q", Blocks(core, 32, 32, 384), 1),
        ("q", Blocks(core, 64, 16, 384), 2),
        ("q", Blocks(core, 80, 16, 384), 3),
    ]


def slot_shapes():
    return [
        [layout.shapes(part_of(ORDERS[order][:step])) for step in range(4)] for _, layout, order in grad_layouts(0, 0)
    ]


def sine_cosine(angle):
    turns = jnp.floor(angle * (1.0 / (2.0 * math.pi)) + 0.5)
    r = angle - turns * 6.28125
    r = r - turns * 0.0019350051879882812
    r = r - turns * 3.0199159819185874e-07
    t = r * 0.5
    t2 = t * t
    s = 1.0 / 6227020800.0
    for c in (-1.0 / 39916800, 1.0 / 362880, -1.0 / 5040, 1.0 / 120, -1.0 / 6, 1.0):
        s = s * t2 + c
    s = s * t
    c_ = 1.0 / 479001600.0
    for c in (-1.0 / 3628800, 1.0 / 40320, -1.0 / 720, 1.0 / 24, -0.5, 1.0):
        c_ = c_ * t2 + c
    return 2.0 * s * c_, 1.0 - 2.0 * s * s


def causal(scores):
    last = scores[:, -256:]
    seen = lax.broadcasted_iota(i32, (256, 256), 1) <= lax.broadcasted_iota(i32, (256, 256), 0)
    last = jnp.where(seen, last, masked_score)
    return last if scores.shape[1] == 256 else jnp.concatenate([scores[:, :-256], last], axis=1)


def turn(head, cosine, sine):
    return head * cosine + pltpu.roll(head, 64, 1) * sine


def dot_first(a, b):
    return lax.dot_general(a, b, (((0,), (0,)), ((), ())), preferred_element_type=f32)


def column_to_rows(column, ref):
    for c in range(4):
        block = jnp.broadcast_to(column[c * 128 : c * 128 + 128], (128, 128)).T
        ref[c : c + 1] = block[0:1]


def rows_to_column(rows):
    return jnp.concatenate([jnp.broadcast_to(rows[c : c + 1], (128, 128)).T for c in range(4)], 0)


def layer_kernel(
    tokens, pos, gain_a, gain_f, qkvw, ow, gw, uw, dw, cot, freq, perm, permo,
    mixed, tgrad, dgain, fin_q, fin_o, fin_g, fin_u, fin_d,
    xf, a1, a2, cotf, stats, qkv, kvr, att, cosb, sinb, middle, gn, posb, packed,
    wqkv, wo, wg, wu, wd, hdd, part, partd, slots, wide, dzf, dmid,
    dq, dkv, dkr, dkin, dproj, small, sums, gsum, rc_g, rc_u, rc_d, rc_q, rc_o,
    send, recv, local, *slot_refs,
):
    here = Place()
    links = Links(send, recv, local)
    x, y, zl, zh, core, quarter = here.x, here.y, here.zl, here.zh, here.core, here.quarter
    hid = zh * 4 + y
    other = 1 - core
    own, y_cols = lanes(x, 384), lanes(y, 384)
    a, b, da, db, oa, ob = pl.ds(0, 48), pl.ds(48, 48), pl.ds(0, 16), pl.ds(16, 16), pl.ds(0, 32), pl.ds(32, 16)
    refs = iter(slot_refs)
    layouts = [
        (name, layout, ORDERS[order], [[next(refs) for _ in shapes] for shapes in steps])
        for (name, layout, order), steps in zip(grad_layouts(core, x), slot_shapes())
    ]
    x_peers = (here.right, here.left, here.far)
    gn[0, :, own] = gain_a[...].reshape(1, 384)
    gn[1, :, own] = gain_f[...].reshape(1, 384)
    here.enter()

    own_qkv, src_qkv = wqkv.at[zh, x, zl, core], qkvw.at[pl.ds(quarter * 96, 96)]
    own_o, src_o = wo.at[zh, y, zl, core, :, own], ow.at[pl.ds(quarter * 48, 48)]
    mirror = [links.make(src_qkv, own_qkv, here.mirror)]
    stay = [pltpu.make_async_copy(src_qkv, own_qkv, local.at[0])]
    links.local_count = 2

    @pl.when(x != y)
    def _():
        for copy in mirror:
            copy.start()

    @pl.when(x == y)
    def _():
        for copy in stay:
            copy.start()

    def hidden_slices(target):
        rows = pl.ds(quarter * 96, 96)
        return [
            (gw.at[rows, lanes(target, 128)], wg.at[x, zl, core, :, lanes(hid, 128)]),
            (uw.at[rows, lanes(target, 128)], wu.at[x, zl, core, :, lanes(hid, 128)]),
            (dw.at[pl.ds(target * 128 + quarter * 32, 32)], wd.at[zh, y, zl, core, :, own]),
        ]

    swaps = []
    for peer, target in ((here.right, here.ahead), (here.left, here.behind), (here.far, here.across)):
        swaps += [links.start(src, dst, peer) for src, dst in hidden_slices(target)]
    swap_kept = [links.keep(src, dst) for src, dst in hidden_slices(x)]
    swaps_o = [links.start(src_o, own_o, peer) for peer in x_peers]
    swap_kept_o = links.keep(src_o, own_o)

    ring_x = RingGather(links, here, lambda half: tokens.at[half], xf)
    kept = [links.keep(tokens, xf.at[:, own])]
    small_sends = []
    for peer in x_peers:
        small_sends.append(links.start(pos, posb.at[x], peer))
        small_sends.append(links.start(gn.at[0, :, own], gn.at[0, :, own], peer))
        small_sends.append(links.start(gn.at[1, :, own], gn.at[1, :, own], peer))
    kept += [links.keep(pos, posb.at[x])]

    @pl.when(x != y)
    def _():
        for copy in mirror:
            copy.wait()

    @pl.when(x == y)
    def _():
        for copy in stay:
            copy.wait()

    pieces = ((0, 32), (32, 32), (64, 16), (80, 16))
    cube_q = [
        CubeGather(links, here, wqkv, Blocks(core, start, size, 384), ORDERS[k]) for k, (start, size) in enumerate(pieces)
    ]
    advance(cube_q)
    for copy in swap_kept:
        copy.wait()
    arrive(swaps)
    cube_g = [CubeGather(links, here, wg, UnitColumns(core, 48 * k, 48), ORDERS[k]) for k in range(2)]
    cube_u = [CubeGather(links, here, wu, UnitColumns(core, 48 * k, 48), ORDERS[2 + k]) for k in range(2)]
    cube_d = [CubeGather(links, here, wd, Blocks(core, 16 * k, 16, D), ORDERS[3 * k]) for k in range(2)]
    ring_x.forward()
    advance(cube_q)
    swap_kept_o.wait()
    arrive(swaps_o)
    cube_o = [CubeGather(links, here, wo, Blocks(core, 16 * k, 16, D), ORDERS[1 + k]) for k in range(3)]
    advance(cube_g)
    advance(cube_u)
    advance(cube_d)
    advance(cube_q)
    advance(cube_o)

    for copy in kept:
        copy.wait()
    arrive(small_sends)
    mine = posb[y]
    mine = jnp.where(zh == 0, mine[0:4], mine[4:8]).astype(f32)
    lane = lax.broadcasted_iota(i32, (128, 128), 1)
    for c in range(4):
        column = jnp.broadcast_to(mine[c : c + 1], (128, 128)).T
        sine, cosine = sine_cosine(column * freq[0:1])
        cosb[pl.ds(c * 128, 128)] = cosine
        sinb[pl.ds(c * 128, 128)] = jnp.where(lane < 64, -sine, sine)

    ring_x.near()
    ring_x.finish()
    ring_c = RingGather(links, here, lambda half: cot.at[half], cotf)
    cot_kept = links.keep(cot, cotf.at[:, own])

    def norm_tokens(i, _):
        rows = pl.ds(pl.multiple_of(i * 64, 64), 64)
        value = xf[rows].astype(f32)
        inverse = lax.rsqrt(jnp.sum(value * value, axis=1, keepdims=True) * (1.0 / D) + epsilon)
        a1[rows] = (value * gn[0]).astype(bf16)
        stats[rows] = jnp.broadcast_to(inverse, (64, 128))
        return 0

    lax.fori_loop(0, 8, norm_tokens, 0)

    advance(cube_q)
    core_qkv = links.spread(wqkv.at[:, :, :, core], [here.twin])
    advance(cube_g)
    advance(cube_u)
    advance(cube_d)
    advance(cube_o)

    arrive(core_qkv)

    def widen(i, _):
        w = wqkv[i].reshape(D, 384)
        for j in range(3):
            hdd[j, :, lanes(i, 512)] = dot(w[j * 512 : j * 512 + 512], perm[...]).astype(bf16)
        return 0

    lax.fori_loop(0, 2, widen, 0)

    def keys_values(g, _):
        pair = dot(a1[...], hdd[:, :, lanes(g * 2 + 1, 256)].reshape(D, 256))
        inverse = stats[...]
        qkv[:, lanes(g * 4 + 2, 128)] = turn(pair[:, :128] * inverse, cosb[...], sinb[...]).astype(bf16)
        qkv[:, lanes(g * 4 + 3, 128)] = (pair[:, 128:] * inverse).astype(bf16)
        return 0

    lax.fori_loop(0, 2, keys_values, 0)
    over = [links.make(qkv.at[:, pl.ds(g * 512 + 256, 256)], kvr.at[g], here.zs[2]) for g in range(2)]

    @pl.when(zh == 0)
    def _():
        for copy in over:
            copy.start()

    advance(cube_g)
    advance(cube_u)
    advance(cube_d)
    advance(cube_o)

    def queries(g, _):
        pair = dot(a1[...], hdd[:, :, lanes(g * 2, 256)].reshape(D, 256))
        inverse = stats[...]
        for h in range(2):
            head = pair[:, h * 128 : h * 128 + 128] * inverse
            qkv[:, lanes(g * 4 + h, 128)] = (turn(head, cosb[...], sinb[...]) * score_scale).astype(bf16)
        return 0

    lax.fori_loop(0, 2, queries, 0)
    ring_c.forward()

    def own_scores(i, _):
        g = i // 2
        for qb in range(2):
            rows, keys = pl.ds(qb * 256, 256), pl.ds(0, qb * 256 + 256)
            q = qkv[rows, lanes(g * 4 + i % 2, 128)]
            s = causal(dot_t(q, qkv[keys, lanes(g * 4 + 2, 128)]))
            m = jnp.max(s, axis=1, keepdims=True)
            e = jnp.exp2(s - m)
            dq[i, rows] = dot(e.astype(bf16), qkv[keys, lanes(g * 4 + 3, 128)])
            dkv[i, rows] = jnp.broadcast_to(m, (256, 128))
            dkr[i, rows] = jnp.broadcast_to(jnp.sum(e, axis=1, keepdims=True), (256, 128))
        return 0

    lax.fori_loop(0, 4, own_scores, 0)

    @pl.when(zh == 1)
    def _():
        for copy in over:
            copy.wait_recv()

        def first_scores(i, _):
            g = i // 2
            for qb in range(2):
                rows = pl.ds(qb * 256, 256)
                q = qkv[rows, lanes(g * 4 + i % 2, 128)]
                s = dot_t(q, kvr[g, :, 0:128])
                old = dkv[i, rows][:, 0:1]
                m = jnp.maximum(old, jnp.max(s, axis=1, keepdims=True))
                e = jnp.exp2(s - m)
                shrink = jnp.exp2(old - m)
                dq[i, rows] = dq[i, rows] * shrink + dot(e.astype(bf16), kvr[g, :, 128:256])
                dkr[i, rows] = dkr[i, rows] * shrink + jnp.sum(e, axis=1, keepdims=True)
                dkv[i, rows] = jnp.broadcast_to(m, (256, 128))
            return 0

        lax.fori_loop(0, 4, first_scores, 0)

    @pl.when(zh == 0)
    def _():
        for copy in over:
            copy.wait_send()

    advance(cube_o)
    core_o = links.spread(wo.at[:, :, :, core], [here.twin])
    lane = lax.broadcasted_iota(i32, (512, 128), 1)
    for i in range(4):
        att[:, i * 128 : i * 128 + 128] = (dq[i] / dkr[i]).astype(bf16)
        stats[...] = jnp.where(lane == i, dkv[i] + jnp.log2(dkr[i]), stats[...])

    packed[...] = dot(att[...], permo[...]).astype(bf16)
    ring_a = RingGather(links, here, lambda half: packed.at[half], dzf)
    dzf[:, own] = packed[...]
    thirds = (dq, dkv, dkr)

    def output_part(block, c):
        return dot(dzf[:, lanes(block, 384)], wo[:, block, :, :, :, lanes(c, 384)].reshape(384, 384))

    def output_first(c, _):
        value = xf[:, lanes(c, 384)].astype(f32) + output_part(x, c)
        for k, ref in enumerate(thirds):
            ref[c] = value[:, k * 128 : k * 128 + 128]
        return 0

    def output_near(c, _):
        value = output_part(here.ahead, c) + output_part(here.behind, c)
        for k, ref in enumerate(thirds):
            ref[c] = ref[c] + value[:, k * 128 : k * 128 + 128]
        return 0

    def output_last(c, _):
        value = output_part(here.across, c)
        for k, ref in enumerate(thirds):
            m = ref[c] + value[:, k * 128 : k * 128 + 128]
            ref[c] = m
            a2[:, lanes(c * 3 + k, 128)] = (m * gn[1, :, lanes(c * 3 + k, 128)]).astype(bf16)
            sums[...] = sums[...] + jnp.sum(m * m, axis=1, keepdims=True)
        return 0

    arrive(core_o)
    lax.fori_loop(0, 4, output_first, 0)
    ring_a.forward()
    advance(cube_g)
    cores = [links.start(wg.at[:, :, core], wg.at[:, :, core], here.twin)]
    advance(cube_u)
    cores.append(links.start(wu.at[:, :, core], wu.at[:, :, core], here.twin))
    advance(cube_d)
    cores.append(links.start(wd.at[:, :, :, core], wd.at[:, :, :, core], here.twin))
    ring_a.near()
    lax.fori_loop(0, 4, output_near, 0)
    cot_kept.wait()
    ring_c.near()
    ring_c.finish()
    sums[...] = jnp.zeros_like(sums)
    ring_a.finish()
    lax.fori_loop(0, 4, output_last, 0)
    wide[...] = jnp.broadcast_to(lax.rsqrt(sums[...] * (1.0 / D) + epsilon), (512, 128))
    for k, ref in enumerate(thirds):
        middle[:, k * 128 : k * 128 + 128] = ref[x]
    links.close()
    arrive(cores)

    sums[...] = jnp.zeros_like(sums)

    def units(n, _):
        cols = lanes(n, 256)
        w_g = wg[:, :, :, :, cols].reshape(D, 256)
        w_u = wu[:, :, :, :, cols].reshape(D, 256)
        w_d = wd[n // 2, pl.ds((n % 2) * 2, 2)].reshape(256, D)
        for rows in (H0, H1):
            inverse = wide[rows][:, 0:1]
            gate = dot(a2[rows], w_g) * inverse
            up = dot(a2[rows], w_u) * inverse
            dh = dot_t(cotf[rows], w_d)
            sg = 1.0 / (1.0 + jnp.exp(-gate))
            silu = gate * sg
            dg = dh * up * (sg + silu * (1.0 - sg))
            du = dh * silu
            hdd[0, rows, cols] = (silu * up).astype(bf16)
            hdd[1, rows, cols] = (dg * inverse).astype(bf16)
            hdd[2, rows, cols] = (du * inverse).astype(bf16)
            inner = jnp.sum(dg * gate + du * up, axis=1, keepdims=True)
            sums[rows] = sums[rows] + inner
        return 0

    lax.fori_loop(0, 4, units, 0)

    def back_block(block):
        return dot_t(hdd[1], wg[block].reshape(384, 1024)) + dot_t(hdd[2], wu[block].reshape(384, 1024))

    scatter = RingScatter(links, here, part, slots.at[0])
    part[here.across] = back_block(here.across).astype(bf16)
    scatter.send_far()
    part[here.ahead] = back_block(here.ahead).astype(bf16)
    part[here.behind] = back_block(here.behind).astype(bf16)
    scatter.send_near()
    column_to_rows(sums[...], small.at[0, x])
    inner_sums = [links.start(small.at[0, x], small.at[0, x], p) for p in x_peers]
    dmid[...] = back_block(x)
    scatter.forward()

    def down_block(block, _):
        cols = lanes(block, 384)
        partd[block] = dot(hdd[0], wd[:, :, :, :, :, cols].reshape(1024, 384)).astype(bf16)
        return 0

    lax.fori_loop(0, 4, down_block, 0)

    def down_grad(n, _):
        rows = hdd[0, :, lanes(n, 256)].T
        for c in range(3):
            cols = pl.ds(c * 512, 512)
            value = dot(rows, cotf[:, cols]).astype(bf16)
            wd[n // 2, pl.ds((n % 2) * 2, 2), :, :, :, cols] = value.reshape(2, 2, 2, 32, 512)
        return 0

    lax.fori_loop(0, 4, down_grad, 0)
    cores = [links.start(wd.at[:, :, :, other], rc_d, here.twin)]

    def up_grads(block, _):
        rows = a2[:, lanes(block, 384)].T
        for source, target in ((1, wg), (2, wu)):
            for c in range(2):
                cols = pl.ds(c * 512, 512)
                target[block, :, :, :, cols] = dot(rows, hdd[source, :, cols]).astype(bf16).reshape(2, 2, 96, 512)
        return 0

    lax.fori_loop(0, 4, up_grads, 0)
    cores.append(links.start(wg.at[:, :, other], rc_g, here.twin))
    cores.append(links.start(wu.at[:, :, other], rc_u, here.twin))

    buffers = {"d": wd, "g": wg, "u": wu, "o": wo, "q": wqkv}
    reduces = {}

    def start_reduce(name):
        reduces[name] = [
            CubeReduce(links, here, buffers[name], layout, order, slots_)
            for piece, layout, order, slots_ in layouts
            if piece == name
        ]

    def core_sum_down(i, _):
        for k in range(2):
            for j in range(2):
                value = wd[k, i, j, core].astype(f32) + rc_d[k, i, j].astype(f32)
                wd[k, i, j, core] = value.astype(bf16)
        return 0

    arrive(cores[0:1])
    lax.fori_loop(0, 4, core_sum_down, 0)
    start_reduce("d")

    arrive(inner_sums)
    inner = rows_to_column(jnp.sum(small[0], axis=0)[0:4])[:, 0:1]
    scatter.finish()
    gsum[...] = jnp.zeros_like(gsum)
    for half, rows in enumerate((H0, H1)):
        da2 = dmid[rows] + scatter.received(half)
        m, inverse = middle[rows], wide[rows][:, 0:1]
        gsum[1:2] = gsum[1:2] + jnp.sum(da2 * m, axis=0, keepdims=True)
        factor = inner[half * 256 : half * 256 + 256] * inverse * inverse * (1.0 / D)
        value = cotf[rows, own].astype(f32) + gn[1, :, own] * da2 - m * factor
        dmid[rows] = value
        dzf[rows, own] = value.astype(bf16)
    ring_z = RingGather(links, here, lambda half: dzf.at[half, own], dzf)
    ring_z.forward()

    for matrix, (name, source) in enumerate((("g", rc_g), ("u", rc_u))):
        arrive(cores[matrix + 1 : matrix + 2])

        def core_sum(i, _, target=buffers[name], source=source):
            for j in range(2):
                target[i, j, core] = (target[i, j, core].astype(f32) + source[i, j].astype(f32)).astype(bf16)
            return 0

        lax.fori_loop(0, 4, core_sum, 0)
        start_reduce(name)

    ring_z.near()
    ring_z.finish()

    scatter_d = RingScatter(links, here, partd, slots.at[1])
    scatter_d.send_far()
    scatter_d.send_near()

    packed[...] = dot_t(dzf[...], wo[:, x].reshape(384, D)).astype(bf16)
    hdd[1, :, 0:512] = dot_t(packed[...], permo[...]).astype(bf16)
    packed[...] = dot(att[...], permo[...]).astype(bf16)
    for c in range(3):
        cols = pl.ds(c * 512, 512)
        value = dot_first(packed[...], dzf[:, cols]).astype(bf16)
        wo[:, x, :, :, :, cols] = value.reshape(2, 2, 2, 48, 512)
    cores = [links.start(wo.at[:, x, :, other], rc_o, here.twin)]

    dq[...] = jnp.zeros_like(dq)
    dkv[...] = jnp.zeros_like(dkv)

    def pair(i, rows, k, v, masked):
        g = i // 2
        head = lanes(i, 128)
        q, grad = qkv[rows, lanes(g * 4 + i % 2, 128)], hdd[1, rows, head]
        delta = jnp.sum(grad.astype(f32) * att[rows, head].astype(f32), axis=1, keepdims=True)
        lane = lax.broadcasted_iota(i32, (256, 128), 1)
        lse = jnp.sum(jnp.where(lane == i, stats[rows], 0.0), axis=1, keepdims=True)
        s = dot_t(q, k)
        if masked:
            s = causal(s)
        p = jnp.exp2(s - lse)
        ds = (p * (dot_t(grad, v) - delta)).astype(bf16)
        dq[i, rows] = dq[i, rows] + dot(ds, k)
        return dot_first(ds, q), dot_first(p.astype(bf16), grad)

    give = [links.make(kvr.at[g], dkin.at[g], here.zs[2]) for g in range(2)]

    @pl.when(zh == 1)
    def _():
        dkr[...] = jnp.zeros_like(dkr)

        def first_half(i, _):
            g = i // 2
            for qb in range(2):
                dk, dv = pair(i, pl.ds(qb * 256, 256), kvr[g, :, 0:128], kvr[g, :, 128:256], False)
                dkr[2 * g] = dkr[2 * g] + dk
                dkr[2 * g + 1] = dkr[2 * g + 1] + dv
            return 0

        for g in range(2):
            lax.fori_loop(2 * g, 2 * g + 2, first_half, 0)
            kvr[g, :, 0:128] = dkr[2 * g].astype(bf16)
            kvr[g, :, 128:256] = dkr[2 * g + 1].astype(bf16)
            give[g].start()

    scatter_d.forward()

    def own_keys(i, _):
        g = i // 2
        for qb in range(2):
            keys = pl.ds(0, qb * 256 + 256)
            k, v = qkv[keys, lanes(g * 4 + 2, 128)], qkv[keys, lanes(g * 4 + 3, 128)]
            dk, dv = pair(i, pl.ds(qb * 256, 256), k, v, True)
            dkv[2 * g, keys] = dkv[2 * g, keys] + dk
            dkv[2 * g + 1, keys] = dkv[2 * g + 1, keys] + dv
        return 0

    lax.fori_loop(0, 4, own_keys, 0)

    @pl.when(zh == 0)
    def _():
        for g in range(2):
            give[g].wait_recv()
            dkv[2 * g] = dkv[2 * g] + dkin[g, :, 0:128].astype(f32)
            dkv[2 * g + 1] = dkv[2 * g + 1] + dkin[g, :, 128:256].astype(f32)

    @pl.when(zh == 1)
    def _():
        for g in range(2):
            give[g].wait_send()

    for name in "dgu":
        advance(reduces[name])
    arrive(cores)
    for g in range(2):
        for j in range(2):
            wo[g, x, j, core] = (wo[g, x, j, core].astype(f32) + rc_o[g, j].astype(f32)).astype(bf16)
    start_reduce("o")

    sums[...] = jnp.zeros_like(sums)
    inverse = stats[:, 4:5]
    for i in range(8):
        cols = pl.ds(i * 128, 128)
        g, place = i // 4, i % 4
        value = dq[2 * g + place] if place < 2 else dkv[2 * g + place - 2]
        if place == 2:
            value = value * math.log(2.0)
        inside = jnp.sum(value * qkv[:, cols].astype(f32), axis=1, keepdims=True)
        if place < 2:
            inside = inside * math.log(2.0)
            value = value * (1.0 / math.sqrt(HD))
        sums[...] = sums[...] + inside
        if place < 3:
            value = turn(value, cosb[...], -sinb[...])
        hdd[0, :, cols] = (value * inverse).astype(bf16)
    column_to_rows(sums[...], small.at[1, x])
    inner_sums = [links.start(small.at[1, x], small.at[1, x], p) for p in x_peers]
    for g in range(2):
        dproj[g] = dot_t(hdd[0, :, g * 512 : g * 512 + 512], perm[...]).astype(bf16)

    def back_input(block):
        return sum(dot_t(dproj[g], wqkv[g, block].reshape(384, 384)) for g in range(2))

    scatter.settle()
    scatter = RingScatter(links, here, part, slots.at[2])
    part[here.across] = back_input(here.across).astype(bf16)
    scatter.send_far()
    part[here.ahead] = back_input(here.ahead).astype(bf16)
    part[here.behind] = back_input(here.behind).astype(bf16)
    scatter.send_near()
    tgrad[...] = back_input(x)

    def qkv_grads(block, _):
        rows = a1[:, lanes(block, 384)].T
        for g in range(2):
            wqkv[g, block] = dot(rows, dproj[g]).astype(bf16).reshape(2, 2, 96, 384)
        return 0

    lax.fori_loop(0, 4, qkv_grads, 0)
    cores.append(links.start(wqkv.at[:, :, :, other], rc_q, here.twin))
    scatter.forward()

    for name in "dgu":
        advance(reduces[name])

    scatter_d.finish()
    for half, rows in enumerate((H0, H1)):
        mixed[rows] = middle[rows] + partd[x, rows].astype(f32) + scatter_d.received(half)

    arrive(cores[1:])
    for g in range(2):

        def core_heads(i, _, g=g):
            for j in range(2):
                value = wqkv[g, i, j, core].astype(f32) + rc_q[g, i, j].astype(f32)
                wqkv[g, i, j, core] = value.astype(bf16)
            return 0

        lax.fori_loop(0, 4, core_heads, 0)
    start_reduce("q")
    advance(reduces["o"])
    for name in "dgu":
        advance(reduces[name])

    arrive(inner_sums)
    inner = rows_to_column(jnp.sum(small[1], axis=0)[0:4])[:, 0:1]
    scatter.finish()
    for half, rows in enumerate((H0, H1)):
        da1 = tgrad[rows] + scatter.received(half)
        source, rinv = xf[rows, own].astype(f32), stats[rows][:, 4:5]
        gsum[0:1] = gsum[0:1] + jnp.sum(da1 * source, axis=0, keepdims=True)
        factor = inner[half * 256 : half * 256 + 256] * rinv * rinv * (1.0 / D)
        tgrad[rows] = dmid[rows] + gn[0, :, own] * da1 - source * factor
    dgain[0] = gsum[...]
    gain_y = [links.start(dgain.at[0], dgain.at[1 + j], here.ys[j]) for j in range(3)]

    for name in "dgu":
        advance(reduces[name])

    def hidden_blocks(target):
        return [
            (wg.at[target, zl, core, :, lanes(hid, 128)], fin_g.at[zl, core, :, lanes(x, 128)]),
            (wu.at[target, zl, core, :, lanes(hid, 128)], fin_u.at[zl, core, :, lanes(x, 128)]),
            (wd.at[zh, y, zl, core, :, lanes(target, 384)], fin_d.at[x, zl, core]),
        ]

    swaps = []
    for peer, target in ((here.right, here.ahead), (here.left, here.behind), (here.far, here.across)):
        swaps += [links.start(src, dst, peer) for src, dst in hidden_blocks(target)]
    swap_kept = [links.keep(src, dst) for src, dst in hidden_blocks(x)]

    for _ in range(2):
        advance(reduces["q"])
        advance(reduces["o"])

    for copy in swap_kept:
        copy.wait()
    arrive(swaps)
    fins = ((fin_g, 0), (fin_u, 0), (fin_d, 1))
    pick = lambda ref, lead, index: ref.at[(slice(None),) * lead + index]
    across_zl = [links.start(v, v, here.zs[0]) for v in (pick(ref, lead, (zl, core)) for ref, lead in fins)]

    arrive(gain_y)
    gsum[...] = dgain[0] + dgain[1] + dgain[2] + dgain[3]
    dgain[4] = gsum[...]
    gain_z = [links.start(dgain.at[4], dgain.at[5 + j], here.zs[j]) for j in range(3)]

    for _ in range(2):
        advance(reduces["q"])
    advance(reduces["o"])
    src_q, src_o = wqkv.at[zh, y, zl, core], wo.at[zh, x, zl, core, :, y_cols]
    dst_q, dst_o = fin_q.at[zl, core], fin_o.at[zl, core]
    mirror = [links.make(src_q, dst_q, here.mirror), links.make(src_o, dst_o, here.mirror)]
    first = links.local_count
    stay = [pltpu.make_async_copy(src_q, dst_q, local.at[first]), pltpu.make_async_copy(src_o, dst_o, local.at[first + 1])]

    @pl.when(x != y)
    def _():
        for copy in mirror:
            copy.start()
        for copy in mirror:
            copy.wait()

    @pl.when(x == y)
    def _():
        for copy in stay:
            copy.start()
        for copy in stay:
            copy.wait()

    head_zl = [links.start(v, v, here.zs[0]) for v in (fin_q.at[zl, core], fin_o.at[zl, core])]
    arrive(across_zl)
    to_core = [links.start(v, v, here.twin) for v in (pick(ref, lead, (slice(None), core)) for ref, lead in fins)]
    arrive(gain_z)
    gsum[...] = dgain[4] + dgain[5] + dgain[6] + dgain[7]
    dgain[8] = gsum[...]
    gain_c = links.start(dgain.at[8], dgain.at[9], here.twin)
    arrive(head_zl)
    head_core = [links.start(v, v, here.twin) for v in (fin_q.at[:, core], fin_o.at[:, core])]
    arrive([gain_c])
    arrive(to_core)
    arrive(head_core)
    links.close()


def outputs_kernel(mixed, tgrad, dgain, g_q, g_o, g_g, g_u, g_d, *outs):
    gains = dgain[8] + dgain[9]
    outs[0][...] = mixed[...]
    outs[1][...] = tgrad[...]
    outs[2][...] = gains[0]
    outs[5][...] = gains[1]
    for out, source in zip((outs[3], outs[4], outs[6], outs[7], outs[8]), (g_q, g_o, g_g, g_u, g_d)):
        out[...] = source[...].reshape(out.shape).astype(f32)


def run_layer(tokens, pos, gain_a, gain_f, qkvw, ow, gw, uw, dw, cot):
    s = jax.ShapeDtypeStruct
    v = pltpu.VMEM
    outs = [
        s((512, 384), f32),
        s((512, 384), f32),
        s((10, 8, 384), f32),
        s((2, 2, 96, 384), bf16),
        s((2, 2, 48, 384), bf16),
        s((2, 2, 96, 512), bf16),
        s((2, 2, 96, 512), bf16),
        s((4, 2, 2, 32, 384), bf16),
    ]
    scratch = [
        v((512, D), bf16),
        v((512, D), bf16),
        v((512, D), bf16),
        v((512, D), bf16),
        v((512, 128), f32),
        v((512, 1024), bf16),
        v((2, 512, 256), bf16),
        v((512, 512), bf16),
        v((512, 128), f32),
        v((512, 128), f32),
        v((512, 384), f32),
        v((2, 1, D), f32),
        v((4, 8, 128), i32),
        v((512, 384), bf16),
        v((2, 4, 2, 2, 96, 384), bf16),
        v((2, 4, 2, 2, 48, D), bf16),
        v((4, 2, 2, 96, 1024), bf16),
        v((4, 2, 2, 96, 1024), bf16),
        v((2, 4, 2, 2, 32, D), bf16),
        v((3, 512, 1024), bf16),
        v((4, 512, 384), bf16),
        v((4, 512, 384), bf16),
        v((3, 6, 256, 384), bf16),
        v((512, 128), f32),
        v((512, D), bf16),
        v((512, 384), f32),
        v((4, 512, 128), f32),
        v((4, 512, 128), f32),
        v((4, 512, 128), f32),
        v((2, 512, 256), bf16),
        v((2, 512, 384), bf16),
        v((2, 4, 8, 128), f32),
        v((512, 1), f32),
        v((8, 384), f32),
        v((4, 2, 96, 1024), bf16),
        v((4, 2, 96, 1024), bf16),
        v((2, 4, 2, 32, D), bf16),
        v((2, 4, 2, 96, 384), bf16),
        v((2, 2, 48, D), bf16),
        pltpu.SemaphoreType.DMA((270,)),
        pltpu.SemaphoreType.DMA((270,)),
        pltpu.SemaphoreType.DMA((20,)),
    ]
    scratch += [v(shape, bf16) for piece in slot_shapes() for step in piece for shape in step]
    return pl.pallas_call(
        layer_kernel,
        out_shape=outs,
        in_specs=[ANY] * 2 + [VM] * 2 + [ANY] * 6 + [VM] * 3,
        out_specs=[VM] * len(outs),
        scratch_shapes=scratch,
        compiler_params=pltpu.CompilerParams(
            collective_id=0, has_side_effects=True, vmem_limit_bytes=63 * 1024 * 1024
        ),
        name="layer",
    )(tokens, pos, gain_a, gain_f, qkvw, ow, gw, uw, dw, cot, *constants())


def constants():
    half = HD // 2
    freq = np.zeros((8, 128), np.float32)
    rates = rope_base ** (-(np.arange(half) * 2.0 / HD))
    freq[:, :half] = rates
    freq[:, 64 : 64 + half] = rates
    perm = np.zeros((384, 512), np.float32)
    permo = np.zeros((512, 384), np.float32)
    for h in range(4):
        for d in range(HD):
            wide = d if (h == 3 or d < half) else d - half + 64
            perm[h * HD + d, h * 128 + wide] = 1
            permo[h * 128 + d, h * HD + d] = 1
    return jnp.asarray(freq), jnp.asarray(perm, bf16), jnp.asarray(permo, bf16)


def per_device(
    tokens,
    positions,
    attn_gain,
    qkv_weight,
    output_weight,
    ffn_gain,
    gate_weight,
    up_weight,
    down_weight,
    cotangent,
):
    parts = run_layer(
        tokens, positions.reshape(8, 128), attn_gain, ffn_gain, qkv_weight, output_weight,
        gate_weight, up_weight, down_weight, cotangent,
    )
    s = jax.ShapeDtypeStruct
    shapes = [(512, 384), (512, 384), (384,), (384, 384), (192, 384), (384,), (384, 512), (384, 512), (512, 384)]
    outs = pl.pallas_call(
        outputs_kernel,
        out_shape=[s(shape, f32) for shape in shapes],
        in_specs=[VM] * 8,
        out_specs=[VM] * 9,
        compiler_params=pltpu.CompilerParams(vmem_limit_bytes=63 * 1024 * 1024),
        name="outputs",
    )(*parts)
    return tuple(outs)


def solution(mesh):
    finer = Mesh(mesh.devices.reshape(2, 2, 4, 2, 4), AXES)
    row = ("y", "zh")
    in_specs = (
        P(DP_ROW, "x"),
        P(("zl", "core", "x")),
        P("x"),
        P("x", row),
        P(row, "x"),
        P("x"),
        P("x", row),
        P("x", row),
        P(row, "x"),
        P(DP_ROW, "x"),
    )
    out_specs = (
        P(DP_ROW, "x"),
        P(DP_ROW, "x"),
        P("x"),
        P("x", row),
        P(row, "x"),
        P("x"),
        P("x", row),
        P("x", row),
        P(row, "x"),
    )
    return jax.shard_map(per_device, mesh=finer, in_specs=in_specs, out_specs=out_specs, check_vma=False)
```
